32 devices in a mesh: dp: 16 (over z, y, x), mp: 2 (over core).
Axes of the slice: x: 2, y: 2, z: 4, core: 2. Of those that a mesh axis runs over, the one named last changes fastest.
Arguments:
- block_input: bfloat16 [2, 2048, 2560], P(None, ('dp', 'mp')), may hold values from -6 to 6
- lengths: int32 [2], replicated, may hold values from 512 to 2048, as said below
- norm_gains: float32 [2, 2560], replicated, may hold values from 0.5 to 1.5
- w_branch: bfloat16 [2, 2560, 2560], P(None, 'dp', 'mp'), may hold values from -0.125 to 0.125
- channel_params: float32 [7, 2560], P(None, 'mp'), may hold values from -3 to 3
- gate_blocks: bfloat16 [2, 10, 256, 256], P(None, 'mp', 'dp'), may hold values from -0.375 to 0.375
- decay_param: float32 [2560], P('mp'), may hold values from -11 to -4
- w_out: bfloat16 [2560, 2560], P('mp', 'dp'), may hold values from -0.3125 to 0.3125
- w_mlp: bfloat16 [2, 2560, 7680], P(None, 'dp', 'mp'), may hold values from -0.125 to 0.125
- w_down: bfloat16 [7680, 2560], P('mp', 'dp'), may hold values from -0.09375 to 0.09375
- out_grad: bfloat16 [2, 2048, 2560], P(None, ('dp', 'mp')), may hold values from -6 to 6
Outputs:
- block_output: bfloat16 [2, 2048, 2560], P(None, ('dp', 'mp'))
- input_grad: float32 [2, 2048, 2560], P(None, ('dp', 'mp'))
- grad_norm_gains: float32 [2, 2560], replicated
- grad_w_branch: float32 [2, 2560, 2560], P(None, 'dp', 'mp')
- grad_channel: float32 [7, 2560], P(None, 'mp')
- grad_gate_blocks: float32 [2, 10, 256, 256], P(None, 'mp', 'dp')
- grad_decay: float32 [2560], P('mp')
- grad_w_out: float32 [2560, 2560], P('mp', 'dp')
- grad_w_mlp: float32 [2, 2560, 7680], P(None, 'dp', 'mp')
- grad_w_down: float32 [7680, 2560], P('mp', 'dp')
The draws below stay inside these ranges and needn't reach their ends.
Inputs may be any that keep to these rules, and one draw needn't show every extreme that they name: lengths[s] is the number of valid leading tokens of slot s; some slot is full in every draw.
All inputs are finite; a program needn't handle non-finite values.
Results may differ from the reference program's by a relative error of at most 0.011.
Values may be sent and summed in bfloat16 or wider, within the bound.
A program may use at most 448 MiB of HBM per device.

```python
import jax
import jax.numpy as jnp
from jax import lax

D = 2560
H = 10
HS = 256
L = 2560
F = 7680
MB = 2
SEQ = 2048
ROWS = 2048
SLOTS = 2


def draw_lengths(key, part):
    length_key, choose_key = jax.random.split(key)
    values = jax.random.randint(length_key, (SLOTS,), SEQ // 4, SEQ + 1)
    full_slot = jax.random.randint(choose_key, (), 0, SLOTS)
    return jnp.where(jnp.arange(SLOTS) == full_slot, SEQ, values).astype(jnp.int32)


def level_of(own_key, dims, shards, smallest, top_value):
    gain = 1.0
    for dim, parts in shards:
        heights = jax.random.uniform(jax.random.fold_in(jax.random.fold_in(own_key, 6), dim), (parts,), jnp.float32, smallest / len(shards), top_value / len(shards))
        gain = gain * jnp.repeat(jnp.exp(heights), dims[dim] // parts).reshape((-1,) + (1,) * (len(dims) - 1 - dim))
    return gain


def scatter_about(stream_key, extent, deviation, limit, cuts=(), held_as=jnp.bfloat16):
    array = jax.random.normal(stream_key, extent, jnp.float32) * deviation
    if len(cuts) > 0:
        array = level_of(stream_key, extent, cuts, -0.22, 0.18) * array
    return jnp.clip(array, min=-limit, max=limit).astype(held_as)


def setup_inputs(seed: int = 0) -> dict:
    streams_of = jax.random.split(jax.random.key(seed), 12)
    block_input = scatter_about(streams_of[0], (MB, ROWS, D), 1.0, 6.0, ((1, 32),))
    lengths = draw_lengths(jax.random.fold_in(streams_of[11], 71), 0)
    norm_gains = jnp.clip(1.0 + 0.1 * jax.random.normal(streams_of[2], (2, D), jnp.float32), 0.5, 1.5)
    w_branch = scatter_about(streams_of[3], (2, D, L), D ** -0.5, 0.125, ((1, 16), (2, 2)))
    channel_params = scatter_about(streams_of[4], (7, L), 0.5, 3.0, ((1, 2),), jnp.float32)
    gate_blocks = scatter_about(streams_of[5], (2, H, HS, HS), HS ** -0.5, 0.375, ((1, 2), (2, 16)))
    decay_param = jnp.clip(-11.0 + 7.0 * jax.random.uniform(streams_of[6], (L,), jnp.float32) ** level_of(streams_of[6], (L,), ((0, 2),), -0.2, 0.2), -11.0, -4.0)
    w_out = scatter_about(streams_of[7], (L, D), (L // 8) ** -0.5, 0.3125, ((0, 2), (1, 16)))
    w_mlp = scatter_about(streams_of[8], (2, D, F), D ** -0.5, 0.125, ((1, 16), (2, 2)))
    w_down = scatter_about(streams_of[9], (F, D), (F // 2) ** -0.5, 0.09375, ((0, 2), (1, 16)))
    out_grad = scatter_about(streams_of[10], (MB, ROWS, D), 1.0, 6.0, ((1, 32),))
    return {"block_input": block_input, "lengths": lengths, "norm_gains": norm_gains, "w_branch": w_branch, "channel_params": channel_params, "gate_blocks": gate_blocks, "decay_param": decay_param, "w_out": w_out, "w_mlp": w_mlp, "w_down": w_down, "out_grad": out_grad}


@jax.custom_vjp
def low(v):
    return lax.optimization_barrier(v.astype(jnp.bfloat16)).astype(jnp.float32)

@jax.custom_vjp
def low_back(v):
    return v

def low_keep(v):
    return (low(v), None)

def low_pass(kept, grad):
    return (grad,)

def back_keep(v):
    return (v, None)

def back_low(kept, grad):
    return (low(grad),)
low.defvjp(low_keep, low_pass)
low_back.defvjp(back_keep, back_low)
EPS = 1e-06
HIGH = lax.Precision.HIGHEST

def combine_pair(earlier, later):
    return (earlier[0] * later[0], later[0] * earlier[1] + later[1])

def rms_norm(values, gain_vec):
    return values * lax.rsqrt(lax.optimization_barrier(jnp.mean(values * values, axis=-1, keepdims=True)) + EPS) * gain_vec

def sequence_forward(params, seq_rows, length):
    norm_gains, w_branch, channel_params, gate_blocks, decay_param, w_out, w_mlp, w_down = params
    position = jnp.arange(SEQ, dtype=jnp.int32)
    normed_a = low(rms_norm(seq_rows, norm_gains[0]))
    branches = jnp.einsum('sd,kdl->ksl', normed_a, w_branch, precision=HIGH)
    gelu_gate = jax.nn.gelu(low_back(branches[0]))
    conv_input = low_back(low(branches[1]))
    padded = jnp.concatenate([jnp.zeros((3, L), jnp.float32), conv_input], axis=0)
    conv_out = channel_params[4] + channel_params[0] * padded[3:] + channel_params[1] * padded[2:SEQ + 2]
    conv_out = conv_out + channel_params[2] * padded[1:SEQ + 1] + channel_params[3] * padded[:SEQ]
    conv_out = low(conv_out)
    blocks = jnp.einsum('shi,ghij->gshj', conv_out.reshape(SEQ, H, HS), gate_blocks, precision=HIGH).reshape(2, SEQ, L)
    gate_vals = jax.nn.sigmoid(low_back(blocks) + channel_params[5:7][:, None, :])
    log_a = -8.0 * gate_vals[1] * jax.nn.softplus(decay_param)
    decay_rate = jnp.exp(log_a)
    multiplier = jnp.where((position == 0)[:, None], 1.0, jnp.sqrt(-jnp.expm1(2.0 * log_a)))
    drive_term = conv_out * gate_vals[0] * multiplier
    state_vals = lax.associative_scan(combine_pair, (decay_rate, drive_term), axis=0)[1]
    mixed_vals = low(state_vals * gelu_gate)
    temporal = low_back(jnp.dot(mixed_vals, w_out, precision=HIGH))
    residual = seq_rows + temporal
    normed_b = low(rms_norm(residual, norm_gains[1]))
    gate_up = low_back(jnp.einsum('sd,kdf->ksf', normed_b, w_mlp, precision=HIGH))
    hidden = low(jax.nn.gelu(gate_up[0]) * gate_up[1])
    mlp_out = low_back(jnp.dot(hidden, w_down, precision=HIGH))
    return jnp.where((position < length)[:, None], residual + mlp_out, 0.0)

def reference(block_input, lengths, norm_gains, w_branch, channel_params, gate_blocks, decay_param, w_out, w_mlp, w_down, out_grad):
    params = (norm_gains, w_branch.astype(jnp.float32), channel_params, gate_blocks.astype(jnp.float32), decay_param, w_out.astype(jnp.float32), w_mlp.astype(jnp.float32), w_down.astype(jnp.float32))
    slot_rows = block_input.astype(jnp.float32).reshape(SLOTS, SEQ, D)

    def forward(params, slot_rows):
        seq_step = jax.checkpoint(lambda pair_item: sequence_forward(params, pair_item[0], pair_item[1]))
        return lax.map(seq_step, (slot_rows, lengths))
    seq_outs, pullback = jax.vjp(forward, params, slot_rows)
    grad_tree, grad_slots = pullback(out_grad.astype(jnp.float32).reshape(SLOTS, SEQ, D))
    return (seq_outs.reshape(MB, SEQ, D).astype(jnp.bfloat16), grad_slots.reshape(MB, SEQ, D), grad_tree[0], grad_tree[1], grad_tree[2], grad_tree[3], grad_tree[4], grad_tree[5], grad_tree[6], grad_tree[7])
```

```python
import functools

import jax
import jax.numpy as jnp
from jax import lax
from jax.experimental import pallas as pl
from jax.experimental.pallas import tpu as pltpu
from jax.sharding import PartitionSpec as P

MESH = pl.DeviceIdType.MESH
VMEM_LIMIT = 56 * 1024 * 1024


EPS = 1e-06
TP = 4
BF = jnp.bfloat16
F32 = jnp.float32


def combine_pair(earlier, later):
    return (earlier[0] * later[0], later[0] * earlier[1] + later[1])


def plan():
    ndp = lax.axis_size("dp")
    ng = ndp // TP
    dp = lax.axis_index("dp")
    return ndp, ng, dp // ng, dp % ng


def z_groups():
    ndp = lax.axis_size("dp")
    ng = ndp // TP
    return [[t * ng + g for t in range(TP)] for g in range(ng)]


def g_groups():
    ndp = lax.axis_size("dp")
    ng = ndp // TP
    return [[t * ng + g for g in range(ng)] for t in range(TP)]


class Comm:
    def __init__(self, send, recv):
        self.send, self.recv, self.n = send, recv, 0
        self.ndp = lax.axis_size("dp")
        self.ng = self.ndp // TP
        dp = lax.axis_index("dp")
        self.t, self.g, self.m = dp // self.ng, dp % self.ng, lax.axis_index("mp")
        self.bits = [1 << k for k in range(self.ng.bit_length() - 1)]

    def at(self, t=None, g=None, m=None):
        t = self.t if t is None else t
        g = self.g if g is None else g
        return (t * self.ng + g, self.m if m is None else m)

    def flip(self, g, b):
        return g + b - 2 * b * ((g // b) % 2)

    def barrier(self):
        sem = pltpu.get_barrier_semaphore()
        partners = [self.at(t=(self.t + o) % TP) for o in range(1, TP)]
        partners += [self.at(g=self.flip(self.g, b)) for b in self.bits] + [self.at(m=1 - self.m)]
        for p in partners:
            pl.semaphore_signal(sem, inc=1, device_id=p, device_id_type=MESH)
        pl.semaphore_wait(sem, len(partners))

    def slot(self):
        self.n += 1
        return self.n - 1

    def to(self, src, dst, dev, slot):
        return pltpu.make_async_remote_copy(
            src_ref=src, dst_ref=dst, send_sem=self.send.at[slot], recv_sem=self.recv.at[slot],
            device_id=dev, device_id_type=MESH,
        )

    def local(self, src, dst, slot):
        return pltpu.make_async_copy(src, dst, self.send.at[slot])


def run(*flows):
    flows = list(flows)
    while flows:
        for f in list(flows):
            try:
                next(f)
            except StopIteration:
                flows.remove(f)


def ag_flow(c, own, full):
    t, m = c.t, c.m
    sib = c.at(m=1 - m)
    up = [c.slot() for _ in range(TP - 1)]
    down = [c.slot() for _ in range(TP - 1)]
    d2u = [c.slot() for _ in range(TP - 1)]
    d2d = [c.slot() for _ in range(TP - 1)]
    d2o, loc = c.slot(), c.slot()

    def up_copy(k):
        b = t - k
        return c.to(own if k == 0 else full.at[:, b, m], full.at[:, b, m], c.at(t=t + 1), up[k])

    def down_copy(k):
        b = t + k
        return c.to(own if k == 0 else full.at[:, b, m], full.at[:, b, m], c.at(t=t - 1), down[k])

    def side(b, slot, src=None):
        return c.to(full.at[:, b, m] if src is None else src, full.at[:, b, m], sib, slot)

    def got(b, slot, mm):
        return c.to(full.at[:, b, mm], full.at[:, b, mm], sib, slot)

    pl.when(t < TP - 1)(lambda: up_copy(0).start())
    pl.when(t > 0)(lambda: down_copy(0).start())
    side(t, d2o, own).start()
    c.local(own, full.at[:, t, m], loc).start()
    yield
    for k in range(TP - 1):
        def from_below():
            got(t - 1 - k, up[k], m).wait_recv()
            side(t - 1 - k, d2u[k]).start()
            if k < TP - 2:
                pl.when(t < TP - 1)(lambda: up_copy(k + 1).start())

        def from_above():
            got(t + 1 + k, down[k], m).wait_recv()
            side(t + 1 + k, d2d[k]).start()
            if k < TP - 2:
                pl.when(t > 0)(lambda: down_copy(k + 1).start())

        pl.when(t - 1 - k >= 0)(from_below)
        pl.when(t + 1 + k < TP)(from_above)
        yield
    c.local(own, full.at[:, t, m], loc).wait()
    side(t, d2o, own).wait_send()
    got(t, d2o, 1 - m).wait_recv()
    for k in range(TP - 1):
        pl.when((t < TP - 1) & (t - k >= 0))(lambda: up_copy(k).wait_send())
        pl.when((t > 0) & (t + k < TP))(lambda: down_copy(k).wait_send())

        def below():
            side(t - 1 - k, d2u[k]).wait_send()
            got(t - 1 - k, d2u[k], 1 - m).wait_recv()

        def above():
            side(t + 1 + k, d2d[k]).wait_send()
            got(t + 1 + k, d2d[k], 1 - m).wait_recv()

        pl.when(t - 1 - k >= 0)(below)
        pl.when(t + 1 + k < TP)(above)


def rs_scratch(rows, width):
    return [
        pltpu.VMEM((2, TP, rows, width), BF),
        pltpu.VMEM((2, TP - 1, 2, rows, width), BF),
        pltpu.VMEM((2, TP - 1, 2, rows, width), BF),
    ]


def rs_flow(c, part, out, sib, inbox, outbox):
    t, m = c.t, c.m
    n = part.shape[3]
    other = c.at(m=1 - m)
    lower = t < TP // 2
    u = jnp.where(lower, t, TP - 1 - t)
    da = jnp.where(lower, 0, 1)
    step = 1 - 2 * da
    near = [c.slot() for _ in range(TP)]
    base = c.n
    for _ in range(2 * (TP - 1)):
        c.slot()

    def real(d):
        return jnp.where(lower, d, TP - 1 - d)

    def cross(d):
        return c.to(part.at[:, real(d), 1 - m], sib.at[:, real(d)], other, near[d])

    def msg(flow, j):
        way = da if flow == 0 else 1 - da
        dev = c.at(t=t + step if flow == 0 else t - step)
        return c.to(outbox.at[way, j], inbox.at[way, j], dev, base + way * (TP - 1) + j)

    def add(d, into, terms):
        b = real(d)

        def rows16(i, _):
            sl = pl.ds(pl.multiple_of(i * 16, 16), 16)
            for s in range(2):
                v = part[s, b, m, sl, :].astype(F32) + sib[s, b, sl, :].astype(F32)
                for way, j in terms:
                    v = v + inbox[way, j, s, sl, :].astype(F32)
                into(s, sl, v)
            return 0

        lax.fori_loop(0, n // 16, rows16, 0)

    def put(way, j):
        def into(s, sl, v):
            outbox[way, j, s, sl, :] = v.astype(BF)
        return into

    def final(s, sl, v):
        out[s, sl, :] = v

    for d in (3, 2, 0, 1):
        cross(d).start()
    yield
    for d, j in ((3, 0), (2, 1)):
        cross(d).wait_recv()
        for lvl in range(2):
            def go():
                if lvl == 1:
                    msg(0, j).wait_recv()
                add(d, put(da, j), [(da, j)] if lvl else [])
                msg(0, j).start()
            pl.when(u == lvl)(go)
        yield
    cross(0).wait_recv()
    cross(1).wait_recv()

    def first():
        add(1, put(da, 2), [])
        msg(0, 2).start()

    pl.when(u == 0)(first)

    def back():
        msg(1, 0).wait_recv()
        add(0, put(1 - da, 0), [(1 - da, 0)])
        msg(1, 0).start()

    pl.when(u == 1)(back)
    yield

    def end0():
        msg(1, 0).wait_recv()
        add(0, final, [(1 - da, 0)])

    def end1():
        msg(0, 2).wait_recv()
        msg(1, 1).wait_recv()
        add(1, final, [(da, 2), (1 - da, 1)])

    pl.when(u == 0)(end0)
    pl.when(u == 1)(end1)
    for d in range(TP):
        cross(d).wait_send()
    for j in range(2):
        msg(0, j).wait_send()
    pl.when(u == 0)(lambda: msg(0, 2).wait_send())
    pl.when(u == 1)(lambda: msg(1, 0).wait_send())


def spread_z(c, src, dst, need=None):
    slots = [c.slot() for _ in range(TP)]

    def copy(o):
        to = (c.t + o) % TP
        return c.to(src(to), dst(c.t), c.at(t=to), slots[o])

    def mine():
        return c.local(src(c.t), dst(c.t), slots[0])

    def back(o):
        frm = (c.t + TP - o) % TP
        return c.to(src(frm), dst(frm), c.at(t=frm), slots[o])

    def when(t, f):
        if need is None:
            f()
        else:
            pl.when(t == need)(f)

    for o in range(1, TP):
        when((c.t + o) % TP, lambda: copy(o).start())
    when(c.t, lambda: mine().start())
    yield
    when(c.t, lambda: mine().wait())
    for o in range(1, TP):
        when(c.t, lambda: back(o).wait_recv())
    yield
    for o in range(1, TP):
        when((c.t + o) % TP, lambda: copy(o).wait_send())


def plane_gather(c, block, order):
    have = [0]
    done = []
    for b in order:
        dev = c.at(g=c.flip(c.g, b))
        sent = []
        for x in have:
            gg = c.g
            for bit in c.bits:
                if x & bit:
                    gg = c.flip(gg, bit)
            copy = c.to(block(gg), block(gg), dev, c.slot())
            copy.start()
            sent.append(copy)
        yield
        for copy in sent:
            copy.wait_recv()
        done += sent
        have = have + [x ^ b for x in have]
    for copy in done:
        copy.wait_send()


def plane_reduce(c, own, sums, inbox, order):
    def place(x):
        gg = c.g
        for bit in c.bits:
            if x & bit:
                gg = c.flip(gg, bit)
        return gg

    left = list(range(c.ng))
    spot = {}
    done = []
    base = 0
    for k, b in enumerate(order):
        dev = c.at(g=c.flip(c.g, b))
        away = [x for x in left if x & b]
        left = [x for x in left if not x & b]
        sent = []
        for i, x in enumerate(away):
            src = own(place(x)) if k == 0 else sums.at[spot[x]]
            copy = c.to(src, inbox.at[base + i], dev, c.slot())
            copy.start()
            sent.append(copy)
        held = []
        if k == 0:
            spot = {x: i for i, x in enumerate(left)}
            for x in left:
                held.append(c.local(own(place(x)), sums.at[spot[x]], c.slot()))
                held[-1].start()
        yield
        for i, x in enumerate(left):
            sent[i].wait_recv()
            if k == 0:
                held[i].wait()
            add_blocks(sums.at[spot[x]], inbox.at[base + i])
        base += len(away)
        done += sent
    for copy in done:
        copy.wait_send()


def add_blocks(a, b):
    def one(i, _):
        a[i] = (a[i].astype(F32) + b[i].astype(F32)).astype(BF)
        return 0

    lax.fori_loop(0, a.shape[0], one, 0)


def call(kernel, out_shape, in_specs, out_specs, scratch, cid, slots=160):
    return pl.pallas_call(
        kernel,
        out_shape=out_shape,
        in_specs=in_specs,
        out_specs=out_specs,
        scratch_shapes=list(scratch) + [pltpu.SemaphoreType.DMA((slots,)), pltpu.SemaphoreType.DMA((slots,))],
        compiler_params=pltpu.CompilerParams(collective_id=cid, has_side_effects=True, vmem_limit_bytes=VMEM_LIMIT),
    )


HBM = pl.BlockSpec(memory_space=pl.ANY)
VM = pl.BlockSpec(memory_space=pltpu.VMEM)


def start_kernel(x, go, gain, wbr, wot, gates, mlp, full_a, full_g, wb, wo, gb, wm, own, zero, send, recv):
    c = Comm(send, recv)
    c.barrier()
    r = wbr.shape[1]

    def head(ref, lead):
        def src(t):
            lane = pl.multiple_of(t * 256, 256)
            return ref.at[(*lead, slice(None), pl.ds(lane, 256))]
        return src

    pieces = []
    for k in range(2):
        pieces.append((head(wbr, (k,)), wb, (k,), wbr.at[k, :, pl.ds(1024, 256)]))
    pieces.append((head(wot, ()), wo, (), wot.at[:, pl.ds(1024, 256)]))
    z = []
    for src, dst, lead, extra in pieces:
        z.append(spread_z(c, src, lambda t, dst=dst, lead=lead: dst.at[(*lead, t, c.g, slice(None), pl.ds(0, 256))]))
        z.append(spread_z(c, lambda t, extra=extra: extra, lambda t, dst=dst, lead=lead: dst.at[(*lead, t, c.g, slice(None), pl.ds(256, 256))], 1))
    z.append(spread_z(c, lambda t: gates.at[:, t], lambda t: gb.at[:, 0, t, c.g]))
    z.append(spread_z(c, lambda t: gates.at[:, 4], lambda t: gb.at[:, 1, t, c.g], 1))
    for f in z:
        next(f)
    x32 = [x[s].astype(F32) for s in range(2)]
    for s in range(2):
        v = x32[s] * lax.rsqrt(jnp.mean(x32[s] * x32[s], axis=-1, keepdims=True) + EPS) * gain[...]
        own[s] = v.astype(BF)
    ag = ag_flow(c, own, full_a)
    next(ag)
    zero[...] = jnp.zeros_like(zero)
    fills = []
    for k in range(2):
        fills.append((zero, wb.at[k, :, c.g, :, pl.ds(256, 256)], c.slot()))
    fills.append((zero, wo.at[:, c.g, :, pl.ds(256, 256)], c.slot()))
    for k in range(2):
        fills.append((zero.at[:, pl.ds(0, gates.shape[2])], gb.at[k, 1, :, c.g], c.slot()))

    def fill():
        for f in fills:
            c.local(*f).start()
        for f in fills:
            c.local(*f).wait()

    pl.when(c.t != 1)(fill)
    zm = [spread_z(c, lambda t, k=k: mlp.at[t, k], lambda t, k=k: wm.at[k, t, c.g]) for k in range(3)]
    for f in z:
        next(f)
    fwd, rev = c.bits, c.bits[::-1]
    g1 = [plane_gather(c, lambda g: wb.at[0, :, g], fwd), plane_gather(c, lambda g: wb.at[1, :, g], rev),
          plane_gather(c, lambda g: wo.at[pl.ds(0, 2), g], fwd), plane_gather(c, lambda g: wo.at[pl.ds(2, 2), g], rev),
          plane_gather(c, lambda g: gb.at[0, :, :, g], fwd), plane_gather(c, lambda g: gb.at[1, :, :, g], rev)]
    for f in g1:
        next(f)
    next(ag)
    ag2 = ag_flow(c, go, full_g)
    for f in zm:
        next(f)
    for f in g1:
        next(f)
    run(ag)
    next(ag2)
    for f in zm:
        next(f)
    g2 = [plane_gather(c, lambda g: wm.at[0, :, g], fwd), plane_gather(c, lambda g: wm.at[1, :, g], rev),
          plane_gather(c, lambda g: wm.at[2, pl.ds(0, 2), g], fwd), plane_gather(c, lambda g: wm.at[2, pl.ds(2, 2), g], rev)]
    run(*z, *zm, *g1, *g2, ag2)


def start_call(x, go, gain, wbr, wot, gates, mlp):
    ng = lax.axis_size("dp") // TP
    _, n, d = x.shape
    r, gr, fs = wbr.shape[1], gates.shape[2], mlp.shape[3]
    S = jax.ShapeDtypeStruct
    return call(
        start_kernel,
        (S((2, TP, 2, n, d), BF), S((2, TP, 2, n, d), BF), S((2, TP, ng, r, 512), BF), S((TP, ng, r, 512), BF),
         S((2, 2, TP, ng, gr, 256), BF), S((3, TP, ng, r, fs), BF)),
        [VM, VM, VM, HBM, HBM, HBM, HBM],
        (HBM,) * 6,
        [pltpu.VMEM((2, n, d), BF), pltpu.VMEM((TP, r, 256), BF)],
        1,
    )(x, go, gain[None], wbr, wot, gates, mlp)


def mid_kernel(part, x, gain, res, full, tot, own, sib, inbox, outbox, send, recv):
    c = Comm(send, recv)
    c.barrier()
    run(rs_flow(c, part, tot, sib, inbox, outbox))
    for s in range(2):
        v = x[s].astype(F32) + tot[s]
        res[s] = v
        own[s] = (v * lax.rsqrt(jnp.mean(v * v, axis=-1, keepdims=True) + EPS) * gain[...]).astype(BF)
    run(ag_flow(c, own, full))


def mid_call(part, x, gain):
    _, n, d = x.shape
    S = jax.ShapeDtypeStruct
    return call(
        mid_kernel,
        (S((2, n, d), F32), S((2, TP, 2, n, d), BF)),
        [VM, VM, VM],
        (VM, HBM),
        [pltpu.VMEM((2, n, d), F32), pltpu.VMEM((2, n, d), BF)] + rs_scratch(n, d),
        2,
    )(part.reshape(2, TP, 2, n, d), x, gain[None])


def back_kernel(part, part2, res, go, gain, gres, gsum, mlp_own, full, tot, own, sib, inbox, outbox, sib2, inbox2, outbox2, send, recv):
    c = Comm(send, recv)
    c.barrier()
    run(rs_flow(c, part, tot, sib, inbox, outbox))
    total = jnp.zeros_like(gsum)
    for s in range(2):
        v = res[s]
        scale = lax.rsqrt(jnp.mean(v * v, axis=-1, keepdims=True) + EPS)
        normal = v * scale
        gn = tot[s]
        total = total + jnp.sum(gn * normal, axis=0, keepdims=True)
        q = gn * gain[...]
        gr = scale * (q - normal * jnp.mean(q * normal, axis=-1, keepdims=True)) + go[s].astype(F32)
        gres[s] = gr
        own[s] = gr.astype(BF)
    gsum[...] = total
    run(ag_flow(c, own, full), rs_flow(c, part2, mlp_own, sib2, inbox2, outbox2))


def back_call(part, part2, res, go, gain):
    _, n, d = go.shape
    S = jax.ShapeDtypeStruct
    shape = (2, TP, 2, n, d)
    return call(
        back_kernel,
        (S((2, n, d), F32), S((1, d), F32), S((2, n, d), F32), S(shape, BF)),
        [VM] * 5,
        (VM, VM, VM, HBM),
        [pltpu.VMEM((2, n, d), F32), pltpu.VMEM((2, n, d), BF)] + rs_scratch(n, d) + rs_scratch(n, d),
        3,
    )(part.reshape(shape), part2.reshape(shape), res, go, gain[None])


def end_kernel(part, x, gres, gain, gwb, gwo, ggb, gwm, gin, gsum, owb, owo, ogb, owm,
               tot, sib, inbox, outbox, su_m, in_m, su_x, in_x, su_g, in_g, send, recv):
    c = Comm(send, recv)
    c.barrier()
    fwd, rev = c.bits, c.bits[::-1]
    red, spread = [], []
    for k in range(3):
        own = lambda g, k=k: gwm.at[k, :, g]
        red.append(plane_reduce(c, own, su_m.at[k], in_m.at[k], rev if k % 2 else fwd))
        spread.append(spread_z(c, lambda t, k=k: su_m.at[k, 0, t], lambda t, k=k: owm.at[k, t]))
    for k in range(3):
        own = (lambda g, k=k: gwb.at[k, :, g]) if k < 2 else (lambda g: gwo.at[:, g])
        out = (lambda t, k=k: owb.at[k, t]) if k < 2 else (lambda t: owo.at[t])
        red.append(plane_reduce(c, own, su_x.at[k], in_x.at[k], fwd if k % 2 else rev))
        spread.append(spread_z(c, lambda t, k=k: su_x.at[k, 0, t], out))
    for k in range(2):
        for h in range(2):
            i = 2 * k + h
            red.append(plane_reduce(c, lambda g, k=k, h=h: ggb.at[k, h, :, g], su_g.at[i], in_g.at[i], fwd if k else rev))
            spread.append(spread_z(c, lambda t, i=i: su_g.at[i, 0, t], lambda t, k=k, h=h: ogb.at[k, h, t]))
    rs = rs_flow(c, part, tot, sib, inbox, outbox)
    next(rs)
    for f in red:
        next(f)
    run(rs)
    total = jnp.zeros_like(gsum)
    for s in range(2):
        v = x[s].astype(F32)
        scale = lax.rsqrt(jnp.mean(v * v, axis=-1, keepdims=True) + EPS)
        normal = v * scale
        gn = tot[s]
        total = total + jnp.sum(gn * normal, axis=0, keepdims=True)
        q = gn * gain[...]
        gin[s] = scale * (q - normal * jnp.mean(q * normal, axis=-1, keepdims=True)) + gres[s]
    gsum[...] = total
    for _ in range(len(c.bits) - 1):
        for f in red:
            next(f)
    for f, s in zip(red, spread):
        run(f)
        next(s)
    run(*spread)


def end_call(part, x, gres, gain, gwb, gwo, ggb, gwm):
    _, n, d = x.shape
    ng = lax.axis_size("dp") // TP
    r, gr, fs = gwb.shape[3], ggb.shape[4], gwm.shape[4]
    S = jax.ShapeDtypeStruct
    half = ng // 2

    def sets(k, rows, width):
        return [pltpu.VMEM((k, half, TP, rows, width), BF), pltpu.VMEM((k, ng - 1, TP, rows, width), BF)]

    return call(
        end_kernel,
        (S((2, n, d), F32), S((1, d), F32), S((2, TP, r, 512), BF), S((TP, r, 512), BF), S((2, 2, TP, gr, 256), BF), S((3, TP, r, fs), BF)),
        [VM] * 4 + [HBM] * 4,
        (VM, VM) + (HBM,) * 4,
        [pltpu.VMEM((2, n, d), F32)] + rs_scratch(n, d) + sets(3, r, fs) + sets(3, r, 512) + sets(4, gr, 256),
        4, 400,
    )(part.reshape(2, TP, 2, n, d), x, gres, gain[None], gwb, gwo, ggb, gwm)


def heads_of(a, axis):
    _, _, t, _ = plan()
    p = lax.dynamic_slice_in_dim(a, t * 256, 256, axis)
    q = lax.dynamic_slice_in_dim(a, 1024, 256, axis)
    q = jnp.where(t == 1, q, jnp.zeros_like(q))
    return jnp.concatenate([p, q], axis)


def heads_back(a, axis):
    ga = lax.all_gather(a, "dp", axis=0, axis_index_groups=z_groups())
    parts = [lax.slice_in_dim(ga[i], 0, 256, axis=axis) for i in range(TP)] + [lax.slice_in_dim(ga[1], 256, 512, axis=axis)]
    return jnp.concatenate(parts, axis)


def gather_g(x):
    return lax.all_gather(x, "dp", axis=0, axis_index_groups=g_groups())


def shift_blocks(x, step):
    ndp, ng, t, g = plan()
    ga = gather_g(x)
    seq = ga.reshape(ng, 2, TP, *x.shape[1:]).transpose(1, 2, 0, 3, 4).reshape(2, ndp, *x.shape[1:])
    z = jnp.zeros_like(seq[:, :1])
    if step == 1:
        seq = jnp.concatenate([z, seq[:, :-1]], 1)
    else:
        seq = jnp.concatenate([seq[:, 1:], z], 1)
    seq = seq.reshape(2, TP, ng, *x.shape[1:])
    return lax.dynamic_index_in_dim(seq, g, 2, False).reshape(x.shape)


def carries(prod, last, reverse):
    ndp, ng, t, g = plan()
    C = prod.shape[-1]
    def seqd(x):
        return gather_g(x).reshape(ng, 2, TP, C).transpose(1, 2, 0, 3).reshape(2, ndp, C)
    p, l = seqd(prod), seqd(last)
    c = jnp.zeros((2, C), F32)
    outs = [None] * ndp
    order = range(ndp - 1, -1, -1) if reverse else range(ndp)
    for i in order:
        outs[i] = c
        c = l[:, i] + p[:, i] * c
    o = jnp.stack(outs, 1).reshape(2, TP, ng, C)
    return lax.dynamic_index_in_dim(o, g, 2, False).reshape(8, C)


def mixer_forward(branch0, conv_input, gb, chan, decay_base, at_start):
    C = conv_input.shape[-1]
    ci = conv_input.reshape(8, -1, C)
    n = ci.shape[1]
    rim = shift_blocks(ci[:, n - 3:], 1)
    ext = jnp.concatenate([rim, ci], 1).astype(F32)
    conv = chan[4] + chan[0] * ext[:, 3:] + chan[1] * ext[:, 2:n + 2]
    conv = conv + chan[2] * ext[:, 1:n + 1] + chan[3] * ext[:, :n]
    conv_low = conv.astype(BF)
    cv = conv_low.astype(F32)
    pre = jnp.einsum("bnhi,ghij->gbnhj", conv_low.reshape(8, n, 2, 256), gb, preferred_element_type=F32).reshape(2, 8, n, C)
    gv = jax.nn.sigmoid(pre + chan[5:7][:, None, None, :])
    log_a = -8.0 * gv[1] * decay_base
    decay = jnp.exp(log_a)
    root = jnp.sqrt(-jnp.expm1(2.0 * log_a))
    mult = jnp.where(at_start, 1.0, root)
    drive = cv * gv[0] * mult
    prod, loc = lax.associative_scan(combine_pair, (decay, drive), axis=1)
    carry = carries(prod[:, -1], loc[:, -1], False)
    state = loc + prod * carry[:, None]
    mixed = (state * jax.nn.gelu(branch0.reshape(8, n, C))).astype(BF)
    return mixed.reshape(8 * n, C), (ext, conv_low, gv, state, carry, prod[:, -1])


def mixer_backward(grad_mixed, branch0, saved, gb, chan, decay_base, at_start):
    ext, conv_low, gv, state, carry, pl_ = saved
    n, C = conv_low.shape[1:]
    cv = conv_low.astype(F32)
    branch0 = branch0.reshape(8, n, C)
    gm = grad_mixed.reshape(8, n, C)
    gelu, pull = jax.vjp(jax.nn.gelu, branch0)
    grad_gate_branch = pull(gm * state)[0]
    gs = gm * gelu
    log_a = -8.0 * gv[1] * decay_base
    decay = jnp.exp(log_a)
    root = jnp.sqrt(-jnp.expm1(2.0 * log_a))
    mult = jnp.where(at_start, 1.0, root)
    rate_next = jnp.concatenate([decay[:, 1:], jnp.ones_like(decay[:, :1])], 1)
    suffix, loc = lax.associative_scan(combine_pair, (rate_next, gs), reverse=True, axis=1)
    back = carries(decay[:, 0] * suffix[:, 0], decay[:, 0] * loc[:, 0], True)
    adj = loc + suffix * back[:, None]
    before = jnp.concatenate([carry[:, None], state[:, :-1]], 1)
    gmult = adj * cv * gv[0]
    glog = adj * before * decay + jnp.where(at_start, 0.0, -gmult * jnp.exp(2.0 * log_a) / root)
    gdec = jnp.sum(glog * (-8.0 * gv[1]), axis=(0, 1))
    gpre = jnp.stack([adj * cv * mult, glog * (-8.0 * decay_base)]) * gv * (1.0 - gv)
    gpl = gpre.astype(BF).reshape(2, 8, n, 2, 256)
    ggb = jnp.einsum("bnhi,gbnhj->ghij", conv_low.reshape(8, n, 2, 256), gpl, preferred_element_type=F32)
    gconv = adj * gv[0] * mult + jnp.einsum("gbnhj,ghij->bnhi", gpl, gb, preferred_element_type=F32).reshape(8, n, C)
    taps = [jnp.sum(gconv * ext[:, 3 - k:3 - k + n], axis=(0, 1)) for k in range(4)]
    rows = jnp.stack(taps + [jnp.sum(gconv, axis=(0, 1)), jnp.sum(gpre[0], axis=(0, 1)), jnp.sum(gpre[1], axis=(0, 1)), gdec])
    nxt = shift_blocks(gconv[:, :3], -1)
    gext = jnp.concatenate([gconv, nxt], 1)
    gci = sum(chan[k] * gext[:, k:k + n] for k in range(4))
    gbr = jnp.stack([grad_gate_branch, gci]).astype(BF)
    return gbr.reshape(2, 8 * n, C), ggb, rows


def dot(a, b, ca, cb):
    return lax.dot_general(a, b, (((ca,), (cb,)), ((), ())), preferred_element_type=F32)


def pack(parts):
    return jnp.stack(parts)


def body(block_input, lengths, norm_gains, w_branch, channel_params, gate_blocks, decay_param, w_out, w_mlp, w_down, out_grad):
    ndp, ng, t, g = plan()
    dp, mp = lax.axis_index("dp"), lax.axis_index("mp")
    rows, width = block_input.shape[1:]
    r = w_branch.shape[1]
    fs = w_mlp.shape[2] // TP
    chan = heads_of(channel_params, 1)
    dpar = heads_of(decay_param[None], 1)[0]
    decay_base = jax.nn.softplus(dpar)
    pos = dp * 2 * rows + mp * rows + jnp.arange(rows, dtype=jnp.int32)
    valid = (pos[None] < lengths[:, None])[..., None]
    blk = jnp.arange(8) % TP * ng + g
    at_start = ((blk[:, None] * 2 * rows + jnp.arange(2 * rows)[None]) == 0)[..., None]
    x = block_input
    grad_own = jnp.where(valid, out_grad, jnp.zeros_like(out_grad))
    mlp = jnp.concatenate([w_mlp, w_down.T[None]], 0).reshape(3, r, TP, fs).transpose(2, 0, 1, 3)
    na, go, wb, wo, gb, wm = start_call(x, grad_own, norm_gains[0], w_branch, w_out.T, gate_blocks, mlp)
    na, go = na.reshape(-1, width), go.reshape(-1, width)
    wb, wo, wm = wb.reshape(2, width, 512), wo.reshape(width, 512), wm.reshape(3, width, fs)
    gb = gb.reshape(2, 2, 256, 256)
    wd = wm[2]
    branch0 = dot(na, wb[0], 1, 0)
    conv_input = dot(na, wb[1], 1, 0).astype(BF)
    mixed, saved = mixer_forward(branch0, conv_input, gb, chan, decay_base, at_start)
    residual, nb = mid_call(dot(mixed, wo, 1, 1).astype(BF), x, norm_gains[1])
    nb = nb.reshape(-1, width)
    first, second = dot(nb, wm[0], 1, 0), dot(nb, wm[1], 1, 0)
    act, act_pull = jax.vjp(jax.nn.gelu, first)
    hidden = (act * second).astype(BF)
    mlp_part = dot(hidden, wd, 1, 1).astype(BF)
    gh = dot(go, wd, 1, 0)
    gwd = dot(go, hidden, 0, 0).astype(BF)
    ggu = [act_pull(gh * second)[0].astype(BF), (gh * act).astype(BF)]
    gwm = [dot(nb, ggu[k], 0, 0).astype(BF) for k in range(2)]
    gnb = (dot(ggu[0], wm[0], 1, 1) + dot(ggu[1], wm[1], 1, 1)).astype(BF)
    gres, gain_b, mlp_own, gmo = back_call(gnb, mlp_part, residual, grad_own, norm_gains[1])
    out = jnp.where(valid, residual + mlp_own, 0.0).astype(BF)
    gmo = gmo.reshape(-1, width)
    gwo = dot(gmo, mixed, 0, 0).astype(BF)
    gbr, ggb, chan_rows = mixer_backward(dot(gmo, wo, 1, 0), branch0, saved, gb, chan, decay_base, at_start)
    gwb = [dot(na, gbr[k], 0, 0).astype(BF) for k in range(2)]
    gna = (dot(gbr[0], wb[0], 1, 1) + dot(gbr[1], wb[1], 1, 1)).astype(BF)
    gr = gate_blocks.shape[2]
    gin, gain_a, owb, owo, ogb, owm = end_call(
        gna, x, gres, norm_gains[0],
        jnp.stack(gwb).reshape(2, TP, ng, r, 512), gwo.reshape(TP, ng, r, 512),
        ggb.astype(BF).reshape(2, 2, TP, ng, gr, 256), jnp.stack(gwm + [gwd]).reshape(3, TP, ng, r, fs),
    )
    owb, owo = owb.astype(F32), owo.astype(F32)
    g_wb = jnp.concatenate([owb[:, i, :, :256] for i in range(TP)] + [owb[:, 1, :, 256:]], -1)
    g_wo = jnp.concatenate([owo[i, :, :256] for i in range(TP)] + [owo[1, :, 256:]], -1).T
    g_gb = jnp.concatenate([ogb[:, 0], ogb[:, 1, 1:2]], 1).astype(F32)
    g_wm = owm[:2].transpose(0, 2, 1, 3).reshape(2, r, TP * fs).astype(F32)
    g_wd = owm[2].transpose(0, 2, 1).reshape(TP * fs, r).astype(F32)
    gains = lax.psum(jnp.concatenate([gain_a, gain_b]), ("dp", "mp"))
    chan_rows = lax.psum(chan_rows, "dp", axis_index_groups=g_groups())
    crow = heads_back(chan_rows, 1)
    return out, gin, gains, g_wb, crow[:7], g_gb, crow[7] * jax.nn.sigmoid(decay_param), g_wo, g_wm, g_wd


def solution(mesh):
    return jax.shard_map(
        body,
        mesh=mesh,
        in_specs=(P(None, ("dp", "mp"), None), P(), P(), P(None, "dp", "mp"), P(None, "mp"), P(None, "mp", "dp", None), P("mp"), P("mp", "dp"), P(None, "dp", "mp"), P("mp", "dp"), P(None, ("dp", "mp"), None)),
        out_specs=(P(None, ("dp", "mp"), None), P(None, ("dp", "mp"), None), P(), P(None, "dp", "mp"), P(None, "mp"), P(None, "mp", "dp", None), P("mp"), P("mp", "dp"), P(None, "dp", "mp"), P("mp", "dp")),
        check_vma=False,
    )
```

```python
import functools

import jax
import jax.numpy as jnp
from jax import lax
from jax.experimental import pallas as pl
from jax.experimental.pallas import tpu as pltpu
from jax.sharding import PartitionSpec as P

MESH = pl.DeviceIdType.MESH
VMEM_LIMIT = 60 * 1024 * 1024


EPS = 1e-06
TP = 4
BF = jnp.bfloat16
F32 = jnp.float32


def plan():
    ndp = lax.axis_size("dp")
    ng = ndp // TP
    dp = lax.axis_index("dp")
    return ndp, ng, dp // ng, dp % ng


class Comm:
    def __init__(self, send, recv):
        self.send, self.recv, self.n = send, recv, 0
        self.ndp = lax.axis_size("dp")
        self.ng = self.ndp // TP
        dp = lax.axis_index("dp")
        self.t, self.g, self.m = dp // self.ng, dp % self.ng, lax.axis_index("mp")
        self.bits = [1 << k for k in range(self.ng.bit_length() - 1)]

    def at(self, t=None, g=None, m=None):
        t = self.t if t is None else t
        g = self.g if g is None else g
        return (t * self.ng + g, self.m if m is None else m)

    def flip(self, g, b):
        return g + b - 2 * b * ((g // b) % 2)

    def barrier(self):
        sem = pltpu.get_barrier_semaphore()
        partners = [self.at(t=(self.t + o) % TP) for o in range(1, TP)]
        partners += [self.at(g=self.flip(self.g, b)) for b in self.bits] + [self.at(m=1 - self.m)]
        for p in partners:
            pl.semaphore_signal(sem, inc=1, device_id=p, device_id_type=MESH)
        pl.semaphore_wait(sem, len(partners))

    def slot(self):
        self.n += 1
        return self.n - 1

    def to(self, src, dst, dev, slot):
        return pltpu.make_async_remote_copy(
            src_ref=src, dst_ref=dst, send_sem=self.send.at[slot], recv_sem=self.recv.at[slot],
            device_id=dev, device_id_type=MESH,
        )

    def local(self, src, dst, slot):
        return pltpu.make_async_copy(src, dst, self.send.at[slot])


def run(*flows):
    flows = list(flows)
    while flows:
        for f in list(flows):
            try:
                next(f)
            except StopIteration:
                flows.remove(f)


def ag_flow(c, own, full):
    t, m = c.t, c.m
    sib = c.at(m=1 - m)
    up = [c.slot() for _ in range(TP - 1)]
    down = [c.slot() for _ in range(TP - 1)]
    d2u = [c.slot() for _ in range(TP - 1)]
    d2d = [c.slot() for _ in range(TP - 1)]
    d2o, loc = c.slot(), c.slot()

    def up_copy(k):
        b = t - k
        return c.to(own if k == 0 else full.at[:, b, m], full.at[:, b, m], c.at(t=t + 1), up[k])

    def down_copy(k):
        b = t + k
        return c.to(own if k == 0 else full.at[:, b, m], full.at[:, b, m], c.at(t=t - 1), down[k])

    def side(b, slot, src=None):
        return c.to(full.at[:, b, m] if src is None else src, full.at[:, b, m], sib, slot)

    def got(b, slot, mm):
        return c.to(full.at[:, b, mm], full.at[:, b, mm], sib, slot)

    pl.when(t < TP - 1)(lambda: up_copy(0).start())
    pl.when(t > 0)(lambda: down_copy(0).start())
    side(t, d2o, own).start()
    c.local(own, full.at[:, t, m], loc).start()
    yield
    for k in range(TP - 1):
        def from_below():
            got(t - 1 - k, up[k], m).wait_recv()
            side(t - 1 - k, d2u[k]).start()
            if k < TP - 2:
                pl.when(t < TP - 1)(lambda: up_copy(k + 1).start())

        def from_above():
            got(t + 1 + k, down[k], m).wait_recv()
            side(t + 1 + k, d2d[k]).start()
            if k < TP - 2:
                pl.when(t > 0)(lambda: down_copy(k + 1).start())

        pl.when(t - 1 - k >= 0)(from_below)
        pl.when(t + 1 + k < TP)(from_above)
        yield
    c.local(own, full.at[:, t, m], loc).wait()
    side(t, d2o, own).wait_send()
    got(t, d2o, 1 - m).wait_recv()
    for k in range(TP - 1):
        pl.when((t < TP - 1) & (t - k >= 0))(lambda: up_copy(k).wait_send())
        pl.when((t > 0) & (t + k < TP))(lambda: down_copy(k).wait_send())

        def below():
            side(t - 1 - k, d2u[k]).wait_send()
            got(t - 1 - k, d2u[k], 1 - m).wait_recv()

        def above():
            side(t + 1 + k, d2d[k]).wait_send()
            got(t + 1 + k, d2d[k], 1 - m).wait_recv()

        pl.when(t - 1 - k >= 0)(below)
        pl.when(t + 1 + k < TP)(above)


def rs_scratch(rows, width):
    return [
        pltpu.VMEM((2, TP, rows, width), BF),
        pltpu.VMEM((2, TP - 1, 2, rows, width), BF),
        pltpu.VMEM((2, TP - 1, 2, rows, width), BF),
    ]


def rs_flow(c, part, out, sib, inbox, outbox):
    t, m = c.t, c.m
    n = part.shape[3]
    other = c.at(m=1 - m)
    lower = t < TP // 2
    u = jnp.where(lower, t, TP - 1 - t)
    da = jnp.where(lower, 0, 1)
    step = 1 - 2 * da
    near = [c.slot() for _ in range(TP)]
    base = c.n
    for _ in range(2 * (TP - 1)):
        c.slot()

    def real(d):
        return jnp.where(lower, d, TP - 1 - d)

    def cross(d):
        return c.to(part.at[:, real(d), 1 - m], sib.at[:, real(d)], other, near[d])

    def msg(flow, j):
        way = da if flow == 0 else 1 - da
        dev = c.at(t=t + step if flow == 0 else t - step)
        return c.to(outbox.at[way, j], inbox.at[way, j], dev, base + way * (TP - 1) + j)

    def add(d, into, terms):
        b = real(d)

        def rows16(i, _):
            sl = pl.ds(pl.multiple_of(i * 16, 16), 16)
            for s in range(2):
                v = part[s, b, m, sl, :].astype(F32) + sib[s, b, sl, :].astype(F32)
                for way, j in terms:
                    v = v + inbox[way, j, s, sl, :].astype(F32)
                into(s, sl, v)
            return 0

        lax.fori_loop(0, n // 16, rows16, 0)

    def put(way, j):
        def into(s, sl, v):
            outbox[way, j, s, sl, :] = v.astype(BF)
        return into

    def final(s, sl, v):
        out[s, sl, :] = v

    for d in (3, 2, 0, 1):
        cross(d).start()
    yield
    for d, j in ((3, 0), (2, 1)):
        cross(d).wait_recv()
        for lvl in range(2):
            def go():
                if lvl == 1:
                    msg(0, j).wait_recv()
                add(d, put(da, j), [(da, j)] if lvl else [])
                msg(0, j).start()
            pl.when(u == lvl)(go)
        yield
    cross(0).wait_recv()
    cross(1).wait_recv()

    def first():
        add(1, put(da, 2), [])
        msg(0, 2).start()

    pl.when(u == 0)(first)

    def back():
        msg(1, 0).wait_recv()
        add(0, put(1 - da, 0), [(1 - da, 0)])
        msg(1, 0).start()

    pl.when(u == 1)(back)
    yield

    def end0():
        msg(1, 0).wait_recv()
        add(0, final, [(1 - da, 0)])

    def end1():
        msg(0, 2).wait_recv()
        msg(1, 1).wait_recv()
        add(1, final, [(da, 2), (1 - da, 1)])

    pl.when(u == 0)(end0)
    pl.when(u == 1)(end1)
    for d in range(TP):
        cross(d).wait_send()
    for j in range(2):
        msg(0, j).wait_send()
    pl.when(u == 0)(lambda: msg(0, 2).wait_send())
    pl.when(u == 1)(lambda: msg(1, 0).wait_send())


def spread_z(c, src, dst, need=None):
    slots = [c.slot() for _ in range(TP)]

    def copy(o):
        to = (c.t + o) % TP
        return c.to(src(to), dst(c.t), c.at(t=to), slots[o])

    def mine():
        return c.local(src(c.t), dst(c.t), slots[0])

    def back(o):
        frm = (c.t + TP - o) % TP
        return c.to(src(frm), dst(frm), c.at(t=frm), slots[o])

    def when(t, f):
        if need is None:
            f()
        else:
            pl.when(t == need)(f)

    for o in range(1, TP):
        when((c.t + o) % TP, lambda: copy(o).start())
    when(c.t, lambda: mine().start())
    yield
    when(c.t, lambda: mine().wait())
    for o in range(1, TP):
        when(c.t, lambda: back(o).wait_recv())
    yield
    for o in range(1, TP):
        when((c.t + o) % TP, lambda: copy(o).wait_send())


def plane_gather(c, block, order):
    have = [0]
    done = []
    for b in order:
        dev = c.at(g=c.flip(c.g, b))
        sent = []
        for x in have:
            gg = c.g
            for bit in c.bits:
                if x & bit:
                    gg = c.flip(gg, bit)
            copy = c.to(block(gg), block(gg), dev, c.slot())
            copy.start()
            sent.append(copy)
        yield
        for copy in sent:
            copy.wait_recv()
        done += sent
        have = have + [x ^ b for x in have]
    for copy in done:
        copy.wait_send()


def plane_reduce(c, own, sums, inbox, order):
    def place(x):
        gg = c.g
        for bit in c.bits:
            if x & bit:
                gg = c.flip(gg, bit)
        return gg

    left = list(range(c.ng))
    spot = {}
    done = []
    base = 0
    for k, b in enumerate(order):
        dev = c.at(g=c.flip(c.g, b))
        away = [x for x in left if x & b]
        left = [x for x in left if not x & b]
        sent = []
        for i, x in enumerate(away):
            src = own(place(x)) if k == 0 else sums.at[spot[x]]
            copy = c.to(src, inbox.at[base + i], dev, c.slot())
            copy.start()
            sent.append(copy)
        held = []
        if k == 0:
            spot = {x: i for i, x in enumerate(left)}
            for x in left:
                held.append(c.local(own(place(x)), sums.at[spot[x]], c.slot()))
                held[-1].start()
        yield
        for i, x in enumerate(left):
            sent[i].wait_recv()
            if k == 0:
                held[i].wait()
            add_blocks(sums.at[spot[x]], inbox.at[base + i])
        base += len(away)
        done += sent
    for copy in done:
        copy.wait_send()


def add_blocks(a, b):
    def one(i, _):
        a[i] = (a[i].astype(F32) + b[i].astype(F32)).astype(BF)
        return 0

    lax.fori_loop(0, a.shape[0], one, 0)


def call(kernel, out_shape, in_specs, out_specs, scratch, cid, slots=160):
    return pl.pallas_call(
        kernel,
        out_shape=out_shape,
        in_specs=in_specs,
        out_specs=out_specs,
        scratch_shapes=list(scratch) + [pltpu.SemaphoreType.DMA((slots,)), pltpu.SemaphoreType.DMA((slots,))],
        compiler_params=pltpu.CompilerParams(collective_id=cid, has_side_effects=True, vmem_limit_bytes=VMEM_LIMIT),
    )


HBM = pl.BlockSpec(memory_space=pl.ANY)
VM = pl.BlockSpec(memory_space=pltpu.VMEM)


def start_kernel(x, go, gain, wbr, wot, gates, mlp, full_a, full_g, wb, wo, gb, wm, own, zero, send, recv):
    c = Comm(send, recv)
    c.barrier()
    r = wbr.shape[1]

    def head(ref, lead):
        def src(t):
            lane = pl.multiple_of(t * 256, 256)
            return ref.at[(*lead, slice(None), pl.ds(lane, 256))]
        return src

    pieces = []
    for k in range(2):
        pieces.append((head(wbr, (k,)), wb, (k,), wbr.at[k, :, pl.ds(1024, 256)]))
    pieces.append((head(wot, ()), wo, (), wot.at[:, pl.ds(1024, 256)]))
    z = []
    for src, dst, lead, extra in pieces:
        z.append(spread_z(c, src, lambda t, dst=dst, lead=lead: dst.at[(*lead, t, c.g, slice(None), pl.ds(0, 256))]))
        z.append(spread_z(c, lambda t, extra=extra: extra, lambda t, dst=dst, lead=lead: dst.at[(*lead, t, c.g, slice(None), pl.ds(256, 256))], 1))
    z.append(spread_z(c, lambda t: gates.at[:, t], lambda t: gb.at[:, 0, t, c.g]))
    z.append(spread_z(c, lambda t: gates.at[:, 4], lambda t: gb.at[:, 1, t, c.g], 1))
    for f in z:
        next(f)
    x32 = [x[s].astype(F32) for s in range(2)]
    for s in range(2):
        v = x32[s] * lax.rsqrt(jnp.mean(x32[s] * x32[s], axis=-1, keepdims=True) + EPS) * gain[...]
        own[s] = v.astype(BF)
    ag = ag_flow(c, own, full_a)
    next(ag)
    zero[...] = jnp.zeros_like(zero)
    fills = []
    for k in range(2):
        fills.append((zero, wb.at[k, :, c.g, :, pl.ds(256, 256)], c.slot()))
    fills.append((zero, wo.at[:, c.g, :, pl.ds(256, 256)], c.slot()))
    for k in range(2):
        fills.append((zero.at[:, pl.ds(0, gates.shape[2])], gb.at[k, 1, :, c.g], c.slot()))

    def fill():
        for f in fills:
            c.local(*f).start()
        for f in fills:
            c.local(*f).wait()

    pl.when(c.t != 1)(fill)
    zm = [spread_z(c, lambda t, k=k: mlp.at[t, k], lambda t, k=k: wm.at[k, t, c.g]) for k in range(3)]
    for f in z:
        next(f)
    fwd, rev = c.bits, c.bits[::-1]
    g1 = [plane_gather(c, lambda g: wb.at[0, :, g], fwd), plane_gather(c, lambda g: wb.at[1, :, g], rev),
          plane_gather(c, lambda g: wo.at[pl.ds(0, 2), g], fwd), plane_gather(c, lambda g: wo.at[pl.ds(2, 2), g], rev),
          plane_gather(c, lambda g: gb.at[0, :, :, g], fwd), plane_gather(c, lambda g: gb.at[1, :, :, g], rev)]
    for f in g1:
        next(f)
    next(ag)
    ag2 = ag_flow(c, go, full_g)
    for f in zm:
        next(f)
    for f in g1:
        next(f)
    run(ag)
    next(ag2)
    for f in zm:
        next(f)
    g2 = [plane_gather(c, lambda g: wm.at[0, :, g], fwd), plane_gather(c, lambda g: wm.at[1, :, g], rev),
          plane_gather(c, lambda g: wm.at[2, pl.ds(0, 2), g], fwd), plane_gather(c, lambda g: wm.at[2, pl.ds(2, 2), g], rev)]
    run(*z, *zm, *g1, *g2, ag2)


def start_call(x, go, gain, wbr, wot, gates, mlp):
    ng = lax.axis_size("dp") // TP
    _, n, d = x.shape
    r, gr, fs = wbr.shape[1], gates.shape[2], mlp.shape[3]
    S = jax.ShapeDtypeStruct
    return call(
        start_kernel,
        (S((2, TP, 2, n, d), BF), S((2, TP, 2, n, d), BF), S((2, TP, ng, r, 512), BF), S((TP, ng, r, 512), BF),
         S((2, 2, TP, ng, gr, 256), BF), S((3, TP, ng, r, fs), BF)),
        [VM, VM, VM, HBM, HBM, HBM, HBM],
        (HBM,) * 6,
        [pltpu.VMEM((2, n, d), BF), pltpu.VMEM((TP, r, 256), BF)],
        1,
    )(x, go, gain[None], wbr, wot, gates, mlp)


def mid_kernel(part, x, gain, res, full, tot, own, sib, inbox, outbox, send, recv):
    c = Comm(send, recv)
    c.barrier()
    run(rs_flow(c, part, tot, sib, inbox, outbox))
    for s in range(2):
        v = x[s].astype(F32) + tot[s]
        res[s] = v
        own[s] = (v * lax.rsqrt(jnp.mean(v * v, axis=-1, keepdims=True) + EPS) * gain[...]).astype(BF)
    run(ag_flow(c, own, full))


def mid_call(part, x, gain):
    _, n, d = x.shape
    S = jax.ShapeDtypeStruct
    return call(
        mid_kernel,
        (S((2, n, d), F32), S((2, TP, 2, n, d), BF)),
        [VM, VM, VM],
        (VM, HBM),
        [pltpu.VMEM((2, n, d), F32), pltpu.VMEM((2, n, d), BF)] + rs_scratch(n, d),
        2,
    )(part.reshape(2, TP, 2, n, d), x, gain[None])


def back_kernel(part, part2, res, go, gain, gres, gsum, mlp_own, full, tot, own, sib, inbox, outbox, sib2, inbox2, outbox2, send, recv):
    c = Comm(send, recv)
    c.barrier()
    run(rs_flow(c, part, tot, sib, inbox, outbox))
    total = jnp.zeros_like(gsum)
    for s in range(2):
        v = res[s]
        scale = lax.rsqrt(jnp.mean(v * v, axis=-1, keepdims=True) + EPS)
        normal = v * scale
        gn = tot[s]
        total = total + jnp.sum(gn * normal, axis=0, keepdims=True)
        q = gn * gain[...]
        gr = scale * (q - normal * jnp.mean(q * normal, axis=-1, keepdims=True)) + go[s].astype(F32)
        gres[s] = gr
        own[s] = gr.astype(BF)
    gsum[...] = total
    run(ag_flow(c, own, full), rs_flow(c, part2, mlp_own, sib2, inbox2, outbox2))


def back_call(part, part2, res, go, gain):
    _, n, d = go.shape
    S = jax.ShapeDtypeStruct
    shape = (2, TP, 2, n, d)
    return call(
        back_kernel,
        (S((2, n, d), F32), S((1, d), F32), S((2, n, d), F32), S(shape, BF)),
        [VM] * 5,
        (VM, VM, VM, HBM),
        [pltpu.VMEM((2, n, d), F32), pltpu.VMEM((2, n, d), BF)] + rs_scratch(n, d) + rs_scratch(n, d),
        3,
    )(part.reshape(shape), part2.reshape(shape), res, go, gain[None])


def small_flow(c, small, inbox, zbox, sbox, gains, table):
    for k, b in enumerate(c.bits):
        copy = c.to(small.at[k], inbox.at[k], c.at(g=c.flip(c.g, b)), c.slot())
        copy.start()
        yield
        copy.wait()
        small[k + 1] = small[k] + inbox[k]
    last = len(c.bits)
    z = spread_z(c, lambda t: small.at[last], lambda t: zbox.at[t])
    next(z)
    yield
    run(z)
    sbox[0] = zbox[0, 0:8] + zbox[1, 0:8] + zbox[2, 0:8] + zbox[3, 0:8]
    table[...] = zbox[:, 8:16, 0:512]
    copy = c.to(sbox.at[0], sbox.at[1], c.at(m=1 - c.m), c.slot())
    copy.start()
    yield
    copy.wait()
    gains[...] = sbox[0] + sbox[1]


def end_kernel(part, x, gres, gain, gwb, gwo, ggb, gwm, gain_b, chan_rows, gin, gains, table, owb, owo, ogb, owm,
               small, small_in, zbox, sbox, tot, sib, inbox, outbox, su_m, in_m, su_x, in_x, su_g, in_g, send, recv):
    c = Comm(send, recv)
    c.barrier()
    fwd, rev = c.bits, c.bits[::-1]
    red, spread = [], []
    for k in range(3):
        own = lambda g, k=k: gwm.at[k, :, g]
        red.append(plane_reduce(c, own, su_m.at[k], in_m.at[k], rev if k % 2 else fwd))
        spread.append(spread_z(c, lambda t, k=k: su_m.at[k, 0, t], lambda t, k=k: owm.at[k, t]))
    for k in range(3):
        own = (lambda g, k=k: gwb.at[k, :, g]) if k < 2 else (lambda g: gwo.at[:, g])
        out = (lambda t, k=k: owb.at[k, t]) if k < 2 else (lambda t: owo.at[t])
        red.append(plane_reduce(c, own, su_x.at[k], in_x.at[k], fwd if k % 2 else rev))
        spread.append(spread_z(c, lambda t, k=k: su_x.at[k, 0, t], out))
    for k in range(2):
        for h in range(2):
            i = 2 * k + h
            red.append(plane_reduce(c, lambda g, k=k, h=h: ggb.at[k, h, :, g], su_g.at[i], in_g.at[i], fwd if k else rev))
            spread.append(spread_z(c, lambda t, i=i: su_g.at[i, 0, t], lambda t, k=k, h=h: ogb.at[k, h, t]))
    rs = rs_flow(c, part, tot, sib, inbox, outbox)
    next(rs)
    for f in red:
        next(f)
    run(rs)
    total = jnp.zeros_like(gain)
    for s in range(2):
        v = x[s].astype(F32)
        scale = lax.rsqrt(jnp.mean(v * v, axis=-1, keepdims=True) + EPS)
        normal = v * scale
        gn = tot[s]
        total = total + jnp.sum(gn * normal, axis=0, keepdims=True)
        q = gn * gain[...]
        gin[s] = scale * (q - normal * jnp.mean(q * normal, axis=-1, keepdims=True)) + gres[s]
    small[0] = jnp.zeros_like(small[0])
    small[0, 0:1, :] = total
    small[0, 1:2, :] = gain_b[...]
    small[0, 8:16, 0:512] = chan_rows[...]
    sm = small_flow(c, small, small_in, zbox, sbox, gains, table)
    next(sm)
    for _ in range(len(c.bits) - 1):
        for f in red:
            next(f)
        next(sm)
    for f, s in zip(red, spread):
        run(f)
        next(s)
    run(sm, *spread)


def end_call(part, x, gres, gain, gwb, gwo, ggb, gwm, gain_b, chan_rows):
    _, n, d = x.shape
    ng = lax.axis_size("dp") // TP
    r, gr, fs = gwb.shape[3], ggb.shape[4], gwm.shape[4]
    S = jax.ShapeDtypeStruct
    half = ng // 2

    def sets(k, rows, width):
        return [pltpu.VMEM((k, half, TP, rows, width), BF), pltpu.VMEM((k, ng - 1, TP, rows, width), BF)]

    return call(
        end_kernel,
        (S((2, n, d), F32), S((8, d), F32), S((TP, 8, 512), F32), S((2, TP, r, 512), BF), S((TP, r, 512), BF), S((2, 2, TP, gr, 256), BF), S((3, TP, r, fs), BF)),
        [VM] * 4 + [HBM] * 4 + [VM] * 2,
        (VM,) * 3 + (HBM,) * 4,
        [pltpu.VMEM((ng.bit_length(), 16, d), F32), pltpu.VMEM((ng.bit_length() - 1, 16, d), F32), pltpu.VMEM((TP, 16, d), F32), pltpu.VMEM((2, 8, d), F32)]
        + [pltpu.VMEM((2, n, d), F32)] + rs_scratch(n, d) + sets(3, r, fs) + sets(3, r, 512) + sets(4, gr, 256),
        4, 400,
    )(part.reshape(2, TP, 2, n, d), x, gres, gain[None], gwb, gwo, ggb, gwm, gain_b, chan_rows)


def heads_of(a, axis):
    _, _, t, _ = plan()
    p = lax.dynamic_slice_in_dim(a, t * 256, 256, axis)
    q = lax.dynamic_slice_in_dim(a, 1024, 256, axis)
    q = jnp.where(t == 1, q, jnp.zeros_like(q))
    return jnp.concatenate([p, q], axis)


def gelu_pair(v):
    k = 0.7978845608028654
    v2 = v * v
    th = jnp.tanh(k * v * (1.0 + 0.044715 * v2))
    half = 0.5 * (1.0 + th)
    return v * half, half + 0.5 * v * (1.0 - th * th) * k * (1.0 + 3.0 * 0.044715 * v2)


def decay_terms(ga, db):
    log_a = -8.0 * ga * db
    y = 2.0 * log_a
    series = 1.0 + y * (1 / 8)
    for k in range(7, 1, -1):
        series = 1.0 + y * (1 / k) * series
    m1 = jnp.where(y > -0.35, y * series, jnp.exp(y) - 1.0)
    return jnp.exp(log_a), jnp.sqrt(-m1)


def lanes_in(ref, rows, v):
    for q in range(ref.shape[0]):
        ref[q, rows, :] = v[:, q * 128:(q + 1) * 128]


def lanes_out(ref, rows):
    return jnp.concatenate([ref[q, rows, :] for q in range(ref.shape[0])], axis=1)


def each(ref, at):
    return [ref[q, at, :] for q in range(ref.shape[0])]


def split(v):
    return [v[:, q * 128:(q + 1) * 128] for q in range(v.shape[1] // 128)]


def plane_partners(c):
    return [c.at(g=(c.g + o) % c.ng) for o in range(1, c.ng)]


def greet(partners):
    sem = pltpu.get_barrier_semaphore()
    for p in partners:
        pl.semaphore_signal(sem, inc=1, device_id=p, device_id_type=MESH)
    pl.semaphore_wait(sem, len(partners))


def share(c, table):
    copies = []
    for o in range(1, c.ng):
        slot = c.slot()
        copies.append((o, slot))
        c.to(table.at[c.g], table.at[c.g], c.at(g=(c.g + o) % c.ng), slot).start()
    for o, slot in copies:
        frm = (c.g + c.ng - o) % c.ng
        c.to(table.at[frm], table.at[frm], c.at(g=frm), slot).wait_recv()
    for o, slot in copies:
        c.to(table.at[c.g], table.at[c.g], c.at(g=(c.g + o) % c.ng), slot).wait_send()


def entering(c, prod, last, width, reverse):
    rows = [None] * (2 * TP)
    spots = [(t, g) for t in range(TP) for g in range(c.ng)]
    for s in range(2):
        cur = jnp.zeros((1, width), F32)
        for t, g in (spots[::-1] if reverse else spots):
            b = s * TP + t
            old = rows[b]
            rows[b] = cur if old is None else jnp.where(c.g == g, cur, old)
            cur = last(g)[b:b + 1] + prod(g)[b:b + 1] * cur
    return jnp.concatenate(rows, axis=0)


def mix_fwd_kernel(br0, ci, gb, chan, db, mixed, conv, gates, state, rim, carry, table, a_ref, d_ref, ext, rim_in, send, recv):
    c = Comm(send, recv)
    greet(plane_partners(c))
    n, width = ci.shape[1], ci.shape[2]
    rslot = c.slot()
    out = c.to(ci.at[:, pl.ds(n - 16, 16)], rim_in, c.at(g=(c.g + 1) % c.ng), rslot)
    out.start()
    out.wait()
    row = lax.broadcasted_iota(jnp.int32, (n, 1), 0)
    for b in range(2 * TP):
        t = b % TP
        same = rim_in[b].astype(F32)[8:]
        prev = jnp.zeros_like(same) if t == 0 else rim_in[b - 1].astype(F32)[8:]
        head = jnp.where(c.g == 0, prev, same)
        rim[b] = head
        ext[b % 2, pl.ds(0, 8), :] = head
        ext[b % 2, pl.ds(8, n), :] = ci[b].astype(F32)
        cv = chan[4:5] + chan[0:1] * ext[b % 2, pl.ds(8, n), :] + chan[1:2] * ext[b % 2, pl.ds(7, n), :]
        cv = cv + chan[2:3] * ext[b % 2, pl.ds(6, n), :] + chan[3:4] * ext[b % 2, pl.ds(5, n), :]
        low = cv.astype(BF)
        rows = pl.ds(b * n, n)
        conv[rows, :] = low
        cv = low.astype(F32)
        gv = []
        for k in range(2):
            pre = jnp.concatenate([jnp.dot(low[:, h * 256:(h + 1) * 256], gb[k, h], preferred_element_type=F32) for h in range(2)], axis=1)
            v = jax.nn.sigmoid(pre + chan[5 + k:6 + k])
            gates[k, rows, :] = v
            gv.append(v)
        decay, mult = decay_terms(gv[1], db[...])
        if t == 0:
            mult = jnp.where((row == 0) & (c.g == 0), 1.0, mult)
        lanes_in(a_ref, rows, decay)
        lanes_in(d_ref, rows, cv * gv[0] * mult)

    def step1(r, ph):
        at = pl.ds(r, 2 * TP, stride=n)
        return [(p * av, h * av + dv) for (p, h), av, dv in zip(ph, each(a_ref, at), each(d_ref, at))]

    one = jnp.ones((2 * TP, 128), F32)
    ph = lax.fori_loop(0, n, step1, [(one, 0.0 * one)] * (width // 128), unroll=8)
    p = jnp.concatenate([v[0] for v in ph], axis=1)
    h = jnp.concatenate([v[1] for v in ph], axis=1)
    table[c.g, 0] = p
    table[c.g, 1] = h
    share(c, table)
    cin = entering(c, lambda g: table[g, 0], lambda g: table[g, 1], width, False)
    carry[...] = cin

    def step2(r, hs):
        at = pl.ds(r, 2 * TP, stride=n)
        hs = [h * av + dv for h, av, dv in zip(hs, each(a_ref, at), each(d_ref, at))]
        for q, h in enumerate(hs):
            d_ref[q, at, :] = h
        return hs

    lax.fori_loop(0, n, step2, split(cin), unroll=8)
    for b in range(2 * TP):
        rows = pl.ds(b * n, n)
        v = lanes_out(d_ref, rows)
        state[rows, :] = v
        mixed[rows, :] = (v * gelu_pair(br0[rows, :])[0]).astype(BF)


def mix_fwd_call(br0, ci, gb, chan, db):
    ng = lax.axis_size("dp") // TP
    rows, width = br0.shape
    n = rows // (2 * TP)
    S = jax.ShapeDtypeStruct
    return call(
        mix_fwd_kernel,
        (S((rows, width), BF), S((rows, width), BF), S((2, rows, width), F32), S((rows, width), F32),
         S((2 * TP, 8, width), F32), S((2 * TP, width), F32), S((ng, 2, 2 * TP, width), F32)),
        [VM] * 5,
        (VM,) * 7,
        [pltpu.VMEM((width // 128, rows, 128), F32), pltpu.VMEM((width // 128, rows, 128), F32), pltpu.VMEM((2, n + 8, width), F32), pltpu.VMEM((2 * TP, 16, width), BF)],
        5, 32,
    )(br0, ci.reshape(2 * TP, n, width), gb, chan, db[None])


def mix_bwd_kernel(gm, br0, ci, gb, chan, db, conv, gates, state, rim, carry, table, gbr, ggb, sums,
                   a_ref, adj, gc, gpl, ext, heads, etab, rim_in, send, recv):
    c = Comm(send, recv)
    greet(plane_partners(c))
    n, width = ci.shape[1], ci.shape[2]
    for b in range(2 * TP):
        rows = pl.ds(b * n, n)
        act, slope = gelu_pair(br0[rows, :])
        g = gm[rows, :]
        lanes_in(adj, rows, g * act)
        gbr[0, rows, :] = (g * state[rows, :] * slope).astype(BF)
        lanes_in(a_ref, rows, jnp.exp(-8.0 * gates[1, rows, :] * db[...]))

    def step1(i, es):
        at = pl.ds(n - 1 - i, 2 * TP, stride=n)
        return [(v + e) * av for v, e, av in zip(each(adj, at), es, each(a_ref, at))]

    e = lax.fori_loop(0, n, step1, [jnp.zeros((2 * TP, 128), F32)] * (width // 128), unroll=8)
    e = jnp.concatenate(e, axis=1)
    etab[c.g] = e
    share(c, etab)
    ein = entering(c, lambda g: table[g, 0], lambda g: etab[g], width, True)

    def step2(i, es):
        at = pl.ds(n - 1 - i, 2 * TP, stride=n)
        vs = [v + e for v, e in zip(each(adj, at), es)]
        for q, v in enumerate(vs):
            adj[q, at, :] = v
        return [v * av for v, av in zip(vs, each(a_ref, at))]

    lax.fori_loop(0, n, step2, split(ein), unroll=8)
    row = lax.broadcasted_iota(jnp.int32, (n, 1), 0)
    total = [jnp.zeros((1, width), F32) for _ in range(8)]
    for b in range(2 * TP):
        rows = pl.ds(b * n, n)
        first = (row == 0) & (c.g == 0) if b % TP == 0 else None
        ad = lanes_out(adj, rows)
        gx, ga = gates[0, rows, :], gates[1, rows, :]
        decay, root = decay_terms(ga, db[...])
        mult = root if first is None else jnp.where(first, 1.0, root)
        cv = conv[rows, :].astype(F32)
        before = jnp.where(row == 0, carry[b:b + 1, :], pltpu.roll(state[rows, :], 1, 0))
        gmult = -(ad * cv * gx) * (decay * decay) / root
        if first is not None:
            gmult = jnp.where(first, 0.0, gmult)
        glog = ad * before * decay + gmult
        total[7] = total[7] + jnp.sum(glog * (-8.0 * ga), axis=0, keepdims=True)
        pre = [ad * cv * mult * gx * (1.0 - gx), glog * (-8.0 * db[...]) * ga * (1.0 - ga)]
        conved = ad * gx * mult
        for k in range(2):
            total[5 + k] = total[5 + k] + jnp.sum(pre[k], axis=0, keepdims=True)
            low = pre[k].astype(BF)
            gpl[k, rows, :] = low
            conved = conved + jnp.concatenate([
                lax.dot_general(low[:, h * 256:(h + 1) * 256], gb[k, h], (((1,), (1,)), ((), ())), preferred_element_type=F32)
                for h in range(2)], axis=1)
        gc[b, pl.ds(0, n), :] = conved
        heads[b] = conved[:8]
        ext[b % 2, pl.ds(0, 8), :] = rim[b]
        ext[b % 2, pl.ds(8, n), :] = ci[b].astype(F32)
        for k in range(4):
            total[k] = total[k] + jnp.sum(conved * ext[b % 2, pl.ds(8 - k, n), :], axis=0, keepdims=True)
        total[4] = total[4] + jnp.sum(conved, axis=0, keepdims=True)
    rslot = c.slot()
    out = c.to(heads, rim_in, c.at(g=(c.g + c.ng - 1) % c.ng), rslot)
    out.start()
    sums[...] = jnp.concatenate(total, axis=0)
    for k in range(2):
        for h in range(2):
            ggb[k, h] = lax.dot_general(conv[:, h * 256:(h + 1) * 256], gpl[k, :, h * 256:(h + 1) * 256], (((0,), (0,)), ((), ())), preferred_element_type=F32)
    out.wait()
    for b in range(2 * TP):
        rows = pl.ds(b * n, n)
        same = rim_in[b]
        nxt = jnp.zeros_like(same) if b % TP == TP - 1 else rim_in[b + 1]
        gc[b, pl.ds(n, 8), :] = jnp.where(c.g == c.ng - 1, nxt, same)
        v = chan[0:1] * gc[b, pl.ds(0, n), :]
        for k in range(1, 4):
            v = v + chan[k:k + 1] * gc[b, pl.ds(k, n), :]
        gbr[1, rows, :] = v.astype(BF)


def mix_bwd_call(gm, br0, ci, gb, chan, db, saved):
    ng = lax.axis_size("dp") // TP
    rows, width = br0.shape
    n = rows // (2 * TP)
    S = jax.ShapeDtypeStruct
    V = pltpu.VMEM
    return call(
        mix_bwd_kernel,
        (S((2, rows, width), BF), S((2, 2, 256, 256), F32), S((8, width), F32)),
        [VM] * 12,
        (VM,) * 3,
        [V((width // 128, rows, 128), F32), V((width // 128, rows, 128), F32), V((2 * TP, n + 8, width), F32), V((2, rows, width), BF),
         V((2, n + 8, width), F32), V((2 * TP, 8, width), F32), V((ng, 2 * TP, width), F32), V((2 * TP, 8, width), F32)],
        6, 32,
    )(gm, br0, ci.reshape(2 * TP, n, width), gb, chan, db[None], *saved)


def dot(a, b, ca, cb):
    return lax.dot_general(a, b, (((ca,), (cb,)), ((), ())), preferred_element_type=F32)


def pack(parts):
    return jnp.stack(parts)


def body(block_input, lengths, norm_gains, w_branch, channel_params, gate_blocks, decay_param, w_out, w_mlp, w_down, out_grad):
    ndp, ng, t, g = plan()
    dp, mp = lax.axis_index("dp"), lax.axis_index("mp")
    rows, width = block_input.shape[1:]
    r = w_branch.shape[1]
    fs = w_mlp.shape[2] // TP
    chan = heads_of(channel_params, 1)
    dpar = heads_of(decay_param[None], 1)[0]
    decay_base = jax.nn.softplus(dpar)
    pos = dp * 2 * rows + mp * rows + jnp.arange(rows, dtype=jnp.int32)
    valid = (pos[None] < lengths[:, None])[..., None]
    x = block_input
    grad_own = jnp.where(valid, out_grad, jnp.zeros_like(out_grad))
    mlp = jnp.concatenate([w_mlp, w_down.T[None]], 0).reshape(3, r, TP, fs).transpose(2, 0, 1, 3)
    na, go, wb, wo, gb, wm = start_call(x, grad_own, norm_gains[0], w_branch, w_out.T, gate_blocks, mlp)
    na, go = na.reshape(-1, width), go.reshape(-1, width)
    wb, wo, wm = wb.reshape(2, width, 512), wo.reshape(width, 512), wm.reshape(3, width, fs)
    gb = gb.reshape(2, 2, 256, 256)
    wd = wm[2]
    branch0 = dot(na, wb[0], 1, 0)
    conv_input = dot(na, wb[1], 1, 0).astype(BF)
    mixed, *saved = mix_fwd_call(branch0, conv_input, gb, chan, decay_base)
    residual, nb = mid_call(dot(mixed, wo, 1, 1).astype(BF), x, norm_gains[1])
    nb = nb.reshape(-1, width)
    first, second = dot(nb, wm[0], 1, 0), dot(nb, wm[1], 1, 0)
    act, act_pull = jax.vjp(jax.nn.gelu, first)
    hidden = (act * second).astype(BF)
    mlp_part = dot(hidden, wd, 1, 1).astype(BF)
    gh = dot(go, wd, 1, 0)
    gwd = dot(go, hidden, 0, 0).astype(BF)
    ggu = [act_pull(gh * second)[0].astype(BF), (gh * act).astype(BF)]
    gwm = [dot(nb, ggu[k], 0, 0).astype(BF) for k in range(2)]
    gnb = (dot(ggu[0], wm[0], 1, 1) + dot(ggu[1], wm[1], 1, 1)).astype(BF)
    gres, gain_b, mlp_own, gmo = back_call(gnb, mlp_part, residual, grad_own, norm_gains[1])
    out = jnp.where(valid, residual + mlp_own, 0.0).astype(BF)
    gmo = gmo.reshape(-1, width)
    gwo = dot(gmo, mixed, 0, 0).astype(BF)
    gbr, ggb, chan_rows = mix_bwd_call(dot(gmo, wo, 1, 0), branch0, conv_input, gb, chan, decay_base, saved)
    gwb = [dot(na, gbr[k], 0, 0).astype(BF) for k in range(2)]
    gna = (dot(gbr[0], wb[0], 1, 1) + dot(gbr[1], wb[1], 1, 1)).astype(BF)
    gr = gate_blocks.shape[2]
    gin, gains, table, owb, owo, ogb, owm = end_call(
        gna, x, gres, norm_gains[0],
        jnp.stack(gwb).reshape(2, TP, ng, r, 512), gwo.reshape(TP, ng, r, 512),
        ggb.astype(BF).reshape(2, 2, TP, ng, gr, 256), jnp.stack(gwm + [gwd]).reshape(3, TP, ng, r, fs), gain_b, chan_rows,
    )
    owb, owo = owb.astype(F32), owo.astype(F32)
    g_wb = jnp.concatenate([owb[:, i, :, :256] for i in range(TP)] + [owb[:, 1, :, 256:]], -1)
    g_wo = jnp.concatenate([owo[i, :, :256] for i in range(TP)] + [owo[1, :, 256:]], -1).T
    g_gb = jnp.concatenate([ogb[:, 0], ogb[:, 1, 1:2]], 1).astype(F32)
    g_wm = owm[:2].transpose(0, 2, 1, 3).reshape(2, r, TP * fs).astype(F32)
    g_wd = owm[2].transpose(0, 2, 1).reshape(TP * fs, r).astype(F32)
    crow = jnp.concatenate([table[i, :, :256] for i in range(TP)] + [table[1, :, 256:]], -1)
    return out, gin, gains[:2], g_wb, crow[:7], g_gb, crow[7] * jax.nn.sigmoid(decay_param), g_wo, g_wm, g_wd


def solution(mesh):
    return jax.shard_map(
        body,
        mesh=mesh,
        in_specs=(P(None, ("dp", "mp"), None), P(), P(), P(None, "dp", "mp"), P(None, "mp"), P(None, "mp", "dp", None), P("mp"), P("mp", "dp"), P(None, "dp", "mp"), P("mp", "dp"), P(None, ("dp", "mp"), None)),
        out_specs=(P(None, ("dp", "mp"), None), P(None, ("dp", "mp"), None), P(), P(None, "dp", "mp"), P(None, "mp"), P(None, "mp", "dp", None), P("mp"), P("mp", "dp"), P(None, "dp", "mp"), P("mp", "dp")),
        check_vma=False,
    )
```

```python
import functools

import jax
import jax.numpy as jnp
from jax import lax
from jax.experimental import pallas as pl
from jax.experimental.pallas import tpu as pltpu
from jax.sharding import PartitionSpec as P

MESH = pl.DeviceIdType.MESH
VMEM_LIMIT = 60 * 1024 * 1024


EPS = 1e-06
TP = 4
BF = jnp.bfloat16
F32 = jnp.float32


def plan():
    ndp = lax.axis_size("dp")
    ng = ndp // TP
    dp = lax.axis_index("dp")
    return ndp, ng, dp // ng, dp % ng


class Comm:
    def __init__(self, send, recv):
        self.send, self.recv, self.n = send, recv, 0
        self.ndp = lax.axis_size("dp")
        self.ng = self.ndp // TP
        dp = lax.axis_index("dp")
        self.t, self.g, self.m = dp // self.ng, dp % self.ng, lax.axis_index("mp")
        self.bits = [1 << k for k in range(self.ng.bit_length() - 1)]

    def at(self, t=None, g=None, m=None):
        t = self.t if t is None else t
        g = self.g if g is None else g
        return (t * self.ng + g, self.m if m is None else m)

    def flip(self, g, b):
        return g + b - 2 * b * ((g // b) % 2)

    def barrier(self):
        sem = pltpu.get_barrier_semaphore()
        partners = [self.at(t=(self.t + o) % TP) for o in range(1, TP)]
        partners += [self.at(g=self.flip(self.g, b)) for b in self.bits] + [self.at(m=1 - self.m)]
        for p in partners:
            pl.semaphore_signal(sem, inc=1, device_id=p, device_id_type=MESH)
        pl.semaphore_wait(sem, len(partners))

    def slot(self):
        self.n += 1
        return self.n - 1

    def to(self, src, dst, dev, slot):
        return pltpu.make_async_remote_copy(
            src_ref=src, dst_ref=dst, send_sem=self.send.at[slot], recv_sem=self.recv.at[slot],
            device_id=dev, device_id_type=MESH,
        )

    def local(self, src, dst, slot):
        return pltpu.make_async_copy(src, dst, self.send.at[slot])


def run(*flows):
    flows = list(flows)
    while flows:
        for f in list(flows):
            try:
                next(f)
            except StopIteration:
                flows.remove(f)


def ag_flow(c, own, full):
    t, m = c.t, c.m
    sib = c.at(m=1 - m)
    up = [c.slot() for _ in range(TP - 1)]
    down = [c.slot() for _ in range(TP - 1)]
    d2u = [c.slot() for _ in range(TP - 1)]
    d2d = [c.slot() for _ in range(TP - 1)]
    d2o, loc = c.slot(), c.slot()

    def up_copy(k):
        b = t - k
        return c.to(own if k == 0 else full.at[:, b, m], full.at[:, b, m], c.at(t=t + 1), up[k])

    def down_copy(k):
        b = t + k
        return c.to(own if k == 0 else full.at[:, b, m], full.at[:, b, m], c.at(t=t - 1), down[k])

    def side(b, slot, src=None):
        return c.to(full.at[:, b, m] if src is None else src, full.at[:, b, m], sib, slot)

    def got(b, slot, mm):
        return c.to(full.at[:, b, mm], full.at[:, b, mm], sib, slot)

    pl.when(t < TP - 1)(lambda: up_copy(0).start())
    pl.when(t > 0)(lambda: down_copy(0).start())
    side(t, d2o, own).start()
    c.local(own, full.at[:, t, m], loc).start()
    yield
    for k in range(TP - 1):
        def from_below():
            got(t - 1 - k, up[k], m).wait_recv()
            side(t - 1 - k, d2u[k]).start()
            if k < TP - 2:
                pl.when(t < TP - 1)(lambda: up_copy(k + 1).start())

        def from_above():
            got(t + 1 + k, down[k], m).wait_recv()
            side(t + 1 + k, d2d[k]).start()
            if k < TP - 2:
                pl.when(t > 0)(lambda: down_copy(k + 1).start())

        pl.when(t - 1 - k >= 0)(from_below)
        pl.when(t + 1 + k < TP)(from_above)
        yield
    c.local(own, full.at[:, t, m], loc).wait()
    side(t, d2o, own).wait_send()
    got(t, d2o, 1 - m).wait_recv()
    for k in range(TP - 1):
        pl.when((t < TP - 1) & (t - k >= 0))(lambda: up_copy(k).wait_send())
        pl.when((t > 0) & (t + k < TP))(lambda: down_copy(k).wait_send())

        def below():
            side(t - 1 - k, d2u[k]).wait_send()
            got(t - 1 - k, d2u[k], 1 - m).wait_recv()

        def above():
            side(t + 1 + k, d2d[k]).wait_send()
            got(t + 1 + k, d2d[k], 1 - m).wait_recv()

        pl.when(t - 1 - k >= 0)(below)
        pl.when(t + 1 + k < TP)(above)


def rs_scratch(rows, width):
    return [
        pltpu.VMEM((2, TP, rows, width), BF),
        pltpu.VMEM((2, TP - 1, 2, rows, width), BF),
        pltpu.VMEM((TP - 1, 2, rows, width), BF),
    ]


def rs_flow(c, part, out, sib, inbox, outbox):
    t, m = c.t, c.m
    n = part.shape[3]
    other = c.at(m=1 - m)
    lower = t < TP // 2
    u = jnp.where(lower, t, TP - 1 - t)
    da = jnp.where(lower, 0, 1)
    step = 1 - 2 * da
    near = [c.slot() for _ in range(TP)]
    base = c.n
    for _ in range(2 * (TP - 1)):
        c.slot()

    def real(d):
        return jnp.where(lower, d, TP - 1 - d)

    def cross(d):
        return c.to(part.at[:, real(d), 1 - m], sib.at[:, real(d)], other, near[d])

    def msg(flow, j):
        way = da if flow == 0 else 1 - da
        dev = c.at(t=t + step if flow == 0 else t - step)
        return c.to(outbox.at[j if flow == 0 else 2], inbox.at[way, j], dev, base + way * (TP - 1) + j)

    def add(d, into, terms):
        b = real(d)

        def rows16(i, _):
            sl = pl.ds(pl.multiple_of(i * 16, 16), 16)
            for s in range(2):
                v = part[s, b, m, sl, :].astype(F32) + sib[s, b, sl, :].astype(F32)
                for way, j in terms:
                    v = v + inbox[way, j, s, sl, :].astype(F32)
                into(s, sl, v)
            return 0

        lax.fori_loop(0, n // 16, rows16, 0)

    def put(j):
        def into(s, sl, v):
            outbox[j, s, sl, :] = v.astype(BF)
        return into

    def final(s, sl, v):
        out[s, sl, :] = v

    for d in (3, 2, 0, 1):
        cross(d).start()
    yield
    for d, j in ((3, 0), (2, 1)):
        cross(d).wait_recv()
        for lvl in range(2):
            def go():
                if lvl == 1:
                    msg(0, j).wait_recv()
                add(d, put(j), [(da, j)] if lvl else [])
                msg(0, j).start()
            pl.when(u == lvl)(go)
        yield
    cross(0).wait_recv()
    cross(1).wait_recv()

    def first():
        add(1, put(2), [])
        msg(0, 2).start()

    pl.when(u == 0)(first)

    def back():
        msg(1, 0).wait_recv()
        add(0, put(2), [(1 - da, 0)])
        msg(1, 0).start()

    pl.when(u == 1)(back)
    yield

    def end0():
        msg(1, 0).wait_recv()
        add(0, final, [(1 - da, 0)])

    def end1():
        msg(0, 2).wait_recv()
        msg(1, 1).wait_recv()
        add(1, final, [(da, 2), (1 - da, 1)])

    pl.when(u == 0)(end0)
    pl.when(u == 1)(end1)
    for d in range(TP):
        cross(d).wait_send()
    for j in range(2):
        msg(0, j).wait_send()
    pl.when(u == 0)(lambda: msg(0, 2).wait_send())
    pl.when(u == 1)(lambda: msg(1, 0).wait_send())


def inner(t):
    return (t == 1) | (t == 2)


def outer(t):
    return (t == 0) | (t == TP - 1)


def fifth(t):
    return t == 1


def cut(width, t):
    tiles = width // 128
    big = -(-tiles // TP)
    small = (tiles - 2 * big) // 2
    return pl.multiple_of((small * t + (big - small) * (t > 1) * (t - 1)) * 128, 128), big * 128, small * 128


def spread_z(c, src, dst, kinds=((None, 0),), owner="to"):
    slots = [c.slot() for _ in range(TP)]

    def each_kind(sender, taker, f):
        own = taker if owner == "to" else sender
        for which, k in kinds:
            if which is None:
                f(k)
            else:
                pl.when(which(own))(functools.partial(f, k))

    def copy(o, k):
        to = (c.t + o) % TP
        return c.to(src(to, k), dst(c.t, k), c.at(t=to), slots[o])

    def back(o, k):
        frm = (c.t + TP - o) % TP
        return c.to(dst(frm, k), dst(frm, k), c.at(t=frm), slots[o])

    for o in range(1, TP):
        each_kind(c.t, (c.t + o) % TP, lambda k: copy(o, k).start())
    each_kind(c.t, c.t, lambda k: c.local(src(c.t, k), dst(c.t, k), slots[0]).start())
    yield
    each_kind(c.t, c.t, lambda k: c.local(src(c.t, k), dst(c.t, k), slots[0]).wait())
    for o in range(1, TP):
        each_kind((c.t + TP - o) % TP, c.t, lambda k: back(o, k).wait_recv())
    yield
    for o in range(1, TP):
        each_kind(c.t, (c.t + o) % TP, lambda k: copy(o, k).wait_send())


def plane_gather(c, block, order, own=None):
    have = [0]
    done = []
    held = None
    if own is not None:
        held = c.local(own, block(c.g), c.slot())
        held.start()
    for b in order:
        dev = c.at(g=c.flip(c.g, b))
        sent = []
        for x in have:
            gg = c.g
            for bit in c.bits:
                if x & bit:
                    gg = c.flip(gg, bit)
            src = own if own is not None and x == 0 else block(gg)
            copy = c.to(src, block(gg), dev, c.slot())
            copy.start()
            sent.append(copy)
        yield
        for copy in sent:
            copy.wait_recv()
        done += sent
        have = have + [x ^ b for x in have]
    for copy in done:
        copy.wait_send()
    if held is not None:
        held.wait()


def plane_reduce(c, own, sums, inbox, order):
    def place(x):
        gg = c.g
        for bit in c.bits:
            if x & bit:
                gg = c.flip(gg, bit)
        return gg

    left = list(range(c.ng))
    spot = {}
    done = []
    base = 0
    for k, b in enumerate(order):
        dev = c.at(g=c.flip(c.g, b))
        away = [x for x in left if x & b]
        left = [x for x in left if not x & b]
        sent = []
        for i, x in enumerate(away):
            src = own(place(x)) if k == 0 else sums.at[spot[x]]
            copy = c.to(src, inbox.at[base + i], dev, c.slot())
            copy.start()
            sent.append(copy)
        held = []
        if k == 0:
            spot = {x: i for i, x in enumerate(left)}
            for x in left:
                held.append(c.local(own(place(x)), sums.at[spot[x]], c.slot()))
                held[-1].start()
        yield
        for i, x in enumerate(left):
            sent[i].wait_recv()
            if k == 0:
                held[i].wait()
            add_blocks(sums.at[spot[x]], inbox.at[base + i])
        base += len(away)
        done += sent
    for copy in done:
        copy.wait_send()


def add_blocks(a, b):
    def one(i, _):
        a[i] = (a[i].astype(F32) + b[i].astype(F32)).astype(BF)
        return 0

    lax.fori_loop(0, a.shape[0], one, 0)


def call(kernel, out_shape, in_specs, out_specs, scratch, cid, slots=160):
    return pl.pallas_call(
        kernel,
        out_shape=out_shape,
        in_specs=in_specs,
        out_specs=out_specs,
        scratch_shapes=list(scratch) + [pltpu.SemaphoreType.DMA((slots,)), pltpu.SemaphoreType.DMA((slots,))],
        compiler_params=pltpu.CompilerParams(collective_id=cid, has_side_effects=True, vmem_limit_bytes=VMEM_LIMIT),
    )


HBM = pl.BlockSpec(memory_space=pl.ANY)
VM = pl.BlockSpec(memory_space=pltpu.VMEM)


def heads_to(ref, dst, extra):
    def src(t, k):
        return ref.at[:, pl.ds(1024, 256)] if extra else ref.at[:, pl.ds(pl.multiple_of(t * 256, 256), 256)]

    def into(t, k):
        return dst(t).at[:, pl.ds(256 if extra else 0, 256)]

    return src, into, (((fifth, 0),) if extra else ((None, 0),))


def units_to(ref, dst):
    width = ref.shape[1]
    _, big, small = cut(width, 0)

    def src(t, k):
        return ref.at[:, pl.ds(cut(width, t)[0], k)]

    def into(t, k):
        return dst(t).at[:, pl.ds(0, k)]

    return src, into, ((inner, big), (outer, small))


def units_back(ref, dst):
    width = dst.shape[1]
    _, big, small = cut(width, 0)

    def src(t, k):
        return ref(t).at[:, pl.ds(0, k)]

    def into(t, k):
        return dst.at[:, pl.ds(cut(width, t)[0], k)]

    return src, into, ((inner, big), (outer, small)), "from"


def heads_out(ref, dst, extra):
    def src(t, k):
        return ref(t).at[:, pl.ds(256 if extra else 0, 256)]

    def into(t, k):
        return dst.at[:, pl.ds(1024, 256)] if extra else dst.at[:, pl.ds(pl.multiple_of(t * 256, 256), 256)]

    return src, into, (((fifth, 0),) if extra else ((None, 0),)), "from"


def start_kernel(x, gain, wbr, wot, gates, full_a, wb0, wb1, wop, gb, own, zero, send, recv):
    c = Comm(send, recv)
    c.barrier()
    wb = (wb0, wb1)
    z = []
    for extra in (False, True):
        for k in range(2):
            z.append(spread_z(c, *heads_to(wbr.at[k], lambda t, k=k: wb[k].at[t, c.g], extra)))
    z.append(spread_z(c, lambda t, k: gates.at[:, t], lambda t, k: gb.at[:, 0, t, c.g]))
    z.append(spread_z(c, lambda t, k: gates.at[:, 4], lambda t, k: gb.at[:, 1, t, c.g], ((fifth, 0),)))
    for f in z:
        next(f)
    for s in range(2):
        v = x[s].astype(F32)
        own[s] = (v * lax.rsqrt(jnp.mean(v * v, axis=-1, keepdims=True) + EPS) * gain[...]).astype(BF)
    ag = ag_flow(c, own, full_a)
    next(ag)
    z2 = [spread_z(c, *heads_to(wot, lambda t: wop.at[t], extra)) for extra in (False, True)]
    for f in z2:
        next(f)
    zero[...] = jnp.zeros_like(zero)
    fills = [(zero, wb[k].at[:, c.g, :, pl.ds(256, 256)], c.slot()) for k in range(2)]
    fills.append((zero, wop.at[:, :, pl.ds(256, 256)], c.slot()))
    for k in range(2):
        fills.append((zero.at[:, pl.ds(0, gates.shape[2])], gb.at[k, 1, :, c.g], c.slot()))

    def fill():
        for f in fills:
            c.local(*f).start()
        for f in fills:
            c.local(*f).wait()

    pl.when(c.t != 1)(fill)
    for f in z:
        next(f)
    fwd, rev = c.bits, c.bits[::-1]
    g1 = [plane_gather(c, lambda g: wb0.at[:, g], fwd), plane_gather(c, lambda g: wb1.at[:, g], rev),
          plane_gather(c, lambda g: gb.at[0, :, :, g], fwd), plane_gather(c, lambda g: gb.at[1, :, :, g], rev)]
    for f in g1:
        next(f)
    next(ag)
    run(*g1, ag, *z, *z2)


def start_call(x, gain, wbr, wot, gates):
    ng = lax.axis_size("dp") // TP
    _, n, d = x.shape
    r, gr = wbr.shape[1], gates.shape[2]
    S = jax.ShapeDtypeStruct
    return call(
        start_kernel,
        (S((2, TP, 2, n, d), BF), S((TP, ng, r, 512), BF), S((TP, ng, r, 512), BF), S((TP, r, 512), BF), S((2, 2, TP, ng, gr, 256), BF)),
        [VM, VM, HBM, HBM, HBM],
        (HBM,) * 5,
        [pltpu.VMEM((2, n, d), BF), pltpu.VMEM((TP, r, 256), BF)],
        1,
    )(x, gain[None], wbr, wot, gates)


def mid_kernel(part, x, go, gain, p0, m1, m2, zero, res, full, full_g, w0, w1, w2, tot, own, sib, inbox, outbox, send, recv):
    c = Comm(send, recv)
    c.barrier()
    fwd, rev = c.bits, c.bits[::-1]
    rs = rs_flow(c, part, tot, sib, inbox, outbox)
    next(rs)
    pad = zero.shape[2]
    fills = [(zero, w.at[:, c.g, :, pl.ds(w.shape[3] - pad, pad)], c.slot()) for w in (w1, w2)]

    def fill():
        for f in fills:
            c.local(*f).start()
        for f in fills:
            c.local(*f).wait()

    g0 = plane_gather(c, lambda g: w0.at[:, g], fwd, p0)
    next(g0)
    z1 = spread_z(c, *units_to(m1, lambda t: w1.at[t, c.g]))
    next(z1)
    pl.when(outer(c.t))(fill)
    z2 = spread_z(c, *units_to(m2, lambda t: w2.at[t, c.g]))
    next(rs)
    next(z2)
    next(rs)
    next(z1)
    g1 = plane_gather(c, lambda g: w1.at[:, g], rev)
    next(g1)
    next(rs)
    next(g0)
    next(z2)
    half = [plane_gather(c, lambda g: w2.at[pl.ds(0, 2), g], fwd), plane_gather(c, lambda g: w2.at[pl.ds(2, 2), g], rev)]
    for f in half:
        next(f)
    run(rs)
    for s in range(2):
        v = x[s].astype(F32) + tot[s]
        res[s] = v
        own[s] = (v * lax.rsqrt(jnp.mean(v * v, axis=-1, keepdims=True) + EPS) * gain[...]).astype(BF)
    ag = ag_flow(c, own, full)
    next(ag)
    ag2 = ag_flow(c, go, full_g)
    next(ag2)
    run(g1, ag, *half, ag2, g0, z1, z2)


def mid_call(part, x, go, gain, p0, m1, m2):
    _, n, d = x.shape
    ng = lax.axis_size("dp") // TP
    _, r, fs = p0.shape
    _, big, small = cut(m1.shape[1], 0)
    zero = jnp.zeros((TP, r, big - small), BF)
    S = jax.ShapeDtypeStruct
    w = S((TP, ng, r, fs), BF)
    return call(
        mid_kernel,
        (S((2, n, d), F32), S((2, TP, 2, n, d), BF), S((2, TP, 2, n, d), BF), w, w, w),
        [VM, VM, VM, VM, HBM, HBM, HBM, VM],
        (VM,) + (HBM,) * 5,
        [pltpu.VMEM((2, n, d), F32), pltpu.VMEM((2, n, d), BF)] + rs_scratch(n, d),
        2,
    )(part.reshape(2, TP, 2, n, d), x, go, gain[None], p0, m1, m2, zero)


def back_kernel(part, part2, res, go, gain, h0, h1, h2, gres, gsum, mlp_own, full, o0, r1, r2,
                tot, own, sib, inbox, outbox, sib2, inbox2, outbox2, su, ib, send, recv):
    c = Comm(send, recv)
    c.barrier()
    fwd, rev = c.bits, c.bits[::-1]
    rs = rs_flow(c, part, tot, sib, inbox, outbox)
    next(rs)
    red = [plane_reduce(c, lambda g, h=h: h.at[:, g], su.at[k], ib.at[k], (fwd, rev, fwd)[k]) for k, h in enumerate((h0, h1, h2))]
    for f in red[:2]:
        next(f)
    rs2 = rs_flow(c, part2, mlp_own, sib2, inbox2, outbox2)
    run(rs)
    total = jnp.zeros_like(gsum)
    for s in range(2):
        v = res[s]
        scale = lax.rsqrt(jnp.mean(v * v, axis=-1, keepdims=True) + EPS)
        normal = v * scale
        gn = tot[s]
        total = total + jnp.sum(gn * normal, axis=0, keepdims=True)
        q = gn * gain[...]
        gr = scale * (q - normal * jnp.mean(q * normal, axis=-1, keepdims=True)) + go[s].astype(F32)
        gres[s] = gr
        own[s] = gr.astype(BF)
    gsum[...] = total
    ag = ag_flow(c, own, full)
    next(ag)
    next(rs2)
    next(red[2])
    next(red[0])
    next(rs2)
    next(ag)
    next(red[1])
    next(rs2)
    next(ag)
    for f in red[2:] + red[:1]:
        for _ in range(len(c.bits) - 1 if f is red[2] else len(c.bits) - 2):
            next(f)
    for f in red[1:2]:
        for _ in range(len(c.bits) - 2):
            next(f)
    next(rs2)
    finish(red[0])
    s0 = spread_z(c, *units_back(lambda t: su.at[0, 0, t], o0))
    next(s0)
    finish(ag)
    finish(rs2)
    finish(red[1])
    l1 = c.local(su.at[1, 0], r1, c.slot())
    l1.start()
    finish(red[2])
    l2 = c.local(su.at[2, 0], r2, c.slot())
    l2.start()
    run(s0)
    l1.wait()
    l2.wait()


def finish(f):
    for _ in f:
        pass


def back_call(part, part2, res, go, gain, h0, h1, h2, units):
    _, n, d = go.shape
    _, ng, r, fs = h0.shape
    S = jax.ShapeDtypeStruct
    shape = (2, TP, 2, n, d)
    return call(
        back_kernel,
        (S((2, n, d), F32), S((1, d), F32), S((2, n, d), F32), S(shape, BF), S((r, units), BF), S((TP, r, fs), BF), S((TP, r, fs), BF)),
        [VM] * 5 + [HBM] * 3,
        (VM, VM, VM, HBM, HBM, HBM, HBM),
        [pltpu.VMEM((2, n, d), F32), pltpu.VMEM((2, n, d), BF)] + rs_scratch(n, d) + rs_scratch(n, d)
        + [pltpu.VMEM((3, ng // 2, TP, r, fs), BF), pltpu.VMEM((3, ng - 1, TP, r, fs), BF)],
        3, 256,
    )(part.reshape(shape), part2.reshape(shape), res, go, gain[None], h0, h1, h2)


def small_flow(c, small, inbox, zbox, sbox, gains, table):
    for k, b in enumerate(c.bits):
        copy = c.to(small.at[k], inbox.at[k], c.at(g=c.flip(c.g, b)), c.slot())
        copy.start()
        yield
        copy.wait()
        small[k + 1] = small[k] + inbox[k]
    last = len(c.bits)
    z = spread_z(c, lambda t, k: small.at[last], lambda t, k: zbox.at[t])
    next(z)
    yield
    run(z)
    sbox[0] = zbox[0, 0:8] + zbox[1, 0:8] + zbox[2, 0:8] + zbox[3, 0:8]
    table[...] = zbox[:, 8:16, 0:512]
    copy = c.to(sbox.at[0], sbox.at[1], c.at(m=1 - c.m), c.slot())
    copy.start()
    yield
    copy.wait()
    gains[...] = sbox[0] + sbox[1]


def end_kernel(part, x, gres, gain, gwb0, gwb1, ggb, rwo, r2, gain_b, chan_rows, gin, gains, table, owb, owo, ogb, o2,
               small, small_in, zbox, sbox, tot, sib, inbox, outbox, su_x, in_x, su_g, in_g, send, recv):
    c = Comm(send, recv)
    c.barrier()
    fwd, rev = c.bits, c.bits[::-1]
    red, spread = [], []
    for k, gw in enumerate((gwb0, gwb1)):
        red.append(plane_reduce(c, lambda g, gw=gw: gw.at[:, g], su_x.at[k], in_x.at[k], rev if k else fwd))
        for extra in (False, True):
            spread.append((k, spread_z(c, *heads_out(lambda t, k=k: su_x.at[k, 0, t], owb.at[k], extra))))
    for k in range(2):
        for h in range(2):
            i = 2 * k + h
            red.append(plane_reduce(c, lambda g, k=k, h=h: ggb.at[k, h, :, g], su_g.at[i], in_g.at[i], fwd if k else rev))
            spread.append((2 + i, spread_z(
                c, lambda t, q, i=i: su_g.at[i, 0, t], lambda t, q, k=k, h=h: ogb.at[k, 4 if h else t],
                ((fifth, 0),) if h else ((None, 0),), "from")))
    rs = rs_flow(c, part, tot, sib, inbox, outbox)
    next(rs)
    for f in red:
        next(f)
    z0 = [spread_z(c, *units_back(lambda t: r2.at[t], o2))]
    for extra in (False, True):
        z0.append(spread_z(c, *heads_out(lambda t: rwo.at[t], owo, extra)))
    next(rs)
    for f in z0:
        next(f)
    finish(rs)
    total = jnp.zeros_like(gain)
    for s in range(2):
        v = x[s].astype(F32)
        scale = lax.rsqrt(jnp.mean(v * v, axis=-1, keepdims=True) + EPS)
        normal = v * scale
        gn = tot[s]
        total = total + jnp.sum(gn * normal, axis=0, keepdims=True)
        q = gn * gain[...]
        gin[s] = scale * (q - normal * jnp.mean(q * normal, axis=-1, keepdims=True)) + gres[s]
    small[0] = jnp.zeros_like(small[0])
    small[0, 0:1, :] = total
    small[0, 1:2, :] = gain_b[...]
    small[0, 8:16, 0:512] = chan_rows[...]
    sm = small_flow(c, small, small_in, zbox, sbox, gains, table)
    next(sm)
    for _ in range(len(c.bits) - 1):
        for f in red:
            next(f)
        next(sm)
    for i, f in enumerate(red):
        finish(f)
        for k, z in spread:
            if k == i:
                next(z)
    next(sm)
    run(sm, *z0, *[z for _, z in spread])


def end_call(part, x, gres, gain, gwb0, gwb1, ggb, rwo, r2, gain_b, chan_rows, units):
    _, n, d = x.shape
    ng = lax.axis_size("dp") // TP
    r, gr, steps = gwb0.shape[2], ggb.shape[4], (lax.axis_size("dp") // TP).bit_length()
    S = jax.ShapeDtypeStruct

    def sets(k, rows, width):
        return [pltpu.VMEM((k, ng // 2, TP, rows, width), BF), pltpu.VMEM((k, ng - 1, TP, rows, width), BF)]

    return call(
        end_kernel,
        (S((2, n, d), F32), S((8, d), F32), S((TP, 8, 512), F32), S((2, r, 1280), BF), S((r, 1280), BF), S((2, 5, gr, 256), BF), S((r, units), BF)),
        [VM] * 4 + [HBM] * 5 + [VM] * 2,
        (VM,) * 3 + (HBM,) * 4,
        [pltpu.VMEM((steps, 16, d), F32), pltpu.VMEM((steps - 1, 16, d), F32), pltpu.VMEM((TP, 16, d), F32), pltpu.VMEM((2, 8, d), F32),
         pltpu.VMEM((2, n, d), F32)] + rs_scratch(n, d) + sets(2, r, 512) + sets(4, gr, 256),
        4, 256,
    )(part.reshape(2, TP, 2, n, d), x, gres, gain[None], gwb0, gwb1, ggb, rwo, r2, gain_b, chan_rows)


def heads_of(a, axis):
    _, _, t, _ = plan()
    p = lax.dynamic_slice_in_dim(a, t * 256, 256, axis)
    q = lax.dynamic_slice_in_dim(a, 1024, 256, axis)
    q = jnp.where(t == 1, q, jnp.zeros_like(q))
    return jnp.concatenate([p, q], axis)


def gelu_pair(v):
    k = 0.7978845608028654
    v2 = v * v
    th = jnp.tanh(k * v * (1.0 + 0.044715 * v2))
    half = 0.5 * (1.0 + th)
    return v * half, half + 0.5 * v * (1.0 - th * th) * k * (1.0 + 3.0 * 0.044715 * v2)


def decay_terms(ga, db):
    log_a = -8.0 * ga * db
    y = 2.0 * log_a
    series = 1.0 + y * (1 / 8)
    for k in range(7, 1, -1):
        series = 1.0 + y * (1 / k) * series
    m1 = jnp.where(y > -0.35, y * series, jnp.exp(y) - 1.0)
    return jnp.exp(log_a), jnp.sqrt(-m1)


def lanes_in(ref, rows, v):
    for q in range(ref.shape[0]):
        ref[q, rows, :] = v[:, q * 128:(q + 1) * 128]


def lanes_out(ref, rows):
    return jnp.concatenate([ref[q, rows, :] for q in range(ref.shape[0])], axis=1)


def each(ref, at):
    return [ref[q, at, :] for q in range(ref.shape[0])]


def split(v):
    return [v[:, q * 128:(q + 1) * 128] for q in range(v.shape[1] // 128)]


def plane_partners(c):
    return [c.at(g=(c.g + o) % c.ng) for o in range(1, c.ng)]


def greet(partners):
    sem = pltpu.get_barrier_semaphore()
    for p in partners:
        pl.semaphore_signal(sem, inc=1, device_id=p, device_id_type=MESH)
    pl.semaphore_wait(sem, len(partners))


def line_partners(c):
    return [c.at(t=(c.t + o) % TP) for o in range(1, TP)]


def share(c, table):
    copies = []
    for o in range(1, c.ng):
        slot = c.slot()
        copies.append((o, slot))
        c.to(table.at[c.g], table.at[c.g], c.at(g=(c.g + o) % c.ng), slot).start()
    for o, slot in copies:
        frm = (c.g + c.ng - o) % c.ng
        c.to(table.at[frm], table.at[frm], c.at(g=frm), slot).wait_recv()
    for o, slot in copies:
        c.to(table.at[c.g], table.at[c.g], c.at(g=(c.g + o) % c.ng), slot).wait_send()


def entering(c, prod, last, width, reverse):
    rows = [None] * (2 * TP)
    spots = [(t, g) for t in range(TP) for g in range(c.ng)]
    for s in range(2):
        cur = jnp.zeros((1, width), F32)
        for t, g in (spots[::-1] if reverse else spots):
            b = s * TP + t
            old = rows[b]
            rows[b] = cur if old is None else jnp.where(c.g == g, cur, old)
            cur = last(g)[b:b + 1] + prod(g)[b:b + 1] * cur
    return jnp.concatenate(rows, axis=0)


def mix_fwd_kernel(br0, ci, gb, chan, db, wop, m0, zero, mixed, conv, gates, state, rim, carry, table, wo, p0, a_ref, d_ref, ext, rim_in, send, recv):
    c = Comm(send, recv)
    greet(plane_partners(c) + line_partners(c))
    n, width = ci.shape[1], ci.shape[2]
    rslot = c.slot()
    out = c.to(ci.at[:, pl.ds(n - 16, 16)], rim_in, c.at(g=(c.g + 1) % c.ng), rslot)
    out.start()
    z0 = spread_z(c, *units_to(m0, lambda t: p0.at[t]))
    next(z0)
    fwd, rev = c.bits, c.bits[::-1]
    g0 = [plane_gather(c, lambda g: wo.at[pl.ds(0, 2), g], fwd, wop.at[pl.ds(0, 2)]), plane_gather(c, lambda g: wo.at[pl.ds(2, 2), g], rev, wop.at[pl.ds(2, 2)])]
    for f in g0:
        next(f)
    pad = zero.shape[2]
    fill = c.local(zero, p0.at[:, :, pl.ds(p0.shape[2] - pad, pad)], c.slot())
    pl.when(outer(c.t))(lambda: fill.start())
    out.wait()
    row = lax.broadcasted_iota(jnp.int32, (n, 1), 0)
    for b in range(2 * TP):
        t = b % TP
        same = rim_in[b].astype(F32)[8:]
        prev = jnp.zeros_like(same) if t == 0 else rim_in[b - 1].astype(F32)[8:]
        head = jnp.where(c.g == 0, prev, same)
        rim[b] = head
        ext[b % 2, pl.ds(0, 8), :] = head
        ext[b % 2, pl.ds(8, n), :] = ci[b].astype(F32)
        cv = chan[4:5] + chan[0:1] * ext[b % 2, pl.ds(8, n), :] + chan[1:2] * ext[b % 2, pl.ds(7, n), :]
        cv = cv + chan[2:3] * ext[b % 2, pl.ds(6, n), :] + chan[3:4] * ext[b % 2, pl.ds(5, n), :]
        low = cv.astype(BF)
        rows = pl.ds(b * n, n)
        conv[rows, :] = low
        cv = low.astype(F32)
        gv = []
        for k in range(2):
            pre = jnp.concatenate([jnp.dot(low[:, h * 256:(h + 1) * 256], gb[k, h], preferred_element_type=F32) for h in range(2)], axis=1)
            v = jax.nn.sigmoid(pre + chan[5 + k:6 + k])
            gates[k, rows, :] = v
            gv.append(v)
        decay, mult = decay_terms(gv[1], db[...])
        if t == 0:
            mult = jnp.where((row == 0) & (c.g == 0), 1.0, mult)
        lanes_in(a_ref, rows, decay)
        lanes_in(d_ref, rows, cv * gv[0] * mult)

    def step1(r, ph):
        at = pl.ds(r, 2 * TP, stride=n)
        return [(p * av, h * av + dv) for (p, h), av, dv in zip(ph, each(a_ref, at), each(d_ref, at))]

    one = jnp.ones((2 * TP, 128), F32)
    ph = lax.fori_loop(0, n, step1, [(one, 0.0 * one)] * (width // 128), unroll=8)
    p = jnp.concatenate([v[0] for v in ph], axis=1)
    h = jnp.concatenate([v[1] for v in ph], axis=1)
    table[c.g, 0] = p
    table[c.g, 1] = h
    for f in g0:
        next(f)
    share(c, table)
    cin = entering(c, lambda g: table[g, 0], lambda g: table[g, 1], width, False)
    carry[...] = cin

    def step2(r, hs):
        at = pl.ds(r, 2 * TP, stride=n)
        hs = [h * av + dv for h, av, dv in zip(hs, each(a_ref, at), each(d_ref, at))]
        for q, h in enumerate(hs):
            d_ref[q, at, :] = h
        return hs

    lax.fori_loop(0, n, step2, split(cin), unroll=8)
    for b in range(2 * TP):
        rows = pl.ds(b * n, n)
        v = lanes_out(d_ref, rows)
        state[rows, :] = v
        mixed[rows, :] = (v * gelu_pair(br0[rows, :])[0]).astype(BF)
    run(*g0, z0)
    pl.when(outer(c.t))(lambda: fill.wait())


def mix_fwd_call(br0, ci, gb, chan, db, wop, m0):
    ng = lax.axis_size("dp") // TP
    rows, width = br0.shape
    n = rows // (2 * TP)
    r = m0.shape[0]
    _, big, small = cut(m0.shape[1], 0)
    S = jax.ShapeDtypeStruct
    return call(
        mix_fwd_kernel,
        (S((rows, width), BF), S((rows, width), BF), S((2, rows, width), F32), S((rows, width), F32),
         S((2 * TP, 8, width), F32), S((2 * TP, width), F32), S((ng, 2, 2 * TP, width), F32), S((TP, ng, r, width), BF), S((TP, r, big), BF)),
        [VM] * 5 + [HBM, HBM, VM],
        (VM,) * 7 + (HBM, HBM),
        [pltpu.VMEM((width // 128, rows, 128), F32), pltpu.VMEM((width // 128, rows, 128), F32), pltpu.VMEM((2, n + 8, width), F32), pltpu.VMEM((2 * TP, 16, width), BF)],
        5, 128,
    )(br0, ci.reshape(2 * TP, n, width), gb, chan, db[None], wop, m0, jnp.zeros((TP, r, big - small), BF))


def mix_bwd_kernel(gm, br0, ci, gb, chan, db, conv, gates, state, rim, carry, table, gwo, r1, gbr, ggb, sums, rwo, o1,
                   a_ref, adj, gc, gpl, ext, heads, etab, rim_in, su, ib, send, recv):
    c = Comm(send, recv)
    greet(plane_partners(c) + line_partners(c))
    n, width = ci.shape[1], ci.shape[2]
    z0 = spread_z(c, *units_back(lambda t: r1.at[t], o1))
    next(z0)
    fwd, rev = c.bits, c.bits[::-1]
    red = [plane_reduce(c, lambda g, k=k: gwo.at[pl.ds(2 * k, 2), g], su.at[k], ib.at[k], rev if k else fwd) for k in range(2)]
    for f in red:
        next(f)
    for b in range(2 * TP):
        rows = pl.ds(b * n, n)
        act, slope = gelu_pair(br0[rows, :])
        g = gm[rows, :]
        lanes_in(adj, rows, g * act)
        gbr[0, rows, :] = (g * state[rows, :] * slope).astype(BF)
        lanes_in(a_ref, rows, jnp.exp(-8.0 * gates[1, rows, :] * db[...]))

    def step1(i, es):
        at = pl.ds(n - 1 - i, 2 * TP, stride=n)
        return [(v + e) * av for v, e, av in zip(each(adj, at), es, each(a_ref, at))]

    e = lax.fori_loop(0, n, step1, [jnp.zeros((2 * TP, 128), F32)] * (width // 128), unroll=8)
    e = jnp.concatenate(e, axis=1)
    etab[c.g] = e
    share(c, etab)
    for f in red:
        for _ in range(len(c.bits) - 1):
            next(f)
    ein = entering(c, lambda g: table[g, 0], lambda g: etab[g], width, True)

    def step2(i, es):
        at = pl.ds(n - 1 - i, 2 * TP, stride=n)
        vs = [v + e for v, e in zip(each(adj, at), es)]
        for q, v in enumerate(vs):
            adj[q, at, :] = v
        return [v * av for v, av in zip(vs, each(a_ref, at))]

    lax.fori_loop(0, n, step2, split(ein), unroll=8)
    row = lax.broadcasted_iota(jnp.int32, (n, 1), 0)
    total = [jnp.zeros((1, width), F32) for _ in range(8)]
    for b in range(2 * TP):
        rows = pl.ds(b * n, n)
        first = (row == 0) & (c.g == 0) if b % TP == 0 else None
        ad = lanes_out(adj, rows)
        gx, ga = gates[0, rows, :], gates[1, rows, :]
        decay, root = decay_terms(ga, db[...])
        mult = root if first is None else jnp.where(first, 1.0, root)
        cv = conv[rows, :].astype(F32)
        before = jnp.where(row == 0, carry[b:b + 1, :], pltpu.roll(state[rows, :], 1, 0))
        gmult = -(ad * cv * gx) * (decay * decay) / root
        if first is not None:
            gmult = jnp.where(first, 0.0, gmult)
        glog = ad * before * decay + gmult
        total[7] = total[7] + jnp.sum(glog * (-8.0 * ga), axis=0, keepdims=True)
        pre = [ad * cv * mult * gx * (1.0 - gx), glog * (-8.0 * db[...]) * ga * (1.0 - ga)]
        conved = ad * gx * mult
        for k in range(2):
            total[5 + k] = total[5 + k] + jnp.sum(pre[k], axis=0, keepdims=True)
            low = pre[k].astype(BF)
            gpl[k, rows, :] = low
            conved = conved + jnp.concatenate([
                lax.dot_general(low[:, h * 256:(h + 1) * 256], gb[k, h], (((1,), (1,)), ((), ())), preferred_element_type=F32)
                for h in range(2)], axis=1)
        gc[b, pl.ds(0, n), :] = conved
        heads[b] = conved[:8]
        ext[b % 2, pl.ds(0, 8), :] = rim[b]
        ext[b % 2, pl.ds(8, n), :] = ci[b].astype(F32)
        for k in range(4):
            total[k] = total[k] + jnp.sum(conved * ext[b % 2, pl.ds(8 - k, n), :], axis=0, keepdims=True)
        total[4] = total[4] + jnp.sum(conved, axis=0, keepdims=True)
    rslot = c.slot()
    out = c.to(heads, rim_in, c.at(g=(c.g + c.ng - 1) % c.ng), rslot)
    out.start()
    sums[...] = jnp.concatenate(total, axis=0)
    for k in range(2):
        for h in range(2):
            ggb[k, h] = lax.dot_general(conv[:, h * 256:(h + 1) * 256], gpl[k, :, h * 256:(h + 1) * 256], (((0,), (0,)), ((), ())), preferred_element_type=F32)
    out.wait()
    for b in range(2 * TP):
        rows = pl.ds(b * n, n)
        same = rim_in[b]
        nxt = jnp.zeros_like(same) if b % TP == TP - 1 else rim_in[b + 1]
        gc[b, pl.ds(n, 8), :] = jnp.where(c.g == c.ng - 1, nxt, same)
        v = chan[0:1] * gc[b, pl.ds(0, n), :]
        for k in range(1, 4):
            v = v + chan[k:k + 1] * gc[b, pl.ds(k, n), :]
        gbr[1, rows, :] = v.astype(BF)
    held = []
    for k, f in enumerate(red):
        finish(f)
        held.append(c.local(su.at[k, 0], rwo.at[pl.ds(2 * k, 2)], c.slot()))
        held[-1].start()
    run(z0)
    for h in held:
        h.wait()


def mix_bwd_call(gm, br0, ci, gb, chan, db, saved, gwo, r1, units):
    ng = lax.axis_size("dp") // TP
    rows, width = br0.shape
    n = rows // (2 * TP)
    r = r1.shape[1]
    S = jax.ShapeDtypeStruct
    V = pltpu.VMEM
    return call(
        mix_bwd_kernel,
        (S((2, rows, width), BF), S((2, 2, 256, 256), F32), S((8, width), F32), S((TP, r, width), BF), S((r, units), BF)),
        [VM] * 12 + [HBM] * 2,
        (VM,) * 3 + (HBM,) * 2,
        [V((width // 128, rows, 128), F32), V((width // 128, rows, 128), F32), V((2 * TP, n + 8, width), F32), V((2, rows, width), BF),
         V((2, n + 8, width), F32), V((2 * TP, 8, width), F32), V((ng, 2 * TP, width), F32), V((2 * TP, 8, width), F32),
         V((2, ng // 2, 2, r, width), BF), V((2, ng - 1, 2, r, width), BF)],
        6, 128,
    )(gm, br0, ci.reshape(2 * TP, n, width), gb, chan, db[None], *saved, gwo, r1)


def dot(a, b, ca, cb):
    return lax.dot_general(a, b, (((ca,), (cb,)), ((), ())), preferred_element_type=F32)


def body(block_input, lengths, norm_gains, w_branch, channel_params, gate_blocks, decay_param, w_out, w_mlp, w_down, out_grad):
    ndp, ng, t, g = plan()
    dp, mp = lax.axis_index("dp"), lax.axis_index("mp")
    rows, width = block_input.shape[1:]
    r, gr, units = w_branch.shape[1], gate_blocks.shape[2], w_mlp.shape[2]
    fs = cut(units, 0)[1]
    chan = heads_of(channel_params, 1)
    dpar = heads_of(decay_param[None], 1)[0]
    decay_base = jax.nn.softplus(dpar)
    pos = dp * 2 * rows + mp * rows + jnp.arange(rows, dtype=jnp.int32)
    valid = (pos[None] < lengths[:, None])[..., None]
    x = block_input
    grad_own = jnp.where(valid, out_grad, jnp.zeros_like(out_grad))
    na, wb0, wb1, wop, gb = start_call(x, norm_gains[0], w_branch, w_out.T, gate_blocks)
    na = na.reshape(-1, width)
    wb0, wb1 = wb0.reshape(width, 512), wb1.reshape(width, 512)
    gb = gb.reshape(2, 2, 256, 256)
    branch0 = dot(na, wb0, 1, 0)
    conv_input = dot(na, wb1, 1, 0).astype(BF)
    mixed, *saved, wo, p0 = mix_fwd_call(branch0, conv_input, gb, chan, decay_base, wop, w_mlp[0])
    wo = wo.reshape(width, 512)
    residual, nb, go, w0, w1, wd = mid_call(dot(mixed, wo, 1, 1).astype(BF), x, grad_own, norm_gains[1], p0, w_mlp[1], w_down.T)
    nb, go = nb.reshape(-1, width), go.reshape(-1, width)
    w0, w1, wd = w0.reshape(width, fs), w1.reshape(width, fs), wd.reshape(width, fs)
    first, second = dot(nb, w0, 1, 0), dot(nb, w1, 1, 0)
    act, act_pull = jax.vjp(jax.nn.gelu, first)
    hidden = (act * second).astype(BF)
    mlp_part = dot(hidden, wd, 1, 1).astype(BF)
    gh = dot(go, wd, 1, 0)
    block = (TP, ng, r, fs)
    gwd = dot(go, hidden, 0, 0).astype(BF).reshape(block)
    ggu = [act_pull(gh * second)[0].astype(BF), (gh * act).astype(BF)]
    gw0, gw1 = [dot(nb, v, 0, 0).astype(BF).reshape(block) for v in ggu]
    gnb = (dot(ggu[0], w0, 1, 1) + dot(ggu[1], w1, 1, 1)).astype(BF)
    gres, gain_b, mlp_own, gmo, o0, r1, r2 = back_call(gnb, mlp_part, residual, grad_own, norm_gains[1], gw0, gw1, gwd, units)
    out = jnp.where(valid, residual + mlp_own, 0.0).astype(BF)
    gmo = gmo.reshape(-1, width)
    block = (TP, ng, r, 512)
    gwo = dot(gmo, mixed, 0, 0).astype(BF).reshape(block)
    gbr, ggb, chan_rows, rwo, o1 = mix_bwd_call(dot(gmo, wo, 1, 0), branch0, conv_input, gb, chan, decay_base, saved, gwo, r1, units)
    gwb0, gwb1 = [dot(na, gbr[k], 0, 0).astype(BF).reshape(block) for k in range(2)]
    gna = (dot(gbr[0], wb0, 1, 1) + dot(gbr[1], wb1, 1, 1)).astype(BF)
    gin, gains, table, owb, owo, ogb, o2 = end_call(
        gna, x, gres, norm_gains[0], gwb0, gwb1, ggb.astype(BF).reshape(2, 2, TP, ng, gr, 256), rwo, r2, gain_b, chan_rows, units,
    )
    g_wb, g_wo, g_gb = owb.astype(F32), owo.astype(F32).T, ogb.astype(F32)
    g_wm, g_wd = jnp.stack([o0, o1]).astype(F32), o2.astype(F32).T
    crow = jnp.concatenate([table[i, :, :256] for i in range(TP)] + [table[1, :, 256:]], -1)
    return out, gin, gains[:2], g_wb, crow[:7], g_gb, crow[7] * jax.nn.sigmoid(decay_param), g_wo, g_wm, g_wd


def solution(mesh):
    return jax.shard_map(
        body,
        mesh=mesh,
        in_specs=(P(None, ("dp", "mp"), None), P(), P(), P(None, "dp", "mp"), P(None, "mp"), P(None, "mp", "dp", None), P("mp"), P("mp", "dp"), P(None, "dp", "mp"), P("mp", "dp"), P(None, ("dp", "mp"), None)),
        out_specs=(P(None, ("dp", "mp"), None), P(None, ("dp", "mp"), None), P(), P(None, "dp", "mp"), P(None, "mp"), P(None, "mp", "dp", None), P("mp"), P("mp", "dp"), P(None, "dp", "mp"), P("mp", "dp")),
        check_vma=False,
    )
```

```python
import functools

import jax
import jax.numpy as jnp
from jax import lax
from jax.experimental import pallas as pl
from jax.experimental.pallas import tpu as pltpu
from jax.sharding import PartitionSpec as P

MESH = pl.DeviceIdType.MESH
VMEM_LIMIT = 60 * 1024 * 1024


EPS = 1e-06
TP = 4
BF = jnp.bfloat16
F32 = jnp.float32


def plan():
    ndp = lax.axis_size("dp")
    ng = ndp // TP
    dp = lax.axis_index("dp")
    return ndp, ng, dp // ng, dp % ng


class Comm:
    def __init__(self, send, recv):
        self.send, self.recv, self.n = send, recv, 0
        self.ndp = lax.axis_size("dp")
        self.ng = self.ndp // TP
        dp = lax.axis_index("dp")
        self.t, self.g, self.m = dp // self.ng, dp % self.ng, lax.axis_index("mp")
        self.bits = [1 << k for k in range(self.ng.bit_length() - 1)]

    def at(self, t=None, g=None, m=None):
        t = self.t if t is None else t
        g = self.g if g is None else g
        return (t * self.ng + g, self.m if m is None else m)

    def fifth(self, t=None):
        return (self.t if t is None else t) == 1 + self.m

    def flip(self, g, b):
        return g + b - 2 * b * ((g // b) % 2)

    def barrier(self):
        sem = pltpu.get_barrier_semaphore()
        partners = [self.at(t=(self.t + o) % TP) for o in range(1, TP)]
        partners += [self.at(g=self.flip(self.g, b)) for b in self.bits] + [self.at(m=1 - self.m)]
        for p in partners:
            pl.semaphore_signal(sem, inc=1, device_id=p, device_id_type=MESH)
        pl.semaphore_wait(sem, len(partners))

    def slot(self):
        self.n += 1
        return self.n - 1

    def to(self, src, dst, dev, slot):
        return pltpu.make_async_remote_copy(
            src_ref=src, dst_ref=dst, send_sem=self.send.at[slot], recv_sem=self.recv.at[slot],
            device_id=dev, device_id_type=MESH,
        )

    def local(self, src, dst, slot):
        return pltpu.make_async_copy(src, dst, self.send.at[slot])


def finish(*flows):
    for f in flows:
        for _ in f:
            pass


def step(*flows):
    for f in flows:
        next(f)


def run(*flows):
    flows = list(flows)
    while flows:
        for f in list(flows):
            try:
                next(f)
            except StopIteration:
                flows.remove(f)


def ag_flow(c, own, full, late=False):
    t, m = c.t, c.m
    sib = c.at(m=1 - m)

    def slots():
        return [[c.slot() for _ in range(2)] for _ in range(TP - 1)]

    up, down, d2u, d2d = slots(), slots(), slots(), slots()
    d2o, loc = [c.slot() for _ in range(2)], [c.slot() for _ in range(2)]

    def row(b, s, mm):
        return full.at[s, b, mm]

    def up_copy(k, s):
        b = t - k
        return c.to(own.at[s] if k == 0 else row(b, s, m), row(b, s, m), c.at(t=t + 1), up[k][s])

    def down_copy(k, s):
        b = t + k
        return c.to(own.at[s] if k == 0 else row(b, s, m), row(b, s, m), c.at(t=t - 1), down[k][s])

    def side(b, slot, s, src=None):
        return c.to(row(b, s, m) if src is None else src, row(b, s, m), sib, slot)

    def got(b, slot, s, mm):
        return c.to(row(b, s, mm), row(b, s, mm), sib, slot)

    def both(f):
        return lambda: [f(s) for s in range(2)] and None

    pl.when((t < TP - 1) & (t > 0) if late else t < TP - 1)(both(lambda s: up_copy(0, s).start()))
    pl.when((t > 0) & (t < TP - 1) if late else t > 0)(both(lambda s: down_copy(0, s).start()))
    for s in range(2):
        side(t, d2o[s], s, own.at[s]).start()
        c.local(own.at[s], row(t, s, m), loc[s]).start()
    yield
    if late:
        pl.when(t == 0)(both(lambda s: up_copy(0, s).start()))
        pl.when(t == TP - 1)(both(lambda s: down_copy(0, s).start()))
        yield
    for k in range(TP - 1):
        def from_below(s):
            got(t - 1 - k, up[k][s], s, m).wait_recv()
            if k < TP - 2:
                pl.when(t < TP - 1)(lambda: up_copy(k + 1, s).start())
            side(t - 1 - k, d2u[k][s], s).start()

        def from_above(s):
            got(t + 1 + k, down[k][s], s, m).wait_recv()
            if k < TP - 2:
                pl.when(t > 0)(lambda: down_copy(k + 1, s).start())
            side(t + 1 + k, d2d[k][s], s).start()

        for s in range(2):
            pl.when(t - 1 - k >= 0)(lambda: from_below(s))
            pl.when(t + 1 + k < TP)(lambda: from_above(s))
        yield
    for s in range(2):
        c.local(own.at[s], row(t, s, m), loc[s]).wait()
        side(t, d2o[s], s, own.at[s]).wait_send()
        got(t, d2o[s], s, 1 - m).wait_recv()
    for k in range(TP - 1):
        pl.when((t < TP - 1) & (t - k >= 0))(both(lambda s: up_copy(k, s).wait_send()))
        pl.when((t > 0) & (t + k < TP))(both(lambda s: down_copy(k, s).wait_send()))

        def below(s):
            side(t - 1 - k, d2u[k][s], s).wait_send()
            got(t - 1 - k, d2u[k][s], s, 1 - m).wait_recv()

        def above(s):
            side(t + 1 + k, d2d[k][s], s).wait_send()
            got(t + 1 + k, d2d[k][s], s, 1 - m).wait_recv()

        pl.when(t - 1 - k >= 0)(both(below))
        pl.when(t + 1 + k < TP)(both(above))


def rs_scratch(rows, width):
    return [
        pltpu.VMEM((2, TP, rows, width), BF),
        pltpu.VMEM((2, TP - 1, 2, rows, width), BF),
        pltpu.VMEM((TP - 1, 2, rows, width), BF),
    ]


def rs_flow(c, part, out, sib, inbox, outbox):
    t, m = c.t, c.m
    n = part.shape[3]
    other = c.at(m=1 - m)
    lower = t < TP // 2
    u = jnp.where(lower, t, TP - 1 - t)
    da = jnp.where(lower, 0, 1)
    hop = 1 - 2 * da
    near = [[c.slot() for _ in range(2)] for _ in range(TP)]
    base = c.n
    for _ in range(4 * (TP - 1)):
        c.slot()

    def real(d):
        return jnp.where(lower, d, TP - 1 - d)

    def cross(d, s):
        return c.to(part.at[s, real(d), 1 - m], sib.at[s, real(d)], other, near[d][s])

    def msg(flow, j, s):
        way = da if flow == 0 else 1 - da
        dev = c.at(t=t + hop if flow == 0 else t - hop)
        return c.to(outbox.at[j if flow == 0 else 2, s], inbox.at[way, j, s], dev, base + (way * (TP - 1) + j) * 2 + s)

    def add(d, s, into, terms):
        b = real(d)

        def rows16(i, _):
            sl = pl.ds(pl.multiple_of(i * 16, 16), 16)
            v = part[s, b, m, sl, :].astype(F32) + sib[s, b, sl, :].astype(F32)
            for way, j in terms:
                v = v + inbox[way, j, s, sl, :].astype(F32)
            into(s, sl, v)
            return 0

        lax.fori_loop(0, n // 16, rows16, 0)

    def put(j):
        def into(s, sl, v):
            outbox[j, s, sl, :] = v.astype(BF)
        return into

    def final(s, sl, v):
        out[s, sl, :] = v

    for d in (3, 2, 0, 1):
        for s in range(2):
            cross(d, s).start()
    yield
    for d, j in ((3, 0), (2, 1)):
        for s in range(2):
            cross(d, s).wait_recv()
            for lvl in range(2):
                def go():
                    if lvl == 1:
                        msg(0, j, s).wait_recv()
                    add(d, s, put(j), [(da, j)] if lvl else [])
                    msg(0, j, s).start()
                pl.when(u == lvl)(go)
        yield
    for s in range(2):
        cross(0, s).wait_recv()
        cross(1, s).wait_recv()

        def first():
            add(1, s, put(2), [])
            msg(0, 2, s).start()

        pl.when(u == 0)(first)

        def back():
            msg(1, 0, s).wait_recv()
            add(0, s, put(2), [(1 - da, 0)])
            msg(1, 0, s).start()

        pl.when(u == 1)(back)
    yield
    for s in range(2):
        def end0():
            msg(1, 0, s).wait_recv()
            add(0, s, final, [(1 - da, 0)])

        def end1():
            msg(0, 2, s).wait_recv()
            msg(1, 1, s).wait_recv()
            add(1, s, final, [(da, 2), (1 - da, 1)])

        pl.when(u == 0)(end0)
        pl.when(u == 1)(end1)
    for s in range(2):
        for d in range(TP):
            cross(d, s).wait_send()
        for j in range(2):
            msg(0, j, s).wait_send()
        pl.when(u == 0)(lambda: msg(0, 2, s).wait_send())
        pl.when(u == 1)(lambda: msg(1, 0, s).wait_send())


def inner(t):
    return (t == 1) | (t == 2)


def outer(t):
    return (t == 0) | (t == TP - 1)


def cut(width, t):
    tiles = width // 128
    big = -(-tiles // TP)
    small = (tiles - 2 * big) // 2
    return pl.multiple_of((small * t + (big - small) * (t > 1) * (t - 1)) * 128, 128), big * 128, small * 128


def spread_z(c, src, dst, kinds=((None, 0),), owner="to"):
    slots = [c.slot() for _ in range(TP)]

    def each_kind(sender, taker, f):
        own = taker if owner == "to" else sender
        for which, k in kinds:
            if which is None:
                f(k)
            else:
                pl.when(which(own))(functools.partial(f, k))

    def copy(o, k):
        to = (c.t + o) % TP
        return c.to(src(to, k), dst(c.t, k), c.at(t=to), slots[o])

    def back(o, k):
        frm = (c.t + TP - o) % TP
        return c.to(dst(frm, k), dst(frm, k), c.at(t=frm), slots[o])

    for o in range(1, TP):
        each_kind(c.t, (c.t + o) % TP, lambda k: copy(o, k).start())
    each_kind(c.t, c.t, lambda k: c.local(src(c.t, k), dst(c.t, k), slots[0]).start())
    yield
    each_kind(c.t, c.t, lambda k: c.local(src(c.t, k), dst(c.t, k), slots[0]).wait())
    for o in range(1, TP):
        each_kind((c.t + TP - o) % TP, c.t, lambda k: back(o, k).wait_recv())
    yield
    for o in range(1, TP):
        each_kind(c.t, (c.t + o) % TP, lambda k: copy(o, k).wait_send())


def only(cond, f):
    if cond is None:
        f()
    else:
        pl.when(cond)(f)


def plane_gather(c, block, order, own=None, cond=None):
    have = [0]
    done = []
    held = None
    if own is not None:
        held = c.local(own, block(c.g), c.slot())
        only(cond, lambda: held.start())
    for b in order:
        dev = c.at(g=c.flip(c.g, b))
        sent = []
        for x in have:
            gg = c.g
            for bit in c.bits:
                if x & bit:
                    gg = c.flip(gg, bit)
            src = own if own is not None and x == 0 else block(gg)
            sent.append(c.to(src, block(gg), dev, c.slot()))
        only(cond, lambda: [copy.start() for copy in sent] and None)
        yield
        only(cond, lambda: [copy.wait_recv() for copy in sent] and None)
        done += sent
        have = have + [x ^ b for x in have]
    only(cond, lambda: [copy.wait_send() for copy in done] and None)
    if held is not None:
        only(cond, lambda: held.wait())


def plane_reduce(c, own, sums, inbox, order, cond=None):
    def place(x):
        gg = c.g
        for bit in c.bits:
            if x & bit:
                gg = c.flip(gg, bit)
        return gg

    left = list(range(c.ng))
    spot = {}
    done = []
    base = 0
    for k, b in enumerate(order):
        dev = c.at(g=c.flip(c.g, b))
        away = [x for x in left if x & b]
        left = [x for x in left if not x & b]
        if k == 0:
            spot = {x: i for i, x in enumerate(left)}
        sent = [c.to(own(place(x)) if k == 0 else sums.at[spot[x]], inbox.at[base + i], dev, c.slot()) for i, x in enumerate(away)]
        held = [c.local(own(place(x)), sums.at[spot[x]], c.slot()) for x in left] if k == 0 else []

        def begin():
            for copy in sent + held:
                copy.start()

        only(cond, begin)
        yield

        def take():
            for i, x in enumerate(left):
                sent[i].wait_recv()
                if k == 0:
                    held[i].wait()
                add_blocks(sums.at[spot[x]], inbox.at[base + i])

        only(cond, take)
        base += len(away)
        done += sent
    only(cond, lambda: [copy.wait_send() for copy in done] and None)


def add_blocks(a, b):
    def one(i, _):
        a[i] = a[i] + b[i]
        return 0

    lax.fori_loop(0, a.shape[0], one, 0)


def call(kernel, out_shape, in_specs, out_specs, scratch, cid, slots=160):
    return pl.pallas_call(
        kernel,
        out_shape=out_shape,
        in_specs=in_specs,
        out_specs=out_specs,
        scratch_shapes=list(scratch) + [pltpu.SemaphoreType.DMA((slots,)), pltpu.SemaphoreType.DMA((slots,))],
        compiler_params=pltpu.CompilerParams(collective_id=cid, has_side_effects=True, vmem_limit_bytes=VMEM_LIMIT),
    )


HBM = pl.BlockSpec(memory_space=pl.ANY)
VM = pl.BlockSpec(memory_space=pltpu.VMEM)


def heads_to(c, ref, dst, extra):
    def src(t, k):
        return ref.at[:, pl.ds(1024, 256)] if extra else ref.at[:, pl.ds(pl.multiple_of(t * 256, 256), 256)]

    def into(t, k):
        return dst(t).at[:, pl.ds(256 if extra else 0, 256)]

    return src, into, (((c.fifth, 0),) if extra else ((None, 0),))


def units_to(ref, dst):
    width = ref.shape[1]
    _, big, small = cut(width, 0)

    def src(t, k):
        return ref.at[:, pl.ds(cut(width, t)[0], k)]

    def into(t, k):
        return dst(t).at[:, pl.ds(0, k)]

    return src, into, ((inner, big), (outer, small))


def units_back(ref, dst):
    width = dst.shape[1]
    _, big, small = cut(width, 0)

    def src(t, k):
        return ref(t).at[:, pl.ds(0, k)]

    def into(t, k):
        return dst.at[:, pl.ds(cut(width, t)[0], k)]

    return src, into, ((inner, big), (outer, small)), "from"


def heads_out(c, ref, dst, extra):
    def src(t, k):
        return ref(t).at[:, pl.ds(256 if extra else 0, 256)]

    def into(t, k):
        return dst.at[:, pl.ds(1024, 256)] if extra else dst.at[:, pl.ds(pl.multiple_of(t * 256, 256), 256)]

    return src, into, (((c.fifth, 0),) if extra else ((None, 0),)), "from"


def start_kernel(x, gain, wbr, wot, gates, full_a, wb0, wb1, wop, gb, own, zero, send, recv):
    c = Comm(send, recv)
    c.barrier()
    wb = (wb0, wb1)
    z = []
    for extra in (False, True):
        for k in range(2):
            z.append(spread_z(c, *heads_to(c, wbr.at[k], lambda t, k=k: wb[k].at[t, c.g], extra)))
    z.append(spread_z(c, lambda t, k: gates.at[:, t], lambda t, k: gb.at[:, 0, t, c.g]))
    z.append(spread_z(c, lambda t, k: gates.at[:, 4], lambda t, k: gb.at[:, 1, t, c.g], ((c.fifth, 0),)))
    for f in z:
        next(f)
    for s in range(2):
        v = x[s].astype(F32)
        own[s] = (v * lax.rsqrt(jnp.mean(v * v, axis=-1, keepdims=True) + EPS) * gain[...]).astype(BF)
    zero[...] = jnp.zeros_like(zero)
    fills = [(zero, wb[k].at[:, g, :, pl.ds(256, 256)], c.slot()) for k in range(2) for g in range(c.ng)]
    fills += [(zero.at[:, pl.ds(0, gates.shape[2])], gb.at[k, 1, :, g], c.slot()) for k in range(2) for g in range(c.ng)]
    idle = jnp.logical_not(c.fifth())
    pl.when(idle)(lambda: [c.local(*f).start() for f in fills] and None)
    for f in z:
        next(f)
    fwd, rev = c.bits, c.bits[::-1]
    g1 = []
    for h in range(2):
        for k, order in ((0, fwd), (1, rev)):
            g1.append(plane_gather(c, lambda g, k=k, h=h: wb[k].at[:, g, :, pl.ds(256 * h, 256)], order, None, c.fifth() if h else None))
            g1.append(plane_gather(c, lambda g, k=k, h=h: gb.at[k, h, :, g], order, None, c.fifth() if h else None))
    for f in g1:
        next(f)
    ag = ag_flow(c, own, full_a)
    next(ag)
    z2 = [spread_z(c, *heads_to(c, wot, lambda t: wop.at[t], extra)) for extra in (False, True)]
    for f in g1:
        next(f)
    next(ag)
    for f in z2:
        next(f)
    run(ag, *g1, *z, *z2)
    pl.when(idle)(lambda: [c.local(*f).wait() for f in fills] and None)


def start_call(x, gain, wbr, wot, gates):
    ng = lax.axis_size("dp") // TP
    _, n, d = x.shape
    r, gr = wbr.shape[1], gates.shape[2]
    S = jax.ShapeDtypeStruct
    return call(
        start_kernel,
        (S((2, TP, 2, n, d), BF), S((TP, ng, r, 512), BF), S((TP, ng, r, 512), BF), S((TP, r, 512), BF), S((2, 2, TP, ng, gr, 256), BF)),
        [VM, VM, HBM, HBM, HBM],
        (HBM,) * 5,
        [pltpu.VMEM((2, n, d), BF), pltpu.VMEM((TP, r, 256), BF)],
        1, 256,
    )(x, gain[None], wbr, wot, gates)


MID_LATE = False
MID_ORDER = "r0yar0ay1arNz1aAz2A2"


def mid_kernel(part, x, go, gain, p0, m1, m2, zero, res, full, full_g, w0, w1, w2, tot, own, sib, inbox, outbox, send, recv):
    c = Comm(send, recv)
    c.barrier()
    fwd, rev = c.bits, c.bits[::-1]
    pad = zero.shape[2]
    fills = [(zero, w.at[:, c.g, :, pl.ds(w.shape[3] - pad, pad)], c.slot()) for w in (w1, w2)]

    def gather(w, own=None):
        for k, order in ((0, fwd), (1, rev)):
            at = pl.ds(2 * k, 2)
            yield plane_gather(c, lambda g, at=at: w.at[at, g], order, None if own is None else own.at[at])

    last = len(c.bits) - 1
    rs = rs_flow(c, part, tot, sib, inbox, outbox)
    ag, ag2 = ag_flow(c, own, full), ag_flow(c, go, full_g, MID_LATE)
    z1 = spread_z(c, *units_to(m1, lambda t: w1.at[t, c.g]))
    z2 = spread_z(c, *units_to(m2, lambda t: w2.at[t, c.g]))
    g = [list(gather(w0, p0)), list(gather(w1)), list(gather(w2))]

    def norm():
        finish(rs)
        for s in range(2):
            v = x[s].astype(F32) + tot[s]
            res[s] = v
            own[s] = (v * lax.rsqrt(jnp.mean(v * v, axis=-1, keepdims=True) + EPS) * gain[...]).astype(BF)
        step(ag)

    begun = [0, 0, 0]

    def plane(k):
        if not begun[k]:
            step(*g[k])
        else:
            for _ in range(last):
                step(*g[k])
        begun[k] = 1

    does = {"r": lambda: step(rs), "N": norm, "A": lambda: step(ag), "a": lambda: step(ag2), "y": lambda: step(z1), "z": lambda: step(z2),
            "0": lambda: plane(0), "1": lambda: plane(1), "2": lambda: plane(2)}
    for i, what in enumerate(MID_ORDER):
        does[what]()
        if i == 4:
            pl.when(outer(c.t))(lambda: [c.local(*f).start() for f in fills] and [c.local(*f).wait() for f in fills] and None)
    finish(ag, ag2, *g[0], *g[1], *g[2], z1, z2)


def mid_call(part, x, go, gain, p0, m1, m2):
    _, n, d = x.shape
    ng = lax.axis_size("dp") // TP
    _, r, fs = p0.shape
    _, big, small = cut(m1.shape[1], 0)
    zero = jnp.zeros((TP, r, big - small), BF)
    S = jax.ShapeDtypeStruct
    w = S((TP, ng, r, fs), BF)
    return call(
        mid_kernel,
        (S((2, n, d), F32), S((2, TP, 2, n, d), BF), S((2, TP, 2, n, d), BF), w, w, w),
        [VM, VM, VM, VM, HBM, HBM, HBM, VM],
        (VM,) + (HBM,) * 5,
        [pltpu.VMEM((2, n, d), F32), pltpu.VMEM((2, n, d), BF)] + rs_scratch(n, d),
        2,
    )(part.reshape(2, TP, 2, n, d), x, go, gain[None], p0, m1, m2, zero)


def back_kernel(part, part2, res, go, gain, h0, h1, h2, gres, gsum, mlp_own, full, o0, o1, r2,
                tot, own, sib, inbox, outbox, sib2, inbox2, outbox2, su, ib, send, recv):
    c = Comm(send, recv)
    c.barrier()
    fwd, rev = c.bits, c.bits[::-1]
    rs = rs_flow(c, part, tot, sib, inbox, outbox)
    next(rs)
    red = []
    for k, h in enumerate((h0, h1, h2)):
        red.append([plane_reduce(c, lambda g, h=h, q=q: h.at[pl.ds(2 * q, 2), g], su.at[2 * k + q], ib.at[2 * k + q], (fwd, rev)[q]) for q in range(2)])
    last = len(c.bits) - 1

    def onward(parts):
        for _ in range(last):
            step(*parts)

    step(*red[0])
    step(rs)
    step(*red[1])
    onward(red[0])
    step(rs)
    step(rs)
    rs2 = rs_flow(c, part2, mlp_own, sib2, inbox2, outbox2)
    finish(rs)
    total = jnp.zeros_like(gsum)
    for s in range(2):
        v = res[s]
        scale = lax.rsqrt(jnp.mean(v * v, axis=-1, keepdims=True) + EPS)
        normal = v * scale
        gn = tot[s]
        total = total + jnp.sum(gn * normal, axis=0, keepdims=True)
        q = gn * gain[...]
        gr = scale * (q - normal * jnp.mean(q * normal, axis=-1, keepdims=True)) + go[s].astype(F32)
        gres[s] = gr
        own[s] = gr.astype(BF)
    gsum[...] = total
    ag = ag_flow(c, own, full)
    step(ag, rs2)
    finish(*red[0])
    s0 = spread_z(c, *units_back(lambda t: su.at[t // 2, 0, t % 2], o0))
    step(s0)
    step(*red[2])
    onward(red[1])
    step(ag, rs2)
    held = []

    def keep(k, out):
        finish(*red[k])
        for q in range(2):
            held.append(c.local(su.at[2 * k + q, 0], out.at[pl.ds(2 * q, 2)], c.slot()))
            held[-1].start()

    step(ag, rs2)
    onward(red[2])
    finish(*red[1])
    s1 = spread_z(c, *units_back(lambda t: su.at[2 + t // 2, 0, t % 2], o1))
    step(s1)
    step(rs2)
    finish(ag, rs2)
    keep(2, r2)
    finish(s0, s1)
    for h in held:
        h.wait()


def back_call(part, part2, res, go, gain, h0, h1, h2, units):
    _, n, d = go.shape
    _, ng, r, fs = h0.shape
    S = jax.ShapeDtypeStruct
    shape = (2, TP, 2, n, d)
    return call(
        back_kernel,
        (S((2, n, d), F32), S((1, d), F32), S((2, n, d), F32), S(shape, BF), S((r, units), BF), S((r, units), BF), S((TP, r, fs), BF)),
        [VM] * 5 + [HBM] * 3,
        (VM, VM, VM, HBM, HBM, HBM, HBM),
        [pltpu.VMEM((2, n, d), F32), pltpu.VMEM((2, n, d), BF)] + rs_scratch(n, d) + rs_scratch(n, d)
        + [pltpu.VMEM((6, ng // 2, 2, r, fs), BF), pltpu.VMEM((6, ng - 1, 2, r, fs), BF)],
        3, 256,
    )(part.reshape(shape), part2.reshape(shape), res, go, gain[None], h0, h1, h2)


def small_flow(c, small, inbox, zbox, sbox, gains, table):
    for k, b in enumerate(c.bits):
        copy = c.to(small.at[k], inbox.at[k], c.at(g=c.flip(c.g, b)), c.slot())
        copy.start()
        yield
        copy.wait()
        small[k + 1] = small[k] + inbox[k]
    last = len(c.bits)
    z = spread_z(c, lambda t, k: small.at[last], lambda t, k: zbox.at[t])
    next(z)
    yield
    run(z)
    sbox[0] = zbox[0, 0:8] + zbox[1, 0:8] + zbox[2, 0:8] + zbox[3, 0:8]
    table[...] = zbox[:, 8:16, 0:512]
    copy = c.to(sbox.at[0], sbox.at[1], c.at(m=1 - c.m), c.slot())
    copy.start()
    yield
    copy.wait()
    gains[...] = sbox[0] + sbox[1]


def end_kernel(part, x, gres, gain, gwb0, gwb1, ggb, rwo, gain_b, chan_rows, gin, gains, table, owb, owo, ogb,
               small, small_in, zbox, sbox, tot, sib, inbox, outbox, su_x, in_x, su_g, in_g, send, recv):
    c = Comm(send, recv)
    c.barrier()
    fwd, rev = c.bits, c.bits[::-1]
    red, spread = [], []
    for h in range(2):
        for k, gw in enumerate((gwb0, gwb1)):
            i, order, cond = 2 * h + k, rev if k else fwd, c.fifth() if h else None
            red.append(plane_reduce(c, lambda g, gw=gw, h=h: gw.at[:, g, :, pl.ds(256 * h, 256)], su_x.at[i], in_x.at[i], order, cond))
            lane = (lambda t: pl.ds(1024, 256)) if h else (lambda t: pl.ds(pl.multiple_of(t * 256, 256), 256))
            which = ((c.fifth, 0),) if h else ((None, 0),)
            spread.append((len(red) - 1, spread_z(c, lambda t, q, i=i: su_x.at[i, 0, t], lambda t, q, k=k, lane=lane: owb.at[k, :, lane(t)], which, "from")))
            red.append(plane_reduce(c, lambda g, k=k, h=h: ggb.at[k, h, :, g], su_g.at[i], in_g.at[i], order, cond))
            spread.append((len(red) - 1, spread_z(c, lambda t, q, i=i: su_g.at[i, 0, t], lambda t, q, k=k, h=h: ogb.at[k, 4 if h else t], which, "from")))
    rs = rs_flow(c, part, tot, sib, inbox, outbox)
    next(rs)
    for f in red:
        next(f)
    z0 = []
    for extra in (False, True):
        z0.append(spread_z(c, *heads_out(c, lambda t: rwo.at[t], owo, extra)))
    finish(rs)
    step(*z0)
    total = jnp.zeros_like(gain)
    for s in range(2):
        v = x[s].astype(F32)
        scale = lax.rsqrt(jnp.mean(v * v, axis=-1, keepdims=True) + EPS)
        normal = v * scale
        gn = tot[s]
        total = total + jnp.sum(gn * normal, axis=0, keepdims=True)
        q = gn * gain[...]
        gin[s] = scale * (q - normal * jnp.mean(q * normal, axis=-1, keepdims=True)) + gres[s]
    small[0] = jnp.zeros_like(small[0])
    small[0, 0:1, :] = total
    small[0, 1:2, :] = gain_b[...]
    small[0, 8:16, 0:512] = chan_rows[...]
    sm = small_flow(c, small, small_in, zbox, sbox, gains, table)
    next(sm)
    for _ in range(len(c.bits) - 1):
        for f in red:
            next(f)
        next(sm)
    for i, f in enumerate(red):
        finish(f)
        for k, z in spread:
            if k == i:
                next(z)
    next(sm)
    run(sm, *z0, *[z for _, z in spread])


def end_call(part, x, gres, gain, gwb0, gwb1, ggb, rwo, gain_b, chan_rows):
    _, n, d = x.shape
    ng = lax.axis_size("dp") // TP
    r, gr, steps = gwb0.shape[2], ggb.shape[4], (lax.axis_size("dp") // TP).bit_length()
    S = jax.ShapeDtypeStruct

    def sets(k, rows, width):
        return [pltpu.VMEM((k, ng // 2, TP, rows, width), BF), pltpu.VMEM((k, ng - 1, TP, rows, width), BF)]

    return call(
        end_kernel,
        (S((2, n, d), F32), S((8, d), F32), S((TP, 8, 512), F32), S((2, r, 1280), BF), S((r, 1280), BF), S((2, 5, gr, 256), BF)),
        [VM] * 4 + [HBM] * 4 + [VM] * 2,
        (VM,) * 3 + (HBM,) * 3,
        [pltpu.VMEM((steps, 16, d), F32), pltpu.VMEM((steps - 1, 16, d), F32), pltpu.VMEM((TP, 16, d), F32), pltpu.VMEM((2, 8, d), F32),
         pltpu.VMEM((2, n, d), F32)] + rs_scratch(n, d) + sets(4, r, 256) + sets(4, gr, 256),
        4, 256,
    )(part.reshape(2, TP, 2, n, d), x, gres, gain[None], gwb0, gwb1, ggb, rwo, gain_b, chan_rows)


def heads_of(a, axis):
    _, _, t, _ = plan()
    p = lax.dynamic_slice_in_dim(a, t * 256, 256, axis)
    q = lax.dynamic_slice_in_dim(a, 1024, 256, axis)
    q = jnp.where(t == 1 + lax.axis_index("mp"), q, jnp.zeros_like(q))
    return jnp.concatenate([p, q], axis)


def gelu_pair(v):
    k = 0.7978845608028654
    v2 = v * v
    th = jnp.tanh(k * v * (1.0 + 0.044715 * v2))
    half = 0.5 * (1.0 + th)
    return v * half, half + 0.5 * v * (1.0 - th * th) * k * (1.0 + 3.0 * 0.044715 * v2)


def decay_terms(ga, db):
    log_a = -8.0 * ga * db
    y = 2.0 * log_a
    series = 1.0 + y * (1 / 8)
    for k in range(7, 1, -1):
        series = 1.0 + y * (1 / k) * series
    m1 = jnp.where(y > -0.35, y * series, jnp.exp(y) - 1.0)
    return jnp.exp(log_a), jnp.sqrt(-m1)


def lanes_in(ref, rows, v):
    for q in range(ref.shape[0]):
        ref[q, rows, :] = v[:, q * 128:(q + 1) * 128]


def lanes_out(ref, rows):
    return jnp.concatenate([ref[q, rows, :] for q in range(ref.shape[0])], axis=1)


def each(ref, at):
    return [ref[q, at, :] for q in range(ref.shape[0])]


def split(v):
    return [v[:, q * 128:(q + 1) * 128] for q in range(v.shape[1] // 128)]


def plane_partners(c):
    return [c.at(g=(c.g + o) % c.ng) for o in range(1, c.ng)]


def greet(partners):
    sem = pltpu.get_barrier_semaphore()
    for p in partners:
        pl.semaphore_signal(sem, inc=1, device_id=p, device_id_type=MESH)
    pl.semaphore_wait(sem, len(partners))


def line_partners(c):
    return [c.at(t=(c.t + o) % TP) for o in range(1, TP)]


def share(c, table):
    slots = [c.slot() for _ in range(1, c.ng)]
    for o, slot in enumerate(slots, 1):
        c.to(table.at[c.g], table.at[c.g], c.at(g=(c.g + o) % c.ng), slot).start()
    yield
    for o, slot in enumerate(slots, 1):
        frm = (c.g + c.ng - o) % c.ng
        c.to(table.at[frm], table.at[frm], c.at(g=frm), slot).wait_recv()
    for o, slot in enumerate(slots, 1):
        c.to(table.at[c.g], table.at[c.g], c.at(g=(c.g + o) % c.ng), slot).wait_send()


def entering(c, prod, last, width, reverse):
    rows = [None] * (2 * TP)
    spots = [(t, g) for t in range(TP) for g in range(c.ng)]
    for s in range(2):
        cur = jnp.zeros((1, width), F32)
        for t, g in (spots[::-1] if reverse else spots):
            b = s * TP + t
            old = rows[b]
            rows[b] = cur if old is None else jnp.where(c.g == g, cur, old)
            cur = last(g)[b:b + 1] + prod(g)[b:b + 1] * cur
    return jnp.concatenate(rows, axis=0)


def mix_fwd_kernel(na, wb0, wb1, gb, chan, db, wop, m0, zero, blank, mixed, conv, gates, state, rim, carry, table, br0, ci, wo, p0, a_ref, d_ref, ext, rim_in, send, recv):
    c = Comm(send, recv)
    greet(plane_partners(c) + line_partners(c))
    n, width = ci.shape[1], ci.shape[2]
    z0 = spread_z(c, *units_to(m0, lambda t: p0.at[t]))
    next(z0)
    fwd, rev = c.bits, c.bits[::-1]
    g0 = []
    for h in range(2):
        for q, order in ((0, fwd), (1, rev)):
            at, lane = pl.ds(2 * q, 2), pl.ds(256 * h, 256)
            g0.append(plane_gather(c, lambda g, at=at, lane=lane: wo.at[at, g, :, lane], order, wop.at[at, :, lane], c.fifth() if h else None))
    step(*g0)
    fills = [c.local(blank, wo.at[:, g, :, pl.ds(256, 256)], c.slot()) for g in range(c.ng)]
    idle = jnp.logical_not(c.fifth())
    pl.when(idle)(lambda: [f.start() for f in fills] and None)
    pad = zero.shape[2]
    fill = c.local(zero, p0.at[:, :, pl.ds(p0.shape[2] - pad, pad)], c.slot())
    pl.when(outer(c.t))(lambda: fill.start())

    def branch(i, _):
        rows = pl.ds(pl.multiple_of(i * 2 * n, 2 * n), 2 * n)
        v = jnp.dot(na[rows, :], wb1[...], preferred_element_type=F32).astype(BF)
        ci[2 * i] = v[:n]
        ci[2 * i + 1] = v[n:]
        return 0

    lax.fori_loop(0, TP, branch, 0)
    out = c.to(ci.at[:, pl.ds(n - 16, 16)], rim_in, c.at(g=(c.g + 1) % c.ng), c.slot())
    out.start()

    def gate(i, _):
        rows = pl.ds(pl.multiple_of(i * 2 * n, 2 * n), 2 * n)
        br0[rows, :] = jnp.dot(na[rows, :], wb0[...], preferred_element_type=F32)
        return 0

    lax.fori_loop(0, TP, gate, 0)
    out.wait()
    row = lax.broadcasted_iota(jnp.int32, (n, 1), 0)
    for b in range(2 * TP):
        t = b % TP
        same = rim_in[b].astype(F32)[8:]
        prev = jnp.zeros_like(same) if t == 0 else rim_in[b - 1].astype(F32)[8:]
        head = jnp.where(c.g == 0, prev, same)
        rim[b] = head
        ext[b % 2, pl.ds(0, 8), :] = head
        ext[b % 2, pl.ds(8, n), :] = ci[b].astype(F32)
        cv = chan[4:5] + chan[0:1] * ext[b % 2, pl.ds(8, n), :] + chan[1:2] * ext[b % 2, pl.ds(7, n), :]
        cv = cv + chan[2:3] * ext[b % 2, pl.ds(6, n), :] + chan[3:4] * ext[b % 2, pl.ds(5, n), :]
        low = cv.astype(BF)
        rows = pl.ds(b * n, n)
        conv[rows, :] = low
        cv = low.astype(F32)
        gv = []
        for k in range(2):
            pre = jnp.concatenate([jnp.dot(low[:, h * 256:(h + 1) * 256], gb[k, h], preferred_element_type=F32) for h in range(2)], axis=1)
            v = jax.nn.sigmoid(pre + chan[5 + k:6 + k])
            gates[k, rows, :] = v
            gv.append(v)
        decay, mult = decay_terms(gv[1], db[...])
        if t == 0:
            mult = jnp.where((row == 0) & (c.g == 0), 1.0, mult)
        lanes_in(a_ref, rows, decay)
        lanes_in(d_ref, rows, cv * gv[0] * mult)

    def step1(r, ph):
        at = pl.ds(r, 2 * TP, stride=n)
        return [(p * av, h * av + dv) for (p, h), av, dv in zip(ph, each(a_ref, at), each(d_ref, at))]

    one = jnp.ones((2 * TP, 128), F32)
    ph = lax.fori_loop(0, n, step1, [(one, 0.0 * one)] * (width // 128), unroll=8)
    p = jnp.concatenate([v[0] for v in ph], axis=1)
    h = jnp.concatenate([v[1] for v in ph], axis=1)
    table[c.g, 0] = p
    table[c.g, 1] = h
    sh = share(c, table)
    next(sh)
    for f in g0:
        next(f)
    finish(sh)
    cin = entering(c, lambda g: table[g, 0], lambda g: table[g, 1], width, False)
    carry[...] = cin

    def step2(r, hs):
        at = pl.ds(r, 2 * TP, stride=n)
        hs = [h * av + dv for h, av, dv in zip(hs, each(a_ref, at), each(d_ref, at))]
        for q, h in enumerate(hs):
            d_ref[q, at, :] = h
        return hs

    lax.fori_loop(0, n, step2, split(cin), unroll=8)
    for b in range(2 * TP):
        rows = pl.ds(b * n, n)
        v = lanes_out(d_ref, rows)
        state[rows, :] = v
        mixed[rows, :] = (v * gelu_pair(br0[rows, :])[0]).astype(BF)
    run(*g0, z0)
    pl.when(outer(c.t))(lambda: fill.wait())
    pl.when(idle)(lambda: [f.wait() for f in fills] and None)


def mix_fwd_call(na, wb0, wb1, gb, chan, db, wop, m0):
    ng = lax.axis_size("dp") // TP
    rows, width = na.shape[0], wb0.shape[1]
    n = rows // (2 * TP)
    r = m0.shape[0]
    _, big, small = cut(m0.shape[1], 0)
    S = jax.ShapeDtypeStruct
    return call(
        mix_fwd_kernel,
        (S((rows, width), BF), S((rows, width), BF), S((2, rows, width), F32), S((rows, width), F32),
         S((2 * TP, 8, width), F32), S((2 * TP, width), F32), S((ng, 2, 2 * TP, width), F32), S((rows, width), F32), S((2 * TP, n, width), BF), S((TP, ng, r, width), BF), S((TP, r, big), BF)),
        [VM] * 6 + [HBM, HBM, VM, VM],
        (VM,) * 9 + (HBM, HBM),
        [pltpu.VMEM((width // 128, rows, 128), F32), pltpu.VMEM((width // 128, rows, 128), F32), pltpu.VMEM((2, n + 8, width), F32), pltpu.VMEM((2 * TP, 16, width), BF)],
        5, 128,
    )(na, wb0, wb1, gb, chan, db[None], wop, m0, jnp.zeros((TP, r, big - small), BF), jnp.zeros((TP, r, 256), BF))


def mix_bwd_kernel(gmo, wo, wb0, wb1, br0, ci, gb, chan, db, conv, gates, state, rim, carry, table, gwo, r1, gbr, ggb, sums, gna, rwo, o1,
                   gm, a_ref, adj, gc, gpl, ext, heads, etab, rim_in, su, ib, send, recv):
    c = Comm(send, recv)
    greet(plane_partners(c) + line_partners(c))
    n, width = ci.shape[1], ci.shape[2]
    z0 = spread_z(c, *units_back(lambda t: r1.at[t], o1))
    next(z0)
    fwd, rev = c.bits, c.bits[::-1]
    red = []
    for h in range(2):
        for q, order in ((0, fwd), (1, rev)):
            i = 2 * h + q
            red.append(plane_reduce(c, lambda g, h=h, q=q: gwo.at[pl.ds(2 * q, 2), g, :, pl.ds(256 * h, 256)], su.at[i], ib.at[i], order, c.fifth() if h else None))
    for f in red:
        next(f)

    def product(i, _):
        rows = pl.ds(pl.multiple_of(i * 2 * n, 2 * n), 2 * n)
        gm[rows, :] = jnp.dot(gmo[rows, :], wo[...], preferred_element_type=F32)
        return 0

    lax.fori_loop(0, TP, product, 0)
    for b in range(2 * TP):
        rows = pl.ds(b * n, n)
        act, slope = gelu_pair(br0[rows, :])
        g = gm[rows, :]
        lanes_in(adj, rows, g * act)
        gbr[0, rows, :] = (g * state[rows, :] * slope).astype(BF)
        lanes_in(a_ref, rows, jnp.exp(-8.0 * gates[1, rows, :] * db[...]))

    def step1(i, es):
        at = pl.ds(n - 1 - i, 2 * TP, stride=n)
        return [(v + e) * av for v, e, av in zip(each(adj, at), es, each(a_ref, at))]

    e = lax.fori_loop(0, n, step1, [jnp.zeros((2 * TP, 128), F32)] * (width // 128), unroll=8)
    e = jnp.concatenate(e, axis=1)
    etab[c.g] = e
    sh = share(c, etab)
    next(sh)
    for f in red:
        for _ in range(len(c.bits) - 1):
            next(f)
    finish(sh)
    ein = entering(c, lambda g: table[g, 0], lambda g: etab[g], width, True)

    def step2(i, es):
        at = pl.ds(n - 1 - i, 2 * TP, stride=n)
        vs = [v + e for v, e in zip(each(adj, at), es)]
        for q, v in enumerate(vs):
            adj[q, at, :] = v
        return [v * av for v, av in zip(vs, each(a_ref, at))]

    lax.fori_loop(0, n, step2, split(ein), unroll=8)
    row = lax.broadcasted_iota(jnp.int32, (n, 1), 0)
    total = [jnp.zeros((1, width), F32) for _ in range(8)]
    for b in range(2 * TP):
        rows = pl.ds(b * n, n)
        first = (row == 0) & (c.g == 0) if b % TP == 0 else None
        ad = lanes_out(adj, rows)
        gx, ga = gates[0, rows, :], gates[1, rows, :]
        decay, root = decay_terms(ga, db[...])
        mult = root if first is None else jnp.where(first, 1.0, root)
        cv = conv[rows, :].astype(F32)
        before = jnp.where(row == 0, carry[b:b + 1, :], pltpu.roll(state[rows, :], 1, 0))
        gmult = -(ad * cv * gx) * (decay * decay) / root
        if first is not None:
            gmult = jnp.where(first, 0.0, gmult)
        glog = ad * before * decay + gmult
        total[7] = total[7] + jnp.sum(glog * (-8.0 * ga), axis=0, keepdims=True)
        pre = [ad * cv * mult * gx * (1.0 - gx), glog * (-8.0 * db[...]) * ga * (1.0 - ga)]
        conved = ad * gx * mult
        for k in range(2):
            total[5 + k] = total[5 + k] + jnp.sum(pre[k], axis=0, keepdims=True)
            low = pre[k].astype(BF)
            gpl[k, rows, :] = low
            conved = conved + jnp.concatenate([
                lax.dot_general(low[:, h * 256:(h + 1) * 256], gb[k, h], (((1,), (1,)), ((), ())), preferred_element_type=F32)
                for h in range(2)], axis=1)
        gc[b, pl.ds(0, n), :] = conved
        heads[b] = conved[:8]
        ext[b % 2, pl.ds(0, 8), :] = rim[b]
        ext[b % 2, pl.ds(8, n), :] = ci[b].astype(F32)
        for k in range(4):
            total[k] = total[k] + jnp.sum(conved * ext[b % 2, pl.ds(8 - k, n), :], axis=0, keepdims=True)
        total[4] = total[4] + jnp.sum(conved, axis=0, keepdims=True)
    rslot = c.slot()
    out = c.to(heads, rim_in, c.at(g=(c.g + c.ng - 1) % c.ng), rslot)
    out.start()
    sums[...] = jnp.concatenate(total, axis=0)
    for k in range(2):
        for h in range(2):
            ggb[k, h] = lax.dot_general(conv[:, h * 256:(h + 1) * 256], gpl[k, :, h * 256:(h + 1) * 256], (((0,), (0,)), ((), ())), preferred_element_type=F32)
    out.wait()
    for b in range(2 * TP):
        rows = pl.ds(b * n, n)
        same = rim_in[b]
        nxt = jnp.zeros_like(same) if b % TP == TP - 1 else rim_in[b + 1]
        gc[b, pl.ds(n, 8), :] = jnp.where(c.g == c.ng - 1, nxt, same)
        v = chan[0:1] * gc[b, pl.ds(0, n), :]
        for k in range(1, 4):
            v = v + chan[k:k + 1] * gc[b, pl.ds(k, n), :]
        gbr[1, rows, :] = v.astype(BF)

    def onto(i, _):
        rows = pl.ds(pl.multiple_of(i * 2 * n, 2 * n), 2 * n)
        v = [lax.dot_general(gbr[k, rows, :], w[...], (((1,), (1,)), ((), ())), preferred_element_type=F32) for k, w in enumerate((wb0, wb1))]
        gna[rows, :] = (v[0] + v[1]).astype(BF)
        return 0

    lax.fori_loop(0, TP, onto, 0)
    held = []
    for i, f in enumerate(red):
        finish(f)
        held.append(c.local(su.at[i, 0], rwo.at[pl.ds(2 * (i % 2), 2), :, pl.ds(256 * (i // 2), 256)], c.slot()))
        only(c.fifth() if i >= 2 else None, lambda: held[-1].start())
    run(z0)
    for i, h in enumerate(held):
        only(c.fifth() if i >= 2 else None, lambda: h.wait())


def mix_bwd_call(gmo, wo, wb0, wb1, br0, ci, gb, chan, db, saved, gwo, r1, units):
    ng = lax.axis_size("dp") // TP
    rows, width = br0.shape
    n = rows // (2 * TP)
    r = r1.shape[1]
    S = jax.ShapeDtypeStruct
    V = pltpu.VMEM
    return call(
        mix_bwd_kernel,
        (S((2, rows, width), BF), S((2, 2, 256, 256), F32), S((8, width), F32), S(gmo.shape, BF), S((TP, r, width), BF), S((r, units), BF)),
        [VM] * 15 + [HBM] * 2,
        (VM,) * 4 + (HBM,) * 2,
        [V((rows, width), F32), V((width // 128, rows, 128), F32), V((width // 128, rows, 128), F32), V((2 * TP, n + 8, width), F32), V((2, rows, width), BF),
         V((2, n + 8, width), F32), V((2 * TP, 8, width), F32), V((ng, 2 * TP, width), F32), V((2 * TP, 8, width), F32),
         V((4, ng // 2, 2, r, 256), BF), V((4, ng - 1, 2, r, 256), BF)],
        6, 128,
    )(gmo, wo, wb0, wb1, br0, ci, gb, chan, db[None], *saved, gwo, r1)


def mlp_kernel(nb, go, w0, w1, w2, hidden, gg0, gg1, part, gnb, v0, v1, v2, sems):
    copies = [pltpu.make_async_copy(a, b, sems.at[k]) for k, (a, b) in enumerate(((w0, v0), (w1, v1), (w2, v2)))]
    begin = pl.program_id(0) == 0

    @pl.when(begin)
    def _():
        for copy in copies:
            copy.start()

    def ready(k):
        pl.when(begin)(lambda: copies[k].wait())

    def back(a, w):
        return lax.dot_general(a, w, (((1,), (1,)), ((), ())), preferred_element_type=F32)

    ready(0)
    first = jnp.dot(nb[...], v0[...], preferred_element_type=F32)
    ready(1)
    second = jnp.dot(nb[...], v1[...], preferred_element_type=F32)
    act, slope = gelu_pair(first)
    low = (act * second).astype(BF)
    hidden[...] = low
    ready(2)
    gh = jnp.dot(go[...], v2[...], preferred_element_type=F32)
    a, b = (gh * second * slope).astype(BF), (gh * act).astype(BF)
    gg0[...] = a
    gg1[...] = b
    gnb[...] = (back(a, v0[...]) + back(b, v1[...])).astype(BF)
    part[...] = back(low, v2[...]).astype(BF)


def mlp_call(nb, go, w0, w1, w2):
    rows, d = nb.shape
    fs = w0.shape[1]
    n = 256
    S = jax.ShapeDtypeStruct
    wide = pl.BlockSpec((n, d), lambda i: (i, 0))
    slim = pl.BlockSpec((n, fs), lambda i: (i, 0))
    return pl.pallas_call(
        mlp_kernel,
        grid=(rows // n,),
        out_shape=(S((rows, fs), BF),) * 3 + (S((rows, d), BF),) * 2,
        in_specs=[wide, wide, HBM, HBM, HBM],
        out_specs=(slim,) * 3 + (wide,) * 2,
        scratch_shapes=[pltpu.VMEM((d, fs), BF)] * 3 + [pltpu.SemaphoreType.DMA((3,))],
        compiler_params=pltpu.CompilerParams(vmem_limit_bytes=VMEM_LIMIT),
    )(nb, go, w0, w1, w2)


def dot(a, b, ca, cb):
    return lax.dot_general(a, b, (((ca,), (cb,)), ((), ())), preferred_element_type=F32)


def body(block_input, lengths, norm_gains, w_branch, channel_params, gate_blocks, decay_param, w_out, w_mlp, w_down, out_grad):
    ndp, ng, t, g = plan()
    dp, mp = lax.axis_index("dp"), lax.axis_index("mp")
    rows, width = block_input.shape[1:]
    r, gr, units = w_branch.shape[1], gate_blocks.shape[2], w_mlp.shape[2]
    fs = cut(units, 0)[1]
    chan = heads_of(channel_params, 1)
    dpar = heads_of(decay_param[None], 1)[0]
    decay_base = jax.nn.softplus(dpar)
    pos = dp * 2 * rows + mp * rows + jnp.arange(rows, dtype=jnp.int32)
    valid = (pos[None] < lengths[:, None])[..., None]
    x = block_input
    grad_own = jnp.where(valid, out_grad, jnp.zeros_like(out_grad))
    na, wb0, wb1, wop, gb = start_call(x, norm_gains[0], w_branch, w_out.T, gate_blocks)
    na = na.reshape(-1, width)
    wb0, wb1 = wb0.reshape(width, 512), wb1.reshape(width, 512)
    gb = gb.reshape(2, 2, 256, 256)
    mixed, *saved, branch0, conv_input, wo, p0 = mix_fwd_call(na, wb0, wb1, gb, chan, decay_base, wop, w_mlp[0])
    wo = wo.reshape(width, 512)
    residual, nb, go, w0, w1, wd = mid_call(dot(mixed, wo, 1, 1).astype(BF), x, grad_own, norm_gains[1], p0, w_mlp[1], w_down.T)
    nb, go = nb.reshape(-1, width), go.reshape(-1, width)
    w0, w1, wd = w0.reshape(width, fs), w1.reshape(width, fs), wd.reshape(width, fs)
    hidden, gg0, gg1, mlp_part, gnb = mlp_call(nb, go, w0, w1, wd)
    block = (TP, ng, r, fs)
    gwd, gw0, gw1 = [dot(p, q, 0, 0).astype(BF).reshape(block) for p, q in ((go, hidden), (nb, gg0), (nb, gg1))]
    gres, gain_b, mlp_own, gmo, o0, o1, r2 = back_call(gnb, mlp_part, residual, grad_own, norm_gains[1], gw0, gw1, gwd, units)
    out = jnp.where(valid, residual + mlp_own, 0.0).astype(BF)
    gmo = gmo.reshape(-1, width)
    block = (TP, ng, r, 512)
    gwo = dot(gmo, mixed, 0, 0).astype(BF).reshape(block)
    gbr, ggb, chan_rows, gna, rwo, o2 = mix_bwd_call(gmo, wo, wb0, wb1, branch0, conv_input, gb, chan, decay_base, saved, gwo, r2, units)
    gwb0, gwb1 = [dot(na, gbr[k], 0, 0).astype(BF).reshape(block) for k in range(2)]
    gin, gains, table, owb, owo, ogb = end_call(
        gna, x, gres, norm_gains[0], gwb0, gwb1, ggb.astype(BF).reshape(2, 2, TP, ng, gr, 256), rwo, gain_b, chan_rows,
    )
    g_wb, g_wo, g_gb = owb.astype(F32), owo.astype(F32).T, ogb.astype(F32)
    g_wm, g_wd = jnp.stack([o0, o1]).astype(F32), o2.astype(F32).T
    crow = jnp.concatenate([table[i, :, :256] for i in range(TP)] + [jnp.where(mp == 0, table[1, :, 256:], table[2, :, 256:])], -1)
    return out, gin, gains[:2], g_wb, crow[:7], g_gb, crow[7] * jax.nn.sigmoid(decay_param), g_wo, g_wm, g_wd


def solution(mesh):
    return jax.shard_map(
        body,
        mesh=mesh,
        in_specs=(P(None, ("dp", "mp"), None), P(), P(), P(None, "dp", "mp"), P(None, "mp"), P(None, "mp", "dp", None), P("mp"), P("mp", "dp"), P(None, "dp", "mp"), P("mp", "dp"), P(None, ("dp", "mp"), None)),
        out_specs=(P(None, ("dp", "mp"), None), P(None, ("dp", "mp"), None), P(), P(None, "dp", "mp"), P(None, "mp"), P(None, "mp", "dp", None), P("mp"), P("mp", "dp"), P(None, "dp", "mp"), P("mp", "dp")),
        check_vma=False,
    )
```

```python
import functools

import jax
import jax.numpy as jnp
from jax import lax
from jax.experimental import pallas as pl
from jax.experimental.pallas import tpu as pltpu
from jax.sharding import PartitionSpec as P

MESH = pl.DeviceIdType.MESH
VMEM_LIMIT = 60 * 1024 * 1024


EPS = 1e-06
TP = 4
BF = jnp.bfloat16
F32 = jnp.float32


def plan():
    ndp = lax.axis_size("dp")
    ng = ndp // TP
    dp = lax.axis_index("dp")
    return ndp, ng, dp // ng, dp % ng


class Comm:
    def __init__(self, send, recv):
        self.send, self.recv, self.n = send, recv, 0
        self.ndp = lax.axis_size("dp")
        self.ng = self.ndp // TP
        dp = lax.axis_index("dp")
        self.t, self.g, self.m = dp // self.ng, dp % self.ng, lax.axis_index("mp")
        self.bits = [1 << k for k in range(self.ng.bit_length() - 1)]

    def at(self, t=None, g=None, m=None):
        t = self.t if t is None else t
        g = self.g if g is None else g
        return (t * self.ng + g, self.m if m is None else m)

    def fifth(self, t=None):
        return (self.t if t is None else t) == 1 + self.m

    def flip(self, g, b):
        return g + b - 2 * b * ((g // b) % 2)

    def barrier(self):
        sem = pltpu.get_barrier_semaphore()
        partners = [self.at(t=(self.t + o) % TP) for o in range(1, TP)]
        partners += [self.at(g=self.flip(self.g, b)) for b in self.bits] + [self.at(m=1 - self.m)]
        for p in partners:
            pl.semaphore_signal(sem, inc=1, device_id=p, device_id_type=MESH)
        pl.semaphore_wait(sem, len(partners))

    def slot(self):
        self.n += 1
        return self.n - 1

    def to(self, src, dst, dev, slot):
        return pltpu.make_async_remote_copy(
            src_ref=src, dst_ref=dst, send_sem=self.send.at[slot], recv_sem=self.recv.at[slot],
            device_id=dev, device_id_type=MESH,
        )

    def local(self, src, dst, slot):
        return pltpu.make_async_copy(src, dst, self.send.at[slot])


def finish(*flows):
    for f in flows:
        for _ in f:
            pass


def step(*flows):
    for f in flows:
        next(f)


def run(*flows):
    flows = list(flows)
    while flows:
        for f in list(flows):
            try:
                next(f)
            except StopIteration:
                flows.remove(f)


def ag_flow(c, own, full, late=False):
    t, m = c.t, c.m
    sib = c.at(m=1 - m)

    def slots():
        return [[c.slot() for _ in range(2)] for _ in range(TP - 1)]

    up, down, d2u, d2d = slots(), slots(), slots(), slots()
    d2o, loc = [c.slot() for _ in range(2)], [c.slot() for _ in range(2)]

    def row(b, s, mm):
        return full.at[s, b, mm]

    def up_copy(k, s):
        b = t - k
        return c.to(own.at[s] if k == 0 else row(b, s, m), row(b, s, m), c.at(t=t + 1), up[k][s])

    def down_copy(k, s):
        b = t + k
        return c.to(own.at[s] if k == 0 else row(b, s, m), row(b, s, m), c.at(t=t - 1), down[k][s])

    def side(b, slot, s, src=None):
        return c.to(row(b, s, m) if src is None else src, row(b, s, m), sib, slot)

    def got(b, slot, s, mm):
        return c.to(row(b, s, mm), row(b, s, mm), sib, slot)

    def both(f):
        return lambda: [f(s) for s in range(2)] and None

    pl.when((t < TP - 1) & (t > 0) if late else t < TP - 1)(both(lambda s: up_copy(0, s).start()))
    pl.when((t > 0) & (t < TP - 1) if late else t > 0)(both(lambda s: down_copy(0, s).start()))
    for s in range(2):
        side(t, d2o[s], s, own.at[s]).start()
        c.local(own.at[s], row(t, s, m), loc[s]).start()
    yield
    if late:
        pl.when(t == 0)(both(lambda s: up_copy(0, s).start()))
        pl.when(t == TP - 1)(both(lambda s: down_copy(0, s).start()))
        yield
    for k in range(TP - 1):
        def from_below(s):
            got(t - 1 - k, up[k][s], s, m).wait_recv()
            if k < TP - 2:
                pl.when(t < TP - 1)(lambda: up_copy(k + 1, s).start())
            side(t - 1 - k, d2u[k][s], s).start()

        def from_above(s):
            got(t + 1 + k, down[k][s], s, m).wait_recv()
            if k < TP - 2:
                pl.when(t > 0)(lambda: down_copy(k + 1, s).start())
            side(t + 1 + k, d2d[k][s], s).start()

        for s in range(2):
            pl.when(t - 1 - k >= 0)(lambda: from_below(s))
            pl.when(t + 1 + k < TP)(lambda: from_above(s))
        yield
    for s in range(2):
        c.local(own.at[s], row(t, s, m), loc[s]).wait()
        side(t, d2o[s], s, own.at[s]).wait_send()
        got(t, d2o[s], s, 1 - m).wait_recv()
    for k in range(TP - 1):
        pl.when((t < TP - 1) & (t - k >= 0))(both(lambda s: up_copy(k, s).wait_send()))
        pl.when((t > 0) & (t + k < TP))(both(lambda s: down_copy(k, s).wait_send()))

        def below(s):
            side(t - 1 - k, d2u[k][s], s).wait_send()
            got(t - 1 - k, d2u[k][s], s, 1 - m).wait_recv()

        def above(s):
            side(t + 1 + k, d2d[k][s], s).wait_send()
            got(t + 1 + k, d2d[k][s], s, 1 - m).wait_recv()

        pl.when(t - 1 - k >= 0)(both(below))
        pl.when(t + 1 + k < TP)(both(above))


def rs_scratch(rows, width, made=False):
    return [
        pltpu.VMEM((1 if made else 2, 2, TP, rows, width), BF),
        pltpu.VMEM((2, TP - 1, 2, rows, width), BF),
        pltpu.VMEM((TP - 1, 2, rows, width), BF),
    ]


def rs_flow(c, part, out, pair, inbox, outbox, make=None):
    t, m = c.t, c.m
    n = part.shape[3]
    other = c.at(m=1 - m)
    lower = t < TP // 2
    u = jnp.where(lower, t, TP - 1 - t)
    da = jnp.where(lower, 0, 1)
    hop = 1 - 2 * da
    near = [[c.slot() for _ in range(2)] for _ in range(TP)]
    here = [[c.slot() for _ in range(2)] for _ in range(TP)]
    sib = pair.at[pair.shape[0] - 1]
    own = (lambda s, b: part.at[s, b, m]) if make else (lambda s, b: pair.at[0, s, b])
    base = c.n
    for _ in range(4 * (TP - 1)):
        c.slot()

    def real(d):
        return jnp.where(lower, d, TP - 1 - d)

    def cross(d, s):
        return c.to(part.at[s, real(d), 1 - m], sib.at[s, real(d)], other, near[d][s])

    def load(d, s):
        return c.local(part.at[s, real(d), m], own(s, real(d)), here[d][s])

    def near_in(d, s):
        cross(d, s).wait_recv()
        if make is None:
            load(d, s).wait()

    def msg(flow, j, s):
        way = da if flow == 0 else 1 - da
        dev = c.at(t=t + hop if flow == 0 else t - hop)
        return c.to(outbox.at[j if flow == 0 else 2, s], inbox.at[way, j, s], dev, base + (way * (TP - 1) + j) * 2 + s)

    def add(d, s, into, terms):
        b = real(d)

        def rows16(i, _):
            sl = pl.ds(pl.multiple_of(i * 16, 16), 16)
            v = own(s, b)[sl, :].astype(F32) + sib[s, b, sl, :].astype(F32)
            for way, j in terms:
                v = v + inbox[way, j, s, sl, :].astype(F32)
            into(s, sl, v)
            return 0

        lax.fori_loop(0, n // 16, rows16, 0)

    def put(j):
        def into(s, sl, v):
            outbox[j, s, sl, :] = v.astype(BF)
        return into

    def final(s, sl, v):
        out[s, sl, :] = v

    def issue(d):
        if make is not None:
            b = real(d)
            rows = [pl.ds(pl.multiple_of((s * TP + b) * 2 * n, 2 * n), 2 * n) for s in range(2)]
            v = make(rows).astype(BF).reshape(2, 2, n, part.shape[4])
            for s in range(2):
                part[s, b] = v[s]
        for s in range(2):
            if make is None:
                load(d, s).start()
            cross(d, s).start()

    def send_out(d, j):
        for s in range(2):
            near_in(d, s)
            add(d, s, put(j), [])
            msg(0, j, s).start()

    issue(3)
    issue(2)
    yield
    pl.when(u == 0)(lambda: send_out(3, 0))
    issue(1)
    pl.when(u == 0)(lambda: send_out(2, 1))
    issue(0)
    pl.when(u == 0)(lambda: send_out(1, 2))
    yield
    for d, j in ((3, 0), (2, 1)):
        def pass_on():
            for s in range(2):
                near_in(d, s)
                msg(0, j, s).wait_recv()
                add(d, s, put(j), [(da, j)])
                msg(0, j, s).start()

        pl.when(u == 1)(pass_on)
        yield

    def back():
        for s in range(2):
            near_in(0, s)
            msg(1, 0, s).wait_recv()
            add(0, s, put(2), [(1 - da, 0)])
            msg(1, 0, s).start()

    pl.when(u == 1)(back)
    yield
    for s in range(2):
        def end0():
            near_in(0, s)
            msg(1, 0, s).wait_recv()
            add(0, s, final, [(1 - da, 0)])

        def end1():
            near_in(1, s)
            msg(0, 2, s).wait_recv()
            msg(1, 1, s).wait_recv()
            add(1, s, final, [(da, 2), (1 - da, 1)])

        pl.when(u == 0)(end0)
        pl.when(u == 1)(end1)
    for s in range(2):
        for d in range(TP):
            cross(d, s).wait_send()
        for j in range(2):
            msg(0, j, s).wait_send()
        pl.when(u == 0)(lambda: msg(0, 2, s).wait_send())
        pl.when(u == 1)(lambda: msg(1, 0, s).wait_send())


def inner(t):
    return (t == 1) | (t == 2)


def outer(t):
    return (t == 0) | (t == TP - 1)


def cut(width, t):
    tiles = width // 128
    big = -(-tiles // TP)
    small = (tiles - 2 * big) // 2
    return pl.multiple_of((small * t + (big - small) * (t > 1) * (t - 1)) * 128, 128), big * 128, small * 128


def spread_z(c, src, dst, kinds=((None, 0),), owner="to"):
    slots = [c.slot() for _ in range(TP)]

    def each_kind(sender, taker, f):
        own = taker if owner == "to" else sender
        for which, k in kinds:
            if which is None:
                f(k)
            else:
                pl.when(which(own))(functools.partial(f, k))

    def copy(o, k):
        to = (c.t + o) % TP
        return c.to(src(to, k), dst(c.t, k), c.at(t=to), slots[o])

    def back(o, k):
        frm = (c.t + TP - o) % TP
        return c.to(dst(frm, k), dst(frm, k), c.at(t=frm), slots[o])

    for o in range(1, TP):
        each_kind(c.t, (c.t + o) % TP, lambda k: copy(o, k).start())
    each_kind(c.t, c.t, lambda k: c.local(src(c.t, k), dst(c.t, k), slots[0]).start())
    yield
    each_kind(c.t, c.t, lambda k: c.local(src(c.t, k), dst(c.t, k), slots[0]).wait())
    for o in range(1, TP):
        each_kind((c.t + TP - o) % TP, c.t, lambda k: back(o, k).wait_recv())
    yield
    for o in range(1, TP):
        each_kind(c.t, (c.t + o) % TP, lambda k: copy(o, k).wait_send())


def only(cond, f):
    if cond is None:
        f()
    else:
        pl.when(cond)(f)


def plane_gather(c, block, order, own=None, cond=None):
    have = [0]
    done = []
    held = None
    if own is not None:
        held = c.local(own, block(c.g), c.slot())
        only(cond, lambda: held.start())
    for b in order:
        dev = c.at(g=c.flip(c.g, b))
        sent = []
        for x in have:
            gg = c.g
            for bit in c.bits:
                if x & bit:
                    gg = c.flip(gg, bit)
            src = own if own is not None and x == 0 else block(gg)
            sent.append(c.to(src, block(gg), dev, c.slot()))
        only(cond, lambda: [copy.start() for copy in sent] and None)
        yield
        only(cond, lambda: [copy.wait_recv() for copy in sent] and None)
        done += sent
        have = have + [x ^ b for x in have]
    only(cond, lambda: [copy.wait_send() for copy in done] and None)
    if held is not None:
        only(cond, lambda: held.wait())


def plane_reduce(c, own, sums, inbox, order, cond=None):
    def place(x):
        gg = c.g
        for bit in c.bits:
            if x & bit:
                gg = c.flip(gg, bit)
        return gg

    left = list(range(c.ng))
    spot = {}
    done = []
    base = 0
    for k, b in enumerate(order):
        dev = c.at(g=c.flip(c.g, b))
        away = [x for x in left if x & b]
        left = [x for x in left if not x & b]
        if k == 0:
            spot = {x: i for i, x in enumerate(left)}
        sent = [c.to(own(place(x)) if k == 0 else sums.at[spot[x]], inbox.at[base + i], dev, c.slot()) for i, x in enumerate(away)]
        held = [c.local(own(place(x)), sums.at[spot[x]], c.slot()) for x in left] if k == 0 else []

        def begin():
            for copy in sent + held:
                copy.start()

        only(cond, begin)
        yield

        def take():
            for i, x in enumerate(left):
                sent[i].wait_recv()
                if k == 0:
                    held[i].wait()
                add_blocks(sums.at[spot[x]], inbox.at[base + i])

        only(cond, take)
        base += len(away)
        done += sent
    only(cond, lambda: [copy.wait_send() for copy in done] and None)


def add_blocks(a, b):
    def one(i, _):
        a[i] = a[i] + b[i]
        return 0

    lax.fori_loop(0, a.shape[0], one, 0)


def grad_flow(c, lhs, rhs, out, rbuf, lbuf, stage, halves):
    wide = lbuf.shape[2]
    _, ng, r, cols = stage.shape
    load = c.local(rhs, rbuf, c.slot())
    load.start()
    pieces = [c.local(lhs.at[:, pl.ds(k * wide, wide)], lbuf.at[k % 2], c.slot()) for k in range(TP)]
    puts = [c.local(stage.at[k % 2], out.at[k], c.slot()) for k in range(TP)]
    pieces[0].start()
    pieces[1].start()
    load.wait()
    for k in range(TP):
        pieces[k].wait()
        v = lax.dot_general(lbuf[k % 2], rbuf[...], (((0,), (0,)), ((), ())), preferred_element_type=F32)
        if k + 2 < TP:
            pieces[k + 2].start()
        stage[k % 2] = v.astype(BF).reshape(ng, r, cols)
        puts[k].start()
        if k % 2:
            puts[k - 1].wait()
            puts[k].wait()
            step(*halves[k // 2])
            yield


def call(kernel, out_shape, in_specs, out_specs, scratch, cid, slots=160):
    return pl.pallas_call(
        kernel,
        out_shape=out_shape,
        in_specs=in_specs,
        out_specs=out_specs,
        scratch_shapes=list(scratch) + [pltpu.SemaphoreType.DMA((slots,)), pltpu.SemaphoreType.DMA((slots,))],
        compiler_params=pltpu.CompilerParams(collective_id=cid, has_side_effects=True, vmem_limit_bytes=VMEM_LIMIT),
    )


HBM = pl.BlockSpec(memory_space=pl.ANY)
VM = pl.BlockSpec(memory_space=pltpu.VMEM)


def heads_to(c, ref, dst, extra):
    def src(t, k):
        return ref.at[:, pl.ds(1024, 256)] if extra else ref.at[:, pl.ds(pl.multiple_of(t * 256, 256), 256)]

    def into(t, k):
        return dst(t).at[:, pl.ds(256 if extra else 0, 256)]

    return src, into, (((c.fifth, 0),) if extra else ((None, 0),))


def units_to(ref, dst):
    width = ref.shape[1]
    _, big, small = cut(width, 0)

    def src(t, k):
        return ref.at[:, pl.ds(cut(width, t)[0], k)]

    def into(t, k):
        return dst(t).at[:, pl.ds(0, k)]

    return src, into, ((inner, big), (outer, small))


def units_back(ref, dst):
    width = dst.shape[1]
    _, big, small = cut(width, 0)

    def src(t, k):
        return ref(t).at[:, pl.ds(0, k)]

    def into(t, k):
        return dst.at[:, pl.ds(cut(width, t)[0], k)]

    return src, into, ((inner, big), (outer, small)), "from"


def heads_out(c, ref, dst, extra):
    def src(t, k):
        return ref(t).at[:, pl.ds(256 if extra else 0, 256)]

    def into(t, k):
        return dst.at[:, pl.ds(1024, 256)] if extra else dst.at[:, pl.ds(pl.multiple_of(t * 256, 256), 256)]

    return src, into, (((c.fifth, 0),) if extra else ((None, 0),)), "from"


def start_kernel(x, gain, wbr, wot, gates, full_a, wb0, wb1, wop, gb, own, zero, send, recv):
    c = Comm(send, recv)
    c.barrier()
    wb = (wb0, wb1)
    z = []
    for extra in (False, True):
        for k in range(2):
            z.append(spread_z(c, *heads_to(c, wbr.at[k], lambda t, k=k: wb[k].at[t, c.g], extra)))
    z.append(spread_z(c, lambda t, k: gates.at[:, t], lambda t, k: gb.at[:, 0, t, c.g]))
    z.append(spread_z(c, lambda t, k: gates.at[:, 4], lambda t, k: gb.at[:, 1, t, c.g], ((c.fifth, 0),)))
    for f in z:
        next(f)
    for s in range(2):
        v = x[s].astype(F32)
        own[s] = (v * lax.rsqrt(jnp.mean(v * v, axis=-1, keepdims=True) + EPS) * gain[...]).astype(BF)
    zero[...] = jnp.zeros_like(zero)
    fills = [(zero, wb[k].at[:, g, :, pl.ds(256, 256)], c.slot()) for k in range(2) for g in range(c.ng)]
    fills += [(zero.at[:, pl.ds(0, gates.shape[2])], gb.at[k, 1, :, g], c.slot()) for k in range(2) for g in range(c.ng)]
    idle = jnp.logical_not(c.fifth())
    pl.when(idle)(lambda: [c.local(*f).start() for f in fills] and None)
    for f in z:
        next(f)
    fwd, rev = c.bits, c.bits[::-1]
    g1 = []
    for h in range(2):
        for k, order in ((0, fwd), (1, rev)):
            g1.append(plane_gather(c, lambda g, k=k, h=h: wb[k].at[:, g, :, pl.ds(256 * h, 256)], order, None, c.fifth() if h else None))
            g1.append(plane_gather(c, lambda g, k=k, h=h: gb.at[k, h, :, g], order, None, c.fifth() if h else None))
    for f in g1:
        next(f)
    ag = ag_flow(c, own, full_a)
    next(ag)
    z2 = [spread_z(c, *heads_to(c, wot, lambda t: wop.at[t], extra)) for extra in (False, True)]
    for f in g1:
        next(f)
    next(ag)
    for f in z2:
        next(f)
    run(ag, *g1, *z, *z2)
    pl.when(idle)(lambda: [c.local(*f).wait() for f in fills] and None)


def start_call(x, gain, wbr, wot, gates):
    ng = lax.axis_size("dp") // TP
    _, n, d = x.shape
    r, gr = wbr.shape[1], gates.shape[2]
    S = jax.ShapeDtypeStruct
    return call(
        start_kernel,
        (S((2, TP, 2, n, d), BF), S((TP, ng, r, 512), BF), S((TP, ng, r, 512), BF), S((TP, r, 512), BF), S((2, 2, TP, ng, gr, 256), BF)),
        [VM, VM, HBM, HBM, HBM],
        (HBM,) * 5,
        [pltpu.VMEM((2, n, d), BF), pltpu.VMEM((TP, r, 256), BF)],
        1, 256,
    )(x, gain[None], wbr, wot, gates)


MID_LATE = False
MID_ORDER = "r0yarr0ary1arNz1aAz2A2"


def mid_kernel(mixed, wo, x, go, gain, p0, m1, m2, zero, res, full, full_g, w0, w1, w2, tot, own, part, pair, inbox, outbox, send, recv):
    c = Comm(send, recv)
    c.barrier()
    fwd, rev = c.bits, c.bits[::-1]
    pad = zero.shape[2]
    fills = [(zero, w.at[:, c.g, :, pl.ds(w.shape[3] - pad, pad)], c.slot()) for w in (w1, w2)]

    def gather(w, own=None):
        for k, order in ((0, fwd), (1, rev)):
            at = pl.ds(2 * k, 2)
            yield plane_gather(c, lambda g, at=at: w.at[at, g], order, None if own is None else own.at[at])

    last = len(c.bits) - 1

    def make(rows):
        v = jnp.concatenate([mixed[at, :] for at in rows], axis=0)
        return lax.dot_general(v, wo[...], (((1,), (1,)), ((), ())), preferred_element_type=F32)

    rs = rs_flow(c, part, tot, pair, inbox, outbox, make)
    ag, ag2 = ag_flow(c, own, full), ag_flow(c, go, full_g, MID_LATE)
    z1 = spread_z(c, *units_to(m1, lambda t: w1.at[t, c.g]))
    z2 = spread_z(c, *units_to(m2, lambda t: w2.at[t, c.g]))
    g = [list(gather(w0, p0)), list(gather(w1)), list(gather(w2))]

    def norm():
        finish(rs)
        for s in range(2):
            v = x[s].astype(F32) + tot[s]
            res[s] = v
            own[s] = (v * lax.rsqrt(jnp.mean(v * v, axis=-1, keepdims=True) + EPS) * gain[...]).astype(BF)
        step(ag)

    begun = [0, 0, 0]

    def plane(k):
        if not begun[k]:
            step(*g[k])
        else:
            for _ in range(last):
                step(*g[k])
        begun[k] = 1

    does = {"r": lambda: step(rs), "N": norm, "A": lambda: step(ag), "a": lambda: step(ag2), "y": lambda: step(z1), "z": lambda: step(z2),
            "0": lambda: plane(0), "1": lambda: plane(1), "2": lambda: plane(2)}
    for i, what in enumerate(MID_ORDER):
        does[what]()
        if i == 4:
            pl.when(outer(c.t))(lambda: [c.local(*f).start() for f in fills] and [c.local(*f).wait() for f in fills] and None)
    finish(ag, ag2, *g[0], *g[1], *g[2], z1, z2)


def mid_call(mixed, wo, x, go, gain, p0, m1, m2):
    _, n, d = x.shape
    ng = lax.axis_size("dp") // TP
    _, r, fs = p0.shape
    _, big, small = cut(m1.shape[1], 0)
    zero = jnp.zeros((TP, r, big - small), BF)
    S = jax.ShapeDtypeStruct
    w = S((TP, ng, r, fs), BF)
    return call(
        mid_kernel,
        (S((2, n, d), F32), S((2, TP, 2, n, d), BF), S((2, TP, 2, n, d), BF), w, w, w),
        [VM, VM, VM, VM, VM, HBM, HBM, HBM, VM],
        (VM,) + (HBM,) * 5,
        [pltpu.VMEM((2, n, d), F32), pltpu.VMEM((2, n, d), BF), pltpu.VMEM((2, TP, 2, n, d), BF)] + rs_scratch(n, d, True),
        2,
    )(mixed, wo, x, go, gain[None], p0, m1, m2, zero)


def back_kernel(part, part2, res, go, gain, nb, gall, gg0, gg1, hidden, gres, gsum, mlp_own, full, o0, r1, r2, h0, h1, h2,
                tot, own, pair, inbox, outbox, pair2, inbox2, outbox2, su, ib, rbuf, lbuf, stage, send, recv):
    c = Comm(send, recv)
    c.barrier()
    fwd, rev = c.bits, c.bits[::-1]
    rs = rs_flow(c, part, tot, pair, inbox, outbox)
    next(rs)
    red, grad = [], []
    for k, h in enumerate((h0, h1, h2)):
        red.append([plane_reduce(c, lambda g, h=h, q=q: h.at[pl.ds(2 * q, 2), g], su.at[2 * k + q], ib.at[2 * k + q], (fwd, rev)[q]) for q in range(2)])
        grad.append(grad_flow(c, gall if k == 2 else nb, (gg0, gg1, hidden)[k], h, rbuf, lbuf, stage, [[f] for f in red[k]]))
    last = len(c.bits) - 1

    def onward(parts):
        for _ in range(last):
            step(*parts)

    step(rs)
    step(grad[0])
    step(grad[0])
    step(rs)
    step(grad[1])
    step(rs)
    step(grad[1])
    onward(red[0])
    step(rs)
    rs2 = rs_flow(c, part2, mlp_own, pair2, inbox2, outbox2)
    finish(rs)
    total = jnp.zeros_like(gsum)
    for s in range(2):
        v = res[s]
        scale = lax.rsqrt(jnp.mean(v * v, axis=-1, keepdims=True) + EPS)
        normal = v * scale
        gn = tot[s]
        total = total + jnp.sum(gn * normal, axis=0, keepdims=True)
        q = gn * gain[...]
        gr = scale * (q - normal * jnp.mean(q * normal, axis=-1, keepdims=True)) + go[s].astype(F32)
        gres[s] = gr
        own[s] = gr.astype(BF)
    gsum[...] = total
    ag = ag_flow(c, own, full)
    step(ag, rs2)
    step(rs2)
    finish(*red[0])
    s0 = spread_z(c, *units_back(lambda t: su.at[t // 2, 0, t % 2], o0))
    step(s0)
    step(grad[2])
    step(grad[2])
    onward(red[1])
    step(ag, rs2)
    held = []

    def keep(k, out):
        finish(*red[k])
        for q in range(2):
            held.append(c.local(su.at[2 * k + q, 0], out.at[pl.ds(2 * q, 2)], c.slot()))
            held[-1].start()

    step(ag, rs2)
    onward(red[2])
    keep(1, r1)
    step(rs2)
    finish(ag, rs2)
    keep(2, r2)
    finish(s0, *grad)
    for h in held:
        h.wait()


def back_call(part, part2, res, go, gain, nb, gall, gg0, gg1, hidden, ng, r, units):
    _, n, d = go.shape
    rows, fs = hidden.shape
    S = jax.ShapeDtypeStruct
    shape = (2, TP, 2, n, d)
    h = S((TP, ng, r, fs), BF)
    *outs, _, _, _ = call(
        back_kernel,
        (S((2, n, d), F32), S((1, d), F32), S((2, n, d), F32), S(shape, BF), S((r, units), BF), S((TP, r, fs), BF), S((TP, r, fs), BF), h, h, h),
        [HBM] * 2 + [VM] * 3 + [HBM] * 5,
        (VM, VM, VM) + (HBM,) * 7,
        [pltpu.VMEM((2, n, d), F32), pltpu.VMEM((2, n, d), BF)] + rs_scratch(n, d) + rs_scratch(n, d)
        + [pltpu.VMEM((6, ng // 2, 2, r, fs), BF), pltpu.VMEM((6, ng - 1, 2, r, fs), BF)]
        + [pltpu.VMEM((rows, fs), BF), pltpu.VMEM((2, rows, ng * r), BF), pltpu.VMEM((2, ng, r, fs), BF)],
        3, 256,
    )(part.reshape(shape), part2.reshape(shape), res, go, gain[None], nb, gall, gg0, gg1, hidden)
    return outs


def small_flow(c, small, inbox, zbox):
    for k, b in enumerate(c.bits):
        copy = c.to(small.at[k], inbox.at[k], c.at(g=c.flip(c.g, b)), c.slot())
        copy.start()
        yield
        copy.wait()
        small[k + 1] = small[k] + inbox[k]
    last = len(c.bits)
    z = spread_z(c, lambda t, k: small.at[last], lambda t, k: zbox.at[t])
    next(z)
    yield
    run(z)


def end_kernel(wb0, wb1, gbr, x, gres, gain, na, gsrc, ggb, rwo, gain_b, chan_rows, gin, gains, table, owb, owo, ogb, gwb0, gwb1,
               sm_a, in_a, z_a, sm_b, in_b, sbox, z_b, tot, part, pair, inbox, outbox, su_x, in_x, su_g, in_g, rbuf, lbuf, stage, send, recv):
    c = Comm(send, recv)
    c.barrier()
    fwd, rev = c.bits, c.bits[::-1]
    red, spread = [], []
    for h in range(2):
        for k, gw in enumerate((gwb0, gwb1)):
            i, order, cond = 2 * h + k, rev if k else fwd, c.fifth() if h else None
            red.append(plane_reduce(c, lambda g, gw=gw, h=h: gw.at[:, g, :, pl.ds(256 * h, 256)], su_x.at[i], in_x.at[i], order, cond))
            lane = (lambda t: pl.ds(1024, 256)) if h else (lambda t: pl.ds(pl.multiple_of(t * 256, 256), 256))
            which = ((c.fifth, 0),) if h else ((None, 0),)
            spread.append((len(red) - 1, spread_z(c, lambda t, q, i=i: su_x.at[i, 0, t], lambda t, q, k=k, lane=lane: owb.at[k, :, lane(t)], which, "from")))
            red.append(plane_reduce(c, lambda g, k=k, h=h: ggb.at[k, h, :, g], su_g.at[i], in_g.at[i], order, cond))
            spread.append((len(red) - 1, spread_z(c, lambda t, q, i=i: su_g.at[i, 0, t], lambda t, q, k=k, h=h: ogb.at[k, 4 if h else t], which, "from")))

    def make(rows):
        v = [jnp.concatenate([gbr[k, at, :] for at in rows], axis=0) for k in range(2)]
        v = [lax.dot_general(v[k], w[...], (((1,), (1,)), ((), ())), preferred_element_type=F32) for k, w in enumerate((wb0, wb1))]
        return v[0] + v[1]

    rs = rs_flow(c, part, tot, pair, inbox, outbox, make)
    next(rs)
    grad = [grad_flow(c, na, gsrc.at[k], gw, rbuf, lbuf, stage, ([], [red[2 * k], red[4 + 2 * k]])) for k, gw in enumerate((gwb0, gwb1))]
    for k in range(4):
        step(red[2 * k + 1])
    sm_a[0] = chan_rows[...]
    chan = small_flow(c, sm_a, in_a, z_a)
    step(chan)
    z0 = [spread_z(c, *heads_out(c, lambda t: rwo.at[t], owo, extra)) for extra in (False, True)]
    step(rs)
    step(grad[0])
    step(grad[0])
    step(rs)
    step(grad[1])
    step(grad[1])
    for _ in c.bits:
        step(chan)
    step(*z0)
    step(rs)
    for _ in range(len(c.bits) - 1):
        step(*red)
    step(rs)
    for i, f in enumerate(red):
        finish(f)
        for k, z in spread:
            if k == i:
                next(z)
    finish(rs)
    total = jnp.zeros_like(gain)
    for s in range(2):
        v = x[s].astype(F32)
        scale = lax.rsqrt(jnp.mean(v * v, axis=-1, keepdims=True) + EPS)
        normal = v * scale
        gn = tot[s]
        total = total + jnp.sum(gn * normal, axis=0, keepdims=True)
        q = gn * gain[...]
        gin[s] = scale * (q - normal * jnp.mean(q * normal, axis=-1, keepdims=True)) + gres[s]
    quarter = sm_b.shape[2]
    for k in range(4):
        sm_b[0, k:k + 1, :] = total[:, k * quarter:(k + 1) * quarter]
        sm_b[0, 4 + k:5 + k, :] = gain_b[:, k * quarter:(k + 1) * quarter]
    finish(small_flow(c, sm_b, in_b, z_b))
    sbox[0] = z_b[0] + z_b[1] + z_b[2] + z_b[3]
    copy = c.to(sbox.at[0], sbox.at[1], c.at(m=1 - c.m), c.slot())
    copy.start()
    finish(chan)
    table[...] = z_a[...]
    copy.wait()
    gains[...] = sbox[0] + sbox[1]
    run(*grad, *z0, *[z for _, z in spread])


def end_call(wb0, wb1, x, gres, gain, na, gsrc, ggb, rwo, gain_b, chan_rows, r):
    _, n, d = x.shape
    ng = lax.axis_size("dp") // TP
    gr, steps = ggb.shape[4], (lax.axis_size("dp") // TP).bit_length()
    V = pltpu.VMEM
    S = jax.ShapeDtypeStruct

    def sets(k, rows, width):
        return [pltpu.VMEM((k, ng // 2, TP, rows, width), BF), pltpu.VMEM((k, ng - 1, TP, rows, width), BF)]

    *outs, _, _ = call(
        end_kernel,
        (S((2, n, d), F32), S((8, d // 4), F32), S((TP, 8, 512), F32), S((2, r, 1280), BF), S((r, 1280), BF), S((2, 5, gr, 256), BF))
        + (S((TP, ng, r, 512), BF),) * 2,
        [VM] * 6 + [HBM] * 4 + [VM] * 2,
        (VM,) * 3 + (HBM,) * 5,
        [V((steps, 8, 512), F32), V((steps - 1, 8, 512), F32), V((TP, 8, 512), F32),
         V((steps, 8, d // 4), F32), V((steps - 1, 8, d // 4), F32), V((2, 8, d // 4), F32), V((TP, 8, d // 4), F32),
         pltpu.VMEM((2, n, d), F32), pltpu.VMEM((2, TP, 2, n, d), BF)] + rs_scratch(n, d, True) + sets(4, r, 256) + sets(4, gr, 256)
        + [pltpu.VMEM((na.shape[0], 512), BF), pltpu.VMEM((2, na.shape[0], ng * r), BF), pltpu.VMEM((2, ng, r, 512), BF)],
        4, 256,
    )(wb0, wb1, gsrc, x, gres, gain[None], na, gsrc, ggb, rwo, gain_b, chan_rows)
    return outs


def heads_of(a, axis):
    _, _, t, _ = plan()
    p = lax.dynamic_slice_in_dim(a, t * 256, 256, axis)
    q = lax.dynamic_slice_in_dim(a, 1024, 256, axis)
    q = jnp.where(t == 1 + lax.axis_index("mp"), q, jnp.zeros_like(q))
    return jnp.concatenate([p, q], axis)


def gelu_pair(v):
    k = 0.7978845608028654
    v2 = v * v
    th = jnp.tanh(k * v * (1.0 + 0.044715 * v2))
    half = 0.5 * (1.0 + th)
    return v * half, half + 0.5 * v * (1.0 - th * th) * k * (1.0 + 3.0 * 0.044715 * v2)


def decay_terms(ga, db):
    log_a = -8.0 * ga * db
    y = 2.0 * log_a
    series = 1.0 + y * (1 / 8)
    for k in range(7, 1, -1):
        series = 1.0 + y * (1 / k) * series
    m1 = jnp.where(y > -0.35, y * series, jnp.exp(y) - 1.0)
    return jnp.exp(log_a), jnp.sqrt(-m1)


def lanes_in(ref, rows, v):
    for q in range(ref.shape[0]):
        ref[q, rows, :] = v[:, q * 128:(q + 1) * 128]


def lanes_out(ref, rows):
    return jnp.concatenate([ref[q, rows, :] for q in range(ref.shape[0])], axis=1)


def each(ref, at):
    return [ref[q, at, :] for q in range(ref.shape[0])]


def split(v):
    return [v[:, q * 128:(q + 1) * 128] for q in range(v.shape[1] // 128)]


def plane_partners(c):
    return [c.at(g=(c.g + o) % c.ng) for o in range(1, c.ng)]


def greet(partners):
    sem = pltpu.get_barrier_semaphore()
    for p in partners:
        pl.semaphore_signal(sem, inc=1, device_id=p, device_id_type=MESH)
    pl.semaphore_wait(sem, len(partners))


def line_partners(c):
    return [c.at(t=(c.t + o) % TP) for o in range(1, TP)]


def share(c, table):
    slots = [c.slot() for _ in range(1, c.ng)]
    for o, slot in enumerate(slots, 1):
        c.to(table.at[c.g], table.at[c.g], c.at(g=(c.g + o) % c.ng), slot).start()
    yield
    for o, slot in enumerate(slots, 1):
        frm = (c.g + c.ng - o) % c.ng
        c.to(table.at[frm], table.at[frm], c.at(g=frm), slot).wait_recv()
    for o, slot in enumerate(slots, 1):
        c.to(table.at[c.g], table.at[c.g], c.at(g=(c.g + o) % c.ng), slot).wait_send()


def entering(c, prod, last, width, reverse):
    rows = [None] * (2 * TP)
    spots = [(t, g) for t in range(TP) for g in range(c.ng)]
    for s in range(2):
        cur = jnp.zeros((1, width), F32)
        for t, g in (spots[::-1] if reverse else spots):
            b = s * TP + t
            old = rows[b]
            rows[b] = cur if old is None else jnp.where(c.g == g, cur, old)
            cur = last(g)[b:b + 1] + prod(g)[b:b + 1] * cur
    return jnp.concatenate(rows, axis=0)


def mix_fwd_kernel(na, wb0, wb1, gb, chan, db, wop, m0, zero, blank, mixed, conv, gates, state, rim, carry, table, br0, ci, wo, p0, a_ref, d_ref, ext, rim_in, send, recv):
    c = Comm(send, recv)
    greet(plane_partners(c) + line_partners(c))
    n, width = ci.shape[1], ci.shape[2]
    z0 = spread_z(c, *units_to(m0, lambda t: p0.at[t]))
    next(z0)
    fwd, rev = c.bits, c.bits[::-1]
    g0 = []
    for h in range(2):
        for q, order in ((0, fwd), (1, rev)):
            at, lane = pl.ds(2 * q, 2), pl.ds(256 * h, 256)
            g0.append(plane_gather(c, lambda g, at=at, lane=lane: wo.at[at, g, :, lane], order, wop.at[at, :, lane], c.fifth() if h else None))
    step(*g0)
    fills = [c.local(blank, wo.at[:, g, :, pl.ds(256, 256)], c.slot()) for g in range(c.ng)]
    idle = jnp.logical_not(c.fifth())
    pl.when(idle)(lambda: [f.start() for f in fills] and None)
    pad = zero.shape[2]
    fill = c.local(zero, p0.at[:, :, pl.ds(p0.shape[2] - pad, pad)], c.slot())
    pl.when(outer(c.t))(lambda: fill.start())

    def branch(i, _):
        rows = pl.ds(pl.multiple_of(i * 2 * n, 2 * n), 2 * n)
        v = jnp.dot(na[rows, :], wb1[...], preferred_element_type=F32).astype(BF)
        ci[2 * i] = v[:n]
        ci[2 * i + 1] = v[n:]
        return 0

    lax.fori_loop(0, TP, branch, 0)
    out = c.to(ci.at[:, pl.ds(n - 16, 16)], rim_in, c.at(g=(c.g + 1) % c.ng), c.slot())
    out.start()

    def gate(i, _):
        rows = pl.ds(pl.multiple_of(i * 2 * n, 2 * n), 2 * n)
        br0[rows, :] = jnp.dot(na[rows, :], wb0[...], preferred_element_type=F32)
        return 0

    lax.fori_loop(0, TP, gate, 0)
    out.wait()
    row = lax.broadcasted_iota(jnp.int32, (n, 1), 0)
    for b in range(2 * TP):
        t = b % TP
        same = rim_in[b].astype(F32)[8:]
        prev = jnp.zeros_like(same) if t == 0 else rim_in[b - 1].astype(F32)[8:]
        head = jnp.where(c.g == 0, prev, same)
        rim[b] = head
        ext[b % 2, pl.ds(0, 8), :] = head
        ext[b % 2, pl.ds(8, n), :] = ci[b].astype(F32)
        cv = chan[4:5] + chan[0:1] * ext[b % 2, pl.ds(8, n), :] + chan[1:2] * ext[b % 2, pl.ds(7, n), :]
        cv = cv + chan[2:3] * ext[b % 2, pl.ds(6, n), :] + chan[3:4] * ext[b % 2, pl.ds(5, n), :]
        low = cv.astype(BF)
        rows = pl.ds(b * n, n)
        conv[rows, :] = low
        cv = low.astype(F32)
        gv = []
        for k in range(2):
            pre = jnp.concatenate([jnp.dot(low[:, h * 256:(h + 1) * 256], gb[k, h], preferred_element_type=F32) for h in range(2)], axis=1)
            v = jax.nn.sigmoid(pre + chan[5 + k:6 + k])
            gates[k, rows, :] = v
            gv.append(v)
        decay, mult = decay_terms(gv[1], db[...])
        if t == 0:
            mult = jnp.where((row == 0) & (c.g == 0), 1.0, mult)
        lanes_in(a_ref, rows, decay)
        lanes_in(d_ref, rows, cv * gv[0] * mult)

    def step1(r, ph):
        at = pl.ds(r, 2 * TP, stride=n)
        return [(p * av, h * av + dv) for (p, h), av, dv in zip(ph, each(a_ref, at), each(d_ref, at))]

    one = jnp.ones((2 * TP, 128), F32)
    ph = lax.fori_loop(0, n, step1, [(one, 0.0 * one)] * (width // 128), unroll=8)
    p = jnp.concatenate([v[0] for v in ph], axis=1)
    h = jnp.concatenate([v[1] for v in ph], axis=1)
    table[c.g, 0] = p
    table[c.g, 1] = h
    sh = share(c, table)
    next(sh)
    for f in g0:
        next(f)
    finish(sh)
    cin = entering(c, lambda g: table[g, 0], lambda g: table[g, 1], width, False)
    carry[...] = cin

    def step2(r, hs):
        at = pl.ds(r, 2 * TP, stride=n)
        hs = [h * av + dv for h, av, dv in zip(hs, each(a_ref, at), each(d_ref, at))]
        for q, h in enumerate(hs):
            d_ref[q, at, :] = h
        return hs

    lax.fori_loop(0, n, step2, split(cin), unroll=8)
    for b in range(2 * TP):
        rows = pl.ds(b * n, n)
        v = lanes_out(d_ref, rows)
        state[rows, :] = v
        mixed[rows, :] = (v * gelu_pair(br0[rows, :])[0]).astype(BF)
    run(*g0, z0)
    pl.when(outer(c.t))(lambda: fill.wait())
    pl.when(idle)(lambda: [f.wait() for f in fills] and None)


def mix_fwd_call(na, wb0, wb1, gb, chan, db, wop, m0):
    ng = lax.axis_size("dp") // TP
    rows, width = na.shape[0], wb0.shape[1]
    n = rows // (2 * TP)
    r = m0.shape[0]
    _, big, small = cut(m0.shape[1], 0)
    S = jax.ShapeDtypeStruct
    return call(
        mix_fwd_kernel,
        (S((rows, width), BF), S((rows, width), BF), S((2, rows, width), F32), S((rows, width), F32),
         S((2 * TP, 8, width), F32), S((2 * TP, width), F32), S((ng, 2, 2 * TP, width), F32), S((rows, width), F32), S((2 * TP, n, width), BF), S((TP, ng, r, width), BF), S((TP, r, big), BF)),
        [VM] * 6 + [HBM, HBM, VM, VM],
        (VM,) * 9 + (HBM, HBM),
        [pltpu.VMEM((width // 128, rows, 128), F32), pltpu.VMEM((width // 128, rows, 128), F32), pltpu.VMEM((2, n + 8, width), F32), pltpu.VMEM((2 * TP, 16, width), BF)],
        5, 128,
    )(na, wb0, wb1, gb, chan, db[None], wop, m0, jnp.zeros((TP, r, big - small), BF), jnp.zeros((TP, r, 256), BF))


def mix_bwd_kernel(gmo, wo, br0, ci, gb, chan, db, conv, gates, state, rim, carry, table, gwo, r1, r2, gbr, ggb, sums, rwo, o1, o2,
                   gm, a_ref, adj, gc, gpl, ext, heads, etab, rim_in, su, ib, send, recv):
    c = Comm(send, recv)
    greet(plane_partners(c) + line_partners(c))
    n, width = ci.shape[1], ci.shape[2]
    zs = [spread_z(c, *units_back(lambda t, rr=rr: rr.at[t], oo)) for rr, oo in ((r1, o1), (r2, o2))]
    step(*zs)
    fwd, rev = c.bits, c.bits[::-1]
    red = []
    for h in range(2):
        for q, order in ((0, fwd), (1, rev)):
            i = 2 * h + q
            red.append(plane_reduce(c, lambda g, h=h, q=q: gwo.at[pl.ds(2 * q, 2), g, :, pl.ds(256 * h, 256)], su.at[i], ib.at[i], order, c.fifth() if h else None))
    for f in red:
        next(f)

    def product(i, _):
        rows = pl.ds(pl.multiple_of(i * 2 * n, 2 * n), 2 * n)
        gm[rows, :] = jnp.dot(gmo[rows, :], wo[...], preferred_element_type=F32)
        return 0

    lax.fori_loop(0, TP, product, 0)
    for b in range(2 * TP):
        rows = pl.ds(b * n, n)
        act, slope = gelu_pair(br0[rows, :])
        g = gm[rows, :]
        lanes_in(adj, rows, g * act)
        gbr[0, rows, :] = (g * state[rows, :] * slope).astype(BF)
        lanes_in(a_ref, rows, jnp.exp(-8.0 * gates[1, rows, :] * db[...]))

    def step1(i, es):
        at = pl.ds(n - 1 - i, 2 * TP, stride=n)
        return [(v + e) * av for v, e, av in zip(each(adj, at), es, each(a_ref, at))]

    e = lax.fori_loop(0, n, step1, [jnp.zeros((2 * TP, 128), F32)] * (width // 128), unroll=8)
    e = jnp.concatenate(e, axis=1)
    etab[c.g] = e
    sh = share(c, etab)
    next(sh)
    for f in red:
        for _ in range(len(c.bits) - 1):
            next(f)
    finish(sh)
    ein = entering(c, lambda g: table[g, 0], lambda g: etab[g], width, True)

    def step2(i, es):
        at = pl.ds(n - 1 - i, 2 * TP, stride=n)
        vs = [v + e for v, e in zip(each(adj, at), es)]
        for q, v in enumerate(vs):
            adj[q, at, :] = v
        return [v * av for v, av in zip(vs, each(a_ref, at))]

    lax.fori_loop(0, n, step2, split(ein), unroll=8)
    row = lax.broadcasted_iota(jnp.int32, (n, 1), 0)
    total = [jnp.zeros((1, width), F32) for _ in range(8)]
    for b in range(2 * TP):
        rows = pl.ds(b * n, n)
        first = (row == 0) & (c.g == 0) if b % TP == 0 else None
        ad = lanes_out(adj, rows)
        gx, ga = gates[0, rows, :], gates[1, rows, :]
        decay, root = decay_terms(ga, db[...])
        mult = root if first is None else jnp.where(first, 1.0, root)
        cv = conv[rows, :].astype(F32)
        before = jnp.where(row == 0, carry[b:b + 1, :], pltpu.roll(state[rows, :], 1, 0))
        gmult = -(ad * cv * gx) * (decay * decay) / root
        if first is not None:
            gmult = jnp.where(first, 0.0, gmult)
        glog = ad * before * decay + gmult
        total[7] = total[7] + jnp.sum(glog * (-8.0 * ga), axis=0, keepdims=True)
        pre = [ad * cv * mult * gx * (1.0 - gx), glog * (-8.0 * db[...]) * ga * (1.0 - ga)]
        conved = ad * gx * mult
        for k in range(2):
            total[5 + k] = total[5 + k] + jnp.sum(pre[k], axis=0, keepdims=True)
            low = pre[k].astype(BF)
            gpl[k, rows, :] = low
            conved = conved + jnp.concatenate([
                lax.dot_general(low[:, h * 256:(h + 1) * 256], gb[k, h], (((1,), (1,)), ((), ())), preferred_element_type=F32)
                for h in range(2)], axis=1)
        gc[b, pl.ds(0, n), :] = conved
        heads[b] = conved[:8]
        ext[b % 2, pl.ds(0, 8), :] = rim[b]
        ext[b % 2, pl.ds(8, n), :] = ci[b].astype(F32)
        for k in range(4):
            total[k] = total[k] + jnp.sum(conved * ext[b % 2, pl.ds(8 - k, n), :], axis=0, keepdims=True)
        total[4] = total[4] + jnp.sum(conved, axis=0, keepdims=True)
    rslot = c.slot()
    out = c.to(heads, rim_in, c.at(g=(c.g + c.ng - 1) % c.ng), rslot)
    out.start()
    sums[...] = jnp.concatenate(total, axis=0)
    for k in range(2):
        for h in range(2):
            ggb[k, h] = lax.dot_general(conv[:, h * 256:(h + 1) * 256], gpl[k, :, h * 256:(h + 1) * 256], (((0,), (0,)), ((), ())), preferred_element_type=F32)
    out.wait()
    for b in range(2 * TP):
        rows = pl.ds(b * n, n)
        same = rim_in[b]
        nxt = jnp.zeros_like(same) if b % TP == TP - 1 else rim_in[b + 1]
        gc[b, pl.ds(n, 8), :] = jnp.where(c.g == c.ng - 1, nxt, same)
        v = chan[0:1] * gc[b, pl.ds(0, n), :]
        for k in range(1, 4):
            v = v + chan[k:k + 1] * gc[b, pl.ds(k, n), :]
        gbr[1, rows, :] = v.astype(BF)
    held = []
    for i, f in enumerate(red):
        finish(f)
        held.append(c.local(su.at[i, 0], rwo.at[pl.ds(2 * (i % 2), 2), :, pl.ds(256 * (i // 2), 256)], c.slot()))
        only(c.fifth() if i >= 2 else None, lambda: held[-1].start())
    run(*zs)
    for i, h in enumerate(held):
        only(c.fifth() if i >= 2 else None, lambda: h.wait())


def mix_bwd_call(gmo, wo, br0, ci, gb, chan, db, saved, gwo, r1, r2, units):
    ng = lax.axis_size("dp") // TP
    rows, width = br0.shape
    n = rows // (2 * TP)
    r = r1.shape[1]
    S = jax.ShapeDtypeStruct
    V = pltpu.VMEM
    return call(
        mix_bwd_kernel,
        (S((2, rows, width), BF), S((2, 2, 256, 256), F32), S((8, width), F32), S((TP, r, width), BF), S((r, units), BF), S((r, units), BF)),
        [VM] * 13 + [HBM] * 3,
        (VM,) * 3 + (HBM,) * 3,
        [V((rows, width), F32), V((width // 128, rows, 128), F32), V((width // 128, rows, 128), F32), V((2 * TP, n + 8, width), F32), V((2, rows, width), BF),
         V((2, n + 8, width), F32), V((2 * TP, 8, width), F32), V((ng, 2 * TP, width), F32), V((2 * TP, 8, width), F32),
         V((4, ng // 2, 2, r, 256), BF), V((4, ng - 1, 2, r, 256), BF)],
        6, 128,
    )(gmo, wo, br0, ci, gb, chan, db[None], *saved, gwo, r1, r2)


def mlp_kernel(nb, go, w0, w1, w2, hidden, gg0, gg1, part, gnb, v0, v1, v2, sems):
    copies = [pltpu.make_async_copy(a, b, sems.at[k]) for k, (a, b) in enumerate(((w0, v0), (w1, v1), (w2, v2)))]
    begin = pl.program_id(0) == 0

    @pl.when(begin)
    def _():
        for copy in copies:
            copy.start()

    def ready(k):
        pl.when(begin)(lambda: copies[k].wait())

    def back(a, w):
        return lax.dot_general(a, w, (((1,), (1,)), ((), ())), preferred_element_type=F32)

    ready(0)
    first = jnp.dot(nb[...], v0[...], preferred_element_type=F32)
    ready(1)
    second = jnp.dot(nb[...], v1[...], preferred_element_type=F32)
    act, slope = gelu_pair(first)
    low = (act * second).astype(BF)
    hidden[...] = low
    ready(2)
    gh = jnp.dot(go[...], v2[...], preferred_element_type=F32)
    a, b = (gh * second * slope).astype(BF), (gh * act).astype(BF)
    gg0[...] = a
    gg1[...] = b
    gnb[...] = (back(a, v0[...]) + back(b, v1[...])).astype(BF)
    part[...] = back(low, v2[...]).astype(BF)


def mlp_call(nb, go, w0, w1, w2):
    rows, d = nb.shape
    fs = w0.shape[1]
    n = 256
    S = jax.ShapeDtypeStruct
    wide = pl.BlockSpec((n, d), lambda i: (i, 0))
    slim = pl.BlockSpec((n, fs), lambda i: (i, 0))
    return pl.pallas_call(
        mlp_kernel,
        grid=(rows // n,),
        out_shape=(S((rows, fs), BF),) * 3 + (S((rows, d), BF),) * 2,
        in_specs=[wide, wide, HBM, HBM, HBM],
        out_specs=(slim,) * 3 + (wide,) * 2,
        scratch_shapes=[pltpu.VMEM((d, fs), BF)] * 3 + [pltpu.SemaphoreType.DMA((3,))],
        compiler_params=pltpu.CompilerParams(vmem_limit_bytes=VMEM_LIMIT),
    )(nb, go, w0, w1, w2)


def dot(a, b, ca, cb):
    return lax.dot_general(a, b, (((ca,), (cb,)), ((), ())), preferred_element_type=F32)


def body(block_input, lengths, norm_gains, w_branch, channel_params, gate_blocks, decay_param, w_out, w_mlp, w_down, out_grad):
    ndp, ng, t, g = plan()
    dp, mp = lax.axis_index("dp"), lax.axis_index("mp")
    rows, width = block_input.shape[1:]
    r, gr, units = w_branch.shape[1], gate_blocks.shape[2], w_mlp.shape[2]
    fs = cut(units, 0)[1]
    chan = heads_of(channel_params, 1)
    dpar = heads_of(decay_param[None], 1)[0]
    decay_base = jax.nn.softplus(dpar)
    pos = dp * 2 * rows + mp * rows + jnp.arange(rows, dtype=jnp.int32)
    valid = (pos[None] < lengths[:, None])[..., None]
    x = block_input
    grad_own = jnp.where(valid, out_grad, jnp.zeros_like(out_grad))
    na, wb0, wb1, wop, gb = start_call(x, norm_gains[0], w_branch, w_out.T, gate_blocks)
    na = na.reshape(-1, width)
    wb0, wb1 = wb0.reshape(width, 512), wb1.reshape(width, 512)
    gb = gb.reshape(2, 2, 256, 256)
    mixed, *saved, branch0, conv_input, wo, p0 = mix_fwd_call(na, wb0, wb1, gb, chan, decay_base, wop, w_mlp[0])
    wo = wo.reshape(width, 512)
    residual, nb, go, w0, w1, wd = mid_call(mixed, wo, x, grad_own, norm_gains[1], p0, w_mlp[1], w_down.T)
    nb, go = nb.reshape(-1, width), go.reshape(-1, width)
    w0, w1, wd = w0.reshape(width, fs), w1.reshape(width, fs), wd.reshape(width, fs)
    hidden, gg0, gg1, mlp_part, gnb = mlp_call(nb, go, w0, w1, wd)
    gres, gain_b, mlp_own, gmo, o0, r1, r2 = back_call(gnb, mlp_part, residual, grad_own, norm_gains[1], nb, go, gg0, gg1, hidden, ng, r, units)
    out = jnp.where(valid, residual + mlp_own, 0.0).astype(BF)
    gmo = gmo.reshape(-1, width)
    block = (TP, ng, r, 512)
    gwo = dot(gmo, mixed, 0, 0).astype(BF).reshape(block)
    gbr, ggb, chan_rows, rwo, o1, o2 = mix_bwd_call(gmo, wo, branch0, conv_input, gb, chan, decay_base, saved, gwo, r1, r2, units)
    gin, gains, table, owb, owo, ogb = end_call(
        wb0, wb1, x, gres, norm_gains[0], na, gbr, ggb.astype(BF).reshape(2, 2, TP, ng, gr, 256), rwo, gain_b, chan_rows, r,
    )
    g_wb, g_wo, g_gb = owb.astype(F32), owo.astype(F32).T, ogb.astype(F32)
    g_wm, g_wd = jnp.stack([o0, o1]).astype(F32), o2.astype(F32).T
    crow = jnp.concatenate([table[i, :, :256] for i in range(TP)] + [jnp.where(mp == 0, table[1, :, 256:], table[2, :, 256:])], -1)
    return out, gin, gains.reshape(2, width), g_wb, crow[:7], g_gb, crow[7] * jax.nn.sigmoid(decay_param), g_wo, g_wm, g_wd


def solution(mesh):
    return jax.shard_map(
        body,
        mesh=mesh,
        in_specs=(P(None, ("dp", "mp"), None), P(), P(), P(None, "dp", "mp"), P(None, "mp"), P(None, "mp", "dp", None), P("mp"), P("mp", "dp"), P(None, "dp", "mp"), P("mp", "dp"), P(None, ("dp", "mp"), None)),
        out_specs=(P(None, ("dp", "mp"), None), P(None, ("dp", "mp"), None), P(), P(None, "dp", "mp"), P(None, "mp"), P(None, "mp", "dp", None), P("mp"), P("mp", "dp"), P(None, "dp", "mp"), P("mp", "dp")),
        check_vma=False,
    )
```

```python
import functools

import jax
import jax.numpy as jnp
from jax import lax
from jax.experimental import pallas as pl
from jax.experimental.pallas import tpu as pltpu
from jax.sharding import PartitionSpec as P

MESH = pl.DeviceIdType.MESH
VMEM_LIMIT = 60 * 1024 * 1024


EPS = 1e-06
TP = 4
BF = jnp.bfloat16
F32 = jnp.float32


def plan():
    ndp = lax.axis_size("dp")
    ng = ndp // TP
    dp = lax.axis_index("dp")
    return ndp, ng, dp // ng, dp % ng


class Comm:
    def __init__(self, send, recv):
        self.send, self.recv, self.n = send, recv, 0
        self.ndp = lax.axis_size("dp")
        self.ng = self.ndp // TP
        dp = lax.axis_index("dp")
        self.t, self.g, self.m = dp // self.ng, dp % self.ng, lax.axis_index("mp")
        self.bits = [1 << k for k in range(self.ng.bit_length() - 1)]

    def at(self, t=None, g=None, m=None):
        t = self.t if t is None else t
        g = self.g if g is None else g
        return (t * self.ng + g, self.m if m is None else m)

    def fifth(self, t=None):
        return (self.t if t is None else t) == 1 + self.m

    def flip(self, g, b):
        return g + b - 2 * b * ((g // b) % 2)

    def barrier(self):
        sem = pltpu.get_barrier_semaphore()
        partners = [self.at(t=(self.t + o) % TP) for o in range(1, TP)]
        partners += [self.at(g=self.flip(self.g, b)) for b in self.bits] + [self.at(m=1 - self.m)]
        for p in partners:
            pl.semaphore_signal(sem, inc=1, device_id=p, device_id_type=MESH)
        pl.semaphore_wait(sem, len(partners))

    def slot(self):
        self.n += 1
        return self.n - 1

    def to(self, src, dst, dev, slot):
        return pltpu.make_async_remote_copy(
            src_ref=src, dst_ref=dst, send_sem=self.send.at[slot], recv_sem=self.recv.at[slot],
            device_id=dev, device_id_type=MESH,
        )

    def local(self, src, dst, slot):
        return pltpu.make_async_copy(src, dst, self.send.at[slot])


def finish(*flows):
    for f in flows:
        for _ in f:
            pass


def step(*flows):
    for f in flows:
        next(f)


def run(*flows):
    flows = list(flows)
    while flows:
        for f in list(flows):
            try:
                next(f)
            except StopIteration:
                flows.remove(f)


def ag_flow(c, own, full, late=False):
    t, m = c.t, c.m
    sib = c.at(m=1 - m)

    def slots():
        return [[c.slot() for _ in range(2)] for _ in range(TP - 1)]

    up, down, d2u, d2d = slots(), slots(), slots(), slots()
    d2o, loc = [c.slot() for _ in range(2)], [c.slot() for _ in range(2)]

    def row(b, s, mm):
        return full.at[s, b, mm]

    def up_copy(k, s):
        b = t - k
        return c.to(own.at[s] if k == 0 else row(b, s, m), row(b, s, m), c.at(t=t + 1), up[k][s])

    def down_copy(k, s):
        b = t + k
        return c.to(own.at[s] if k == 0 else row(b, s, m), row(b, s, m), c.at(t=t - 1), down[k][s])

    def side(b, slot, s, src=None):
        return c.to(row(b, s, m) if src is None else src, row(b, s, m), sib, slot)

    def got(b, slot, s, mm):
        return c.to(row(b, s, mm), row(b, s, mm), sib, slot)

    def both(f):
        return lambda: [f(s) for s in range(2)] and None

    pl.when((t < TP - 1) & (t > 0) if late else t < TP - 1)(both(lambda s: up_copy(0, s).start()))
    pl.when((t > 0) & (t < TP - 1) if late else t > 0)(both(lambda s: down_copy(0, s).start()))
    for s in range(2):
        side(t, d2o[s], s, own.at[s]).start()
        c.local(own.at[s], row(t, s, m), loc[s]).start()
    yield
    if late:
        pl.when(t == 0)(both(lambda s: up_copy(0, s).start()))
        pl.when(t == TP - 1)(both(lambda s: down_copy(0, s).start()))
        yield
    for k in range(TP - 1):
        def from_below(s):
            got(t - 1 - k, up[k][s], s, m).wait_recv()
            if k < TP - 2:
                pl.when(t < TP - 1)(lambda: up_copy(k + 1, s).start())
            side(t - 1 - k, d2u[k][s], s).start()

        def from_above(s):
            got(t + 1 + k, down[k][s], s, m).wait_recv()
            if k < TP - 2:
                pl.when(t > 0)(lambda: down_copy(k + 1, s).start())
            side(t + 1 + k, d2d[k][s], s).start()

        for s in range(2):
            pl.when(t - 1 - k >= 0)(lambda: from_below(s))
            pl.when(t + 1 + k < TP)(lambda: from_above(s))
        yield
    for s in range(2):
        c.local(own.at[s], row(t, s, m), loc[s]).wait()
        side(t, d2o[s], s, own.at[s]).wait_send()
        got(t, d2o[s], s, 1 - m).wait_recv()
    for k in range(TP - 1):
        pl.when((t < TP - 1) & (t - k >= 0))(both(lambda s: up_copy(k, s).wait_send()))
        pl.when((t > 0) & (t + k < TP))(both(lambda s: down_copy(k, s).wait_send()))

        def below(s):
            side(t - 1 - k, d2u[k][s], s).wait_send()
            got(t - 1 - k, d2u[k][s], s, 1 - m).wait_recv()

        def above(s):
            side(t + 1 + k, d2d[k][s], s).wait_send()
            got(t + 1 + k, d2d[k][s], s, 1 - m).wait_recv()

        pl.when(t - 1 - k >= 0)(both(below))
        pl.when(t + 1 + k < TP)(both(above))


def rs_scratch(rows, width, made=False):
    return [
        pltpu.VMEM((1 if made else 2, 2, TP, rows, width), BF),
        pltpu.VMEM((2, TP - 1, 2, rows, width), BF),
        pltpu.VMEM((TP - 1, 2, rows, width), BF),
    ]


def rs_flow(c, part, out, pair, inbox, outbox, make=None):
    t, m = c.t, c.m
    n = part.shape[3]
    other = c.at(m=1 - m)
    lower = t < TP // 2
    u = jnp.where(lower, t, TP - 1 - t)
    da = jnp.where(lower, 0, 1)
    hop = 1 - 2 * da
    near = [[c.slot() for _ in range(2)] for _ in range(TP)]
    here = [[c.slot() for _ in range(2)] for _ in range(TP)]
    sib = pair.at[pair.shape[0] - 1]
    own = (lambda s, b: part.at[s, b, m]) if make else (lambda s, b: pair.at[0, s, b])
    base = c.n
    for _ in range(4 * (TP - 1)):
        c.slot()

    def real(d):
        return jnp.where(lower, d, TP - 1 - d)

    def cross(d, s):
        return c.to(part.at[s, real(d), 1 - m], sib.at[s, real(d)], other, near[d][s])

    def load(d, s):
        return c.local(part.at[s, real(d), m], own(s, real(d)), here[d][s])

    def near_in(d, s):
        cross(d, s).wait_recv()
        if make is None:
            load(d, s).wait()

    def msg(flow, j, s):
        way = da if flow == 0 else 1 - da
        dev = c.at(t=t + hop if flow == 0 else t - hop)
        return c.to(outbox.at[j if flow == 0 else 2, s], inbox.at[way, j, s], dev, base + (way * (TP - 1) + j) * 2 + s)

    def add(d, s, into, terms):
        b = real(d)

        def rows16(i, _):
            sl = pl.ds(pl.multiple_of(i * 16, 16), 16)
            v = own(s, b)[sl, :].astype(F32) + sib[s, b, sl, :].astype(F32)
            for way, j in terms:
                v = v + inbox[way, j, s, sl, :].astype(F32)
            into(s, sl, v)
            return 0

        lax.fori_loop(0, n // 16, rows16, 0)

    def put(j):
        def into(s, sl, v):
            outbox[j, s, sl, :] = v.astype(BF)
        return into

    def final(s, sl, v):
        out[s, sl, :] = v

    def issue(d):
        if make is not None:
            b = real(d)
            rows = [pl.ds(pl.multiple_of((s * TP + b) * 2 * n, 2 * n), 2 * n) for s in range(2)]
            v = make(rows).astype(BF).reshape(2, 2, n, part.shape[4])
            for s in range(2):
                part[s, b] = v[s]
        for s in range(2):
            if make is None:
                load(d, s).start()
            cross(d, s).start()

    def send_out(d, j):
        for s in range(2):
            near_in(d, s)
            add(d, s, put(j), [])
            msg(0, j, s).start()

    issue(3)
    issue(2)
    yield
    pl.when(u == 0)(lambda: send_out(3, 0))
    issue(1)
    pl.when(u == 0)(lambda: send_out(2, 1))
    issue(0)
    pl.when(u == 0)(lambda: send_out(1, 2))
    yield
    for d, j in ((3, 0), (2, 1)):
        def pass_on():
            for s in range(2):
                near_in(d, s)
                msg(0, j, s).wait_recv()
                add(d, s, put(j), [(da, j)])
                msg(0, j, s).start()

        pl.when(u == 1)(pass_on)
        yield

    def back():
        for s in range(2):
            near_in(0, s)
            msg(1, 0, s).wait_recv()
            add(0, s, put(2), [(1 - da, 0)])
            msg(1, 0, s).start()

    pl.when(u == 1)(back)
    yield
    for s in range(2):
        def end0():
            near_in(0, s)
            msg(1, 0, s).wait_recv()
            add(0, s, final, [(1 - da, 0)])

        def end1():
            near_in(1, s)
            msg(0, 2, s).wait_recv()
            msg(1, 1, s).wait_recv()
            add(1, s, final, [(da, 2), (1 - da, 1)])

        pl.when(u == 0)(end0)
        pl.when(u == 1)(end1)
    for s in range(2):
        for d in range(TP):
            cross(d, s).wait_send()
        for j in range(2):
            msg(0, j, s).wait_send()
        pl.when(u == 0)(lambda: msg(0, 2, s).wait_send())
        pl.when(u == 1)(lambda: msg(1, 0, s).wait_send())


def inner(t):
    return (t == 1) | (t == 2)


def outer(t):
    return (t == 0) | (t == TP - 1)


def cut(width, t):
    tiles = width // 128
    big = -(-tiles // TP)
    small = (tiles - 2 * big) // 2
    return pl.multiple_of((small * t + (big - small) * (t > 1) * (t - 1)) * 128, 128), big * 128, small * 128


def spread_z(c, src, dst, kinds=((None, 0),), owner="to"):
    slots = [c.slot() for _ in range(TP)]

    def each_kind(sender, taker, f):
        own = taker if owner == "to" else sender
        for which, k in kinds:
            if which is None:
                f(k)
            else:
                pl.when(which(own))(functools.partial(f, k))

    def copy(o, k):
        to = (c.t + o) % TP
        return c.to(src(to, k), dst(c.t, k), c.at(t=to), slots[o])

    def back(o, k):
        frm = (c.t + TP - o) % TP
        return c.to(dst(frm, k), dst(frm, k), c.at(t=frm), slots[o])

    for o in range(1, TP):
        each_kind(c.t, (c.t + o) % TP, lambda k: copy(o, k).start())
    each_kind(c.t, c.t, lambda k: c.local(src(c.t, k), dst(c.t, k), slots[0]).start())
    yield
    each_kind(c.t, c.t, lambda k: c.local(src(c.t, k), dst(c.t, k), slots[0]).wait())
    for o in range(1, TP):
        each_kind((c.t + TP - o) % TP, c.t, lambda k: back(o, k).wait_recv())
    yield
    for o in range(1, TP):
        each_kind(c.t, (c.t + o) % TP, lambda k: copy(o, k).wait_send())


def only(cond, f):
    if cond is None:
        f()
    else:
        pl.when(cond)(f)


def plane_gather(c, block, order, own=None, cond=None):
    have = [0]
    done = []
    held = None
    if own is not None:
        held = c.local(own, block(c.g), c.slot())
        only(cond, lambda: held.start())
    for b in order:
        dev = c.at(g=c.flip(c.g, b))
        sent = []
        for x in have:
            gg = c.g
            for bit in c.bits:
                if x & bit:
                    gg = c.flip(gg, bit)
            src = own if own is not None and x == 0 else block(gg)
            sent.append(c.to(src, block(gg), dev, c.slot()))
        only(cond, lambda: [copy.start() for copy in sent] and None)
        yield
        only(cond, lambda: [copy.wait_recv() for copy in sent] and None)
        done += sent
        have = have + [x ^ b for x in have]
    only(cond, lambda: [copy.wait_send() for copy in done] and None)
    if held is not None:
        only(cond, lambda: held.wait())


def plane_reduce(c, own, sums, inbox, order, cond=None):
    def place(x):
        gg = c.g
        for bit in c.bits:
            if x & bit:
                gg = c.flip(gg, bit)
        return gg

    left = list(range(c.ng))
    spot = {}
    done = []
    base = 0
    for k, b in enumerate(order):
        dev = c.at(g=c.flip(c.g, b))
        away = [x for x in left if x & b]
        left = [x for x in left if not x & b]
        if k == 0:
            spot = {x: i for i, x in enumerate(left)}
        sent = [c.to(own(place(x)) if k == 0 else sums.at[spot[x]], inbox.at[base + i], dev, c.slot()) for i, x in enumerate(away)]
        held = [c.local(own(place(x)), sums.at[spot[x]], c.slot()) for x in left] if k == 0 else []

        def begin():
            for copy in sent + held:
                copy.start()

        only(cond, begin)
        yield

        def take():
            for i, x in enumerate(left):
                sent[i].wait_recv()
                if k == 0:
                    held[i].wait()
                add_blocks(sums.at[spot[x]], inbox.at[base + i])

        only(cond, take)
        base += len(away)
        done += sent
    only(cond, lambda: [copy.wait_send() for copy in done] and None)


def add_blocks(a, b):
    def one(i, _):
        a[i] = a[i] + b[i]
        return 0

    lax.fori_loop(0, a.shape[0], one, 0)


def grad_flow(c, lhs, rhs, out, rbuf, lbuf, stage, halves):
    wide = lbuf.shape[2]
    _, ng, r, cols = stage.shape
    load = c.local(rhs, rbuf, c.slot())
    load.start()
    pieces = [c.local(lhs.at[:, pl.ds(k * wide, wide)], lbuf.at[k % 2], c.slot()) for k in range(TP)]
    puts = [c.local(stage.at[k % 2], out.at[k], c.slot()) for k in range(TP)]
    pieces[0].start()
    pieces[1].start()
    load.wait()
    for k in range(TP):
        pieces[k].wait()
        v = lax.dot_general(lbuf[k % 2], rbuf[...], (((0,), (0,)), ((), ())), preferred_element_type=F32)
        if k + 2 < TP:
            pieces[k + 2].start()
        stage[k % 2] = v.astype(BF).reshape(ng, r, cols)
        puts[k].start()
        if k % 2:
            puts[k - 1].wait()
            puts[k].wait()
            step(*halves[k // 2])
            yield


def call(kernel, out_shape, in_specs, out_specs, scratch, cid, slots=160):
    return pl.pallas_call(
        kernel,
        out_shape=out_shape,
        in_specs=in_specs,
        out_specs=out_specs,
        scratch_shapes=list(scratch) + [pltpu.SemaphoreType.DMA((slots,)), pltpu.SemaphoreType.DMA((slots,))],
        compiler_params=pltpu.CompilerParams(collective_id=cid, has_side_effects=True, vmem_limit_bytes=VMEM_LIMIT),
    )


HBM = pl.BlockSpec(memory_space=pl.ANY)
VM = pl.BlockSpec(memory_space=pltpu.VMEM)


def heads_to(c, ref, dst, extra):
    def src(t, k):
        return ref.at[:, pl.ds(1024, 256)] if extra else ref.at[:, pl.ds(pl.multiple_of(t * 256, 256), 256)]

    def into(t, k):
        return dst(t).at[:, pl.ds(256 if extra else 0, 256)]

    return src, into, (((c.fifth, 0),) if extra else ((None, 0),))


def units_to(ref, dst):
    width = ref.shape[1]
    _, big, small = cut(width, 0)

    def src(t, k):
        return ref.at[:, pl.ds(cut(width, t)[0], k)]

    def into(t, k):
        return dst(t).at[:, pl.ds(0, k)]

    return src, into, ((inner, big), (outer, small))


def units_back(ref, dst):
    width = dst.shape[1]
    _, big, small = cut(width, 0)

    def src(t, k):
        return ref(t).at[:, pl.ds(0, k)]

    def into(t, k):
        return dst.at[:, pl.ds(cut(width, t)[0], k)]

    return src, into, ((inner, big), (outer, small)), "from"


def heads_out(c, ref, dst, extra):
    def src(t, k):
        return ref(t).at[:, pl.ds(256 if extra else 0, 256)]

    def into(t, k):
        return dst.at[:, pl.ds(1024, 256)] if extra else dst.at[:, pl.ds(pl.multiple_of(t * 256, 256), 256)]

    return src, into, (((c.fifth, 0),) if extra else ((None, 0),)), "from"


START_ORDER = "azgagaw"


def start_kernel(x, gain, wbr, wot, gates, full_a, wb0, wb1, wop, gb, own, zero, send, recv):
    c = Comm(send, recv)
    c.barrier()
    wb = (wb0, wb1)
    z = []
    for extra in (False, True):
        for k in range(2):
            z.append(spread_z(c, *heads_to(c, wbr.at[k], lambda t, k=k: wb[k].at[t, c.g], extra)))
    z.append(spread_z(c, lambda t, k: gates.at[:, t], lambda t, k: gb.at[:, 0, t, c.g]))
    z.append(spread_z(c, lambda t, k: gates.at[:, 4], lambda t, k: gb.at[:, 1, t, c.g], ((c.fifth, 0),)))
    for f in z:
        next(f)
    for s in range(2):
        v = x[s].astype(F32)
        own[s] = (v * lax.rsqrt(jnp.mean(v * v, axis=-1, keepdims=True) + EPS) * gain[...]).astype(BF)
    zero[...] = jnp.zeros_like(zero)
    fills = [(zero, wb[k].at[:, g, :, pl.ds(256, 256)], c.slot()) for k in range(2) for g in range(c.ng)]
    fills += [(zero.at[:, pl.ds(0, gates.shape[2])], gb.at[k, 1, :, g], c.slot()) for k in range(2) for g in range(c.ng)]
    idle = jnp.logical_not(c.fifth())
    pl.when(idle)(lambda: [c.local(*f).start() for f in fills] and None)
    fwd, rev = c.bits, c.bits[::-1]
    g1 = []
    for h in range(2):
        for k, order in ((0, fwd), (1, rev)):
            g1.append(plane_gather(c, lambda g, k=k, h=h: wb[k].at[:, g, :, pl.ds(256 * h, 256)], order, None, c.fifth() if h else None))
            g1.append(plane_gather(c, lambda g, k=k, h=h: gb.at[k, h, :, g], order, None, c.fifth() if h else None))
    ag = ag_flow(c, own, full_a)
    z2 = [spread_z(c, *heads_to(c, wot, lambda t: wop.at[t], extra)) for extra in (False, True)]
    does = {"z": lambda: step(*z), "g": lambda: step(*g1), "a": lambda: step(ag), "w": lambda: step(*z2)}
    for what in START_ORDER:
        does[what]()
    run(ag, *g1, *z, *z2)
    pl.when(idle)(lambda: [c.local(*f).wait() for f in fills] and None)


def start_call(x, gain, wbr, wot, gates):
    ng = lax.axis_size("dp") // TP
    _, n, d = x.shape
    r, gr = wbr.shape[1], gates.shape[2]
    S = jax.ShapeDtypeStruct
    return call(
        start_kernel,
        (S((2, TP, 2, n, d), BF), S((TP, ng, r, 512), BF), S((TP, ng, r, 512), BF), S((TP, r, 512), BF), S((2, 2, TP, ng, gr, 256), BF)),
        [VM, VM, HBM, HBM, HBM],
        (HBM,) * 5,
        [pltpu.VMEM((2, n, d), BF), pltpu.VMEM((TP, r, 256), BF)],
        1, 256,
    )(x, gain[None], wbr, wot, gates)


MID_LATE = False
MID_ORDER = "ra0yrr0ary1raNza1z2A2A"


def mid_kernel(mixed, wo, x, go, gain, p0, m1, m2, zero, res, full, full_g, w0, w1, w2, tot, own, part, pair, inbox, outbox, send, recv):
    c = Comm(send, recv)
    c.barrier()
    fwd, rev = c.bits, c.bits[::-1]
    pad = zero.shape[2]
    fills = [(zero, w.at[:, c.g, :, pl.ds(w.shape[3] - pad, pad)], c.slot()) for w in (w1, w2)]

    def gather(w, own=None):
        for k, order in ((0, fwd), (1, rev)):
            at = pl.ds(2 * k, 2)
            yield plane_gather(c, lambda g, at=at: w.at[at, g], order, None if own is None else own.at[at])

    last = len(c.bits) - 1

    def make(rows):
        v = jnp.concatenate([mixed[at, :] for at in rows], axis=0)
        return lax.dot_general(v, wo[...], (((1,), (1,)), ((), ())), preferred_element_type=F32)

    rs = rs_flow(c, part, tot, pair, inbox, outbox, make)
    ag, ag2 = ag_flow(c, own, full), ag_flow(c, go, full_g, MID_LATE)
    z1 = spread_z(c, *units_to(m1, lambda t: w1.at[t, c.g]))
    z2 = spread_z(c, *units_to(m2, lambda t: w2.at[t, c.g]))
    g = [list(gather(w0, p0)), list(gather(w1)), list(gather(w2))]

    def norm():
        finish(rs)
        for s in range(2):
            v = x[s].astype(F32) + tot[s]
            res[s] = v
            own[s] = (v * lax.rsqrt(jnp.mean(v * v, axis=-1, keepdims=True) + EPS) * gain[...]).astype(BF)
        step(ag)

    begun = [0, 0, 0]

    def plane(k):
        if not begun[k]:
            step(*g[k])
        else:
            for _ in range(last):
                step(*g[k])
        begun[k] = 1

    does = {"r": lambda: step(rs), "N": norm, "A": lambda: step(ag), "a": lambda: step(ag2), "y": lambda: step(z1), "z": lambda: step(z2),
            "0": lambda: plane(0), "1": lambda: plane(1), "2": lambda: plane(2)}
    for i, what in enumerate(MID_ORDER):
        does[what]()
        if i == 4:
            pl.when(outer(c.t))(lambda: [c.local(*f).start() for f in fills] and [c.local(*f).wait() for f in fills] and None)
    finish(ag, ag2, *g[0], *g[1], *g[2], z1, z2)


def mid_call(mixed, wo, x, go, gain, p0, m1, m2):
    _, n, d = x.shape
    ng = lax.axis_size("dp") // TP
    _, r, fs = p0.shape
    _, big, small = cut(m1.shape[1], 0)
    zero = jnp.zeros((TP, r, big - small), BF)
    S = jax.ShapeDtypeStruct
    w = S((TP, ng, r, fs), BF)
    return call(
        mid_kernel,
        (S((2, n, d), F32), S((2, TP, 2, n, d), BF), S((2, TP, 2, n, d), BF), w, w, w),
        [VM, VM, VM, VM, VM, HBM, HBM, HBM, VM],
        (VM,) + (HBM,) * 5,
        [pltpu.VMEM((2, n, d), F32), pltpu.VMEM((2, n, d), BF), pltpu.VMEM((2, TP, 2, n, d), BF)] + rs_scratch(n, d, True),
        2,
    )(mixed, wo, x, go, gain[None], p0, m1, m2, zero)


def back_kernel(part, part2, res, go, gain, nb, gall, gg0, gg1, hidden, gres, gsum, mlp_own, full, o0, r1, r2, h0, h1, h2,
                tot, own, pair, inbox, outbox, pair2, inbox2, outbox2, su, ib, rbuf, lbuf, stage, send, recv):
    c = Comm(send, recv)
    c.barrier()
    fwd, rev = c.bits, c.bits[::-1]
    rs = rs_flow(c, part, tot, pair, inbox, outbox)
    next(rs)
    red, grad = [], []
    for k, h in enumerate((h0, h1, h2)):
        red.append([plane_reduce(c, lambda g, h=h, q=q: h.at[pl.ds(2 * q, 2), g], su.at[2 * k + q], ib.at[2 * k + q], (fwd, rev)[q]) for q in range(2)])
        grad.append(grad_flow(c, gall if k == 2 else nb, (gg0, gg1, hidden)[k], h, rbuf, lbuf, stage, [[f] for f in red[k]]))
    last = len(c.bits) - 1

    def onward(parts):
        for _ in range(last):
            step(*parts)

    step(rs)
    step(grad[0])
    step(grad[0])
    step(rs)
    step(grad[1])
    step(rs)
    step(grad[1])
    onward(red[0])
    step(rs)
    rs2 = rs_flow(c, part2, mlp_own, pair2, inbox2, outbox2)
    finish(rs)
    total = jnp.zeros_like(gsum)
    for s in range(2):
        v = res[s]
        scale = lax.rsqrt(jnp.mean(v * v, axis=-1, keepdims=True) + EPS)
        normal = v * scale
        gn = tot[s]
        total = total + jnp.sum(gn * normal, axis=0, keepdims=True)
        q = gn * gain[...]
        gr = scale * (q - normal * jnp.mean(q * normal, axis=-1, keepdims=True)) + go[s].astype(F32)
        gres[s] = gr
        own[s] = gr.astype(BF)
    gsum[...] = total
    ag = ag_flow(c, own, full)
    step(ag, rs2)
    step(rs2)
    step(grad[2])
    step(grad[2])
    finish(*red[0])
    s0 = spread_z(c, *units_back(lambda t: su.at[t // 2, 0, t % 2], o0))
    step(s0)
    onward(red[1])
    step(ag, rs2)
    held = []

    def keep(k, out):
        finish(*red[k])
        for q in range(2):
            held.append(c.local(su.at[2 * k + q, 0], out.at[pl.ds(2 * q, 2)], c.slot()))
            held[-1].start()

    step(ag, rs2)
    onward(red[2])
    keep(1, r1)
    step(rs2)
    finish(ag, rs2)
    keep(2, r2)
    finish(s0, *grad)
    for h in held:
        h.wait()


def back_call(part, part2, res, go, gain, nb, gall, gg0, gg1, hidden, ng, r, units):
    _, n, d = go.shape
    rows, fs = hidden.shape
    S = jax.ShapeDtypeStruct
    shape = (2, TP, 2, n, d)
    h = S((TP, ng, r, fs), BF)
    *outs, _, _, _ = call(
        back_kernel,
        (S((2, n, d), F32), S((1, d), F32), S((2, n, d), F32), S(shape, BF), S((r, units), BF), S((TP, r, fs), BF), S((TP, r, fs), BF), h, h, h),
        [HBM] * 2 + [VM] * 3 + [HBM] * 5,
        (VM, VM, VM) + (HBM,) * 7,
        [pltpu.VMEM((2, n, d), F32), pltpu.VMEM((2, n, d), BF)] + rs_scratch(n, d) + rs_scratch(n, d)
        + [pltpu.VMEM((6, ng // 2, 2, r, fs), BF), pltpu.VMEM((6, ng - 1, 2, r, fs), BF)]
        + [pltpu.VMEM((rows, fs), BF), pltpu.VMEM((2, rows, ng * r), BF), pltpu.VMEM((2, ng, r, fs), BF)],
        3, 256,
    )(part.reshape(shape), part2.reshape(shape), res, go, gain[None], nb, gall, gg0, gg1, hidden)
    return outs


def small_flow(c, small, inbox, zbox):
    for k, b in enumerate(c.bits):
        copy = c.to(small.at[k], inbox.at[k], c.at(g=c.flip(c.g, b)), c.slot())
        copy.start()
        yield
        copy.wait()
        small[k + 1] = small[k] + inbox[k]
    last = len(c.bits)
    z = spread_z(c, lambda t, k: small.at[last], lambda t, k: zbox.at[t])
    next(z)
    yield
    run(z)


def end_kernel(wb0, wb1, gbr, x, gres, gain, na, gsrc, gmo, mixed, ggb, gain_b, chan_rows, gin, gains, gchan, gdec, owb, owo, ogb, gwb0, gwb1, gwo,
               sm_a, in_a, z_a, sm_b, in_b, sbox, z_b, tot, part, pair, inbox, outbox, su_x, in_x, su_g, in_g, rbuf, lbuf, stage, send, recv):
    c = Comm(send, recv)
    c.barrier()
    fwd, rev = c.bits, c.bits[::-1]
    red, gate, every = [], [], []
    for k, gw in enumerate((gwb0, gwb1, gwo)):
        red.append(([], []))
        for h in range(2):
            i, cond = 2 * k + h, c.fifth() if h else None
            lane = (lambda t: pl.ds(1024, 256)) if h else (lambda t: pl.ds(pl.multiple_of(t * 256, 256), 256))
            which = ((c.fifth, 0),) if h else ((None, 0),)
            dst = (lambda t, q, k=k, lane=lane: owb.at[k, :, lane(t)]) if k < 2 else (lambda t, q, lane=lane: owo.at[:, lane(t)])
            flows = []
            for q, order in ((0, fwd), (1, rev)):
                at = pl.ds(2 * q, 2)
                flows.append(plane_reduce(c, lambda g, gw=gw, h=h, at=at: gw.at[at, g, :, pl.ds(256 * h, 256)], su_x.at[i, :, at], in_x.at[i, :, at], order, cond))
                red[k][q].append(flows[q])
            every.append((flows, spread_z(c, lambda t, q, i=i: su_x.at[i, 0, t], dst, which, "from")))
            if k < 2:
                gate.append(plane_reduce(c, lambda g, k=k, h=h: ggb.at[k, h, :, g], su_g.at[i], in_g.at[i], rev if k else fwd, cond))
                every.append((gate[-1:], spread_z(c, lambda t, q, i=i: su_g.at[i, 0, t], lambda t, q, k=k, h=h: ogb.at[k, 4 if h else t], which, "from")))

    def onward(*flows):
        for _ in range(len(c.bits) - 1):
            step(*flows)

    def make(rows):
        v = [jnp.concatenate([gbr[k, at, :] for at in rows], axis=0) for k in range(2)]
        v = [lax.dot_general(v[k], w[...], (((1,), (1,)), ((), ())), preferred_element_type=F32) for k, w in enumerate((wb0, wb1))]
        return v[0] + v[1]

    rs = rs_flow(c, part, tot, pair, inbox, outbox, make)
    next(rs)
    grad = [grad_flow(c, lhs, rhs, gw, rbuf, lbuf, stage, red[k]) for k, (lhs, rhs, gw) in enumerate(((na, gsrc.at[0], gwb0), (na, gsrc.at[1], gwb1), (gmo, mixed, gwo)))]
    step(*gate)
    sm_a[0] = chan_rows[...]
    chan = small_flow(c, sm_a, in_a, z_a)
    step(chan)
    step(rs)
    step(grad[2])
    step(grad[2])
    step(rs)
    step(grad[0])
    step(grad[0])
    step(chan)
    step(rs)
    step(grad[1])
    step(grad[1])
    onward(*red[2][0], *red[2][1], *red[0][0], *red[0][1])
    for _ in c.bits[1:]:
        step(chan)
    step(rs)
    onward(*red[1][0], *red[1][1], *gate)
    for flows, z in every:
        finish(*flows)
        step(z)
    finish(rs)
    total = jnp.zeros_like(gain)
    for s in range(2):
        v = x[s].astype(F32)
        scale = lax.rsqrt(jnp.mean(v * v, axis=-1, keepdims=True) + EPS)
        normal = v * scale
        gn = tot[s]
        total = total + jnp.sum(gn * normal, axis=0, keepdims=True)
        q = gn * gain[...]
        gin[s] = scale * (q - normal * jnp.mean(q * normal, axis=-1, keepdims=True)) + gres[s]
    quarter = sm_b.shape[2]
    for k in range(4):
        sm_b[0, k:k + 1, :] = total[:, k * quarter:(k + 1) * quarter]
        sm_b[0, 4 + k:5 + k, :] = gain_b[:, k * quarter:(k + 1) * quarter]
    finish(small_flow(c, sm_b, in_b, z_b))
    sbox[0] = z_b[0] + z_b[1] + z_b[2] + z_b[3]
    copy = c.to(sbox.at[0], sbox.at[1], c.at(m=1 - c.m), c.slot())
    copy.start()
    finish(chan)
    fifth = z_a[1 + c.m]
    for out, rows in ((gchan, slice(0, 7)), (gdec, slice(7, 8))):
        for t in range(TP):
            out[:, t * 256:(t + 1) * 256] = z_a[t, rows, :256]
        out[:, 1024:] = fifth[rows, 256:]
    copy.wait()
    gains[...] = sbox[0] + sbox[1]
    run(*grad, *[z for _, z in every])


def end_call(wb0, wb1, x, gres, gain, na, gsrc, gmo, mixed, ggb, gain_b, chan_rows, r):
    _, n, d = x.shape
    ng = lax.axis_size("dp") // TP
    gr, steps = ggb.shape[4], (lax.axis_size("dp") // TP).bit_length()
    V = pltpu.VMEM
    S = jax.ShapeDtypeStruct

    def sets(k, rows, width):
        return [pltpu.VMEM((k, ng // 2, TP, rows, width), BF), pltpu.VMEM((k, ng - 1, TP, rows, width), BF)]

    *outs, _, _, _ = call(
        end_kernel,
        (S((2, n, d), F32), S((8, d // 4), F32), S((7, 1280), F32), S((1, 1280), F32), S((2, r, 1280), BF), S((r, 1280), BF), S((2, 5, gr, 256), BF))
        + (S((TP, ng, r, 512), BF),) * 3,
        [VM] * 6 + [HBM] * 4 + [HBM] + [VM] * 2,
        (VM,) * 4 + (HBM,) * 6,
        [V((steps, 8, 512), F32), V((steps - 1, 8, 512), F32), V((TP, 8, 512), F32),
         V((steps, 8, d // 4), F32), V((steps - 1, 8, d // 4), F32), V((2, 8, d // 4), F32), V((TP, 8, d // 4), F32),
         pltpu.VMEM((2, n, d), F32), pltpu.VMEM((2, TP, 2, n, d), BF)] + rs_scratch(n, d, True) + sets(6, r, 256) + sets(4, gr, 256)
        + [pltpu.VMEM((na.shape[0], 512), BF), pltpu.VMEM((2, na.shape[0], ng * r), BF), pltpu.VMEM((2, ng, r, 512), BF)],
        4, 256,
    )(wb0, wb1, gsrc, x, gres, gain[None], na, gsrc, gmo, mixed, ggb, gain_b, chan_rows)
    return outs


def heads_of(a, axis):
    _, _, t, _ = plan()
    p = lax.dynamic_slice_in_dim(a, t * 256, 256, axis)
    q = lax.dynamic_slice_in_dim(a, 1024, 256, axis)
    q = jnp.where(t == 1 + lax.axis_index("mp"), q, jnp.zeros_like(q))
    return jnp.concatenate([p, q], axis)


def gelu_pair(v):
    k = 0.7978845608028654
    v2 = v * v
    th = jnp.tanh(k * v * (1.0 + 0.044715 * v2))
    half = 0.5 * (1.0 + th)
    return v * half, half + 0.5 * v * (1.0 - th * th) * k * (1.0 + 3.0 * 0.044715 * v2)


def decay_terms(ga, db):
    log_a = -8.0 * ga * db
    y = 2.0 * log_a
    series = 1.0 + y * (1 / 8)
    for k in range(7, 1, -1):
        series = 1.0 + y * (1 / k) * series
    m1 = jnp.where(y > -0.35, y * series, jnp.exp(y) - 1.0)
    return jnp.exp(log_a), jnp.sqrt(-m1)


def lanes_in(ref, rows, v):
    for q in range(ref.shape[0]):
        ref[q, rows, :] = v[:, q * 128:(q + 1) * 128]


def lanes_out(ref, rows):
    return jnp.concatenate([ref[q, rows, :] for q in range(ref.shape[0])], axis=1)


def each(ref, at):
    return [ref[q, at, :] for q in range(ref.shape[0])]


def split(v):
    return [v[:, q * 128:(q + 1) * 128] for q in range(v.shape[1] // 128)]


def plane_partners(c):
    return [c.at(g=(c.g + o) % c.ng) for o in range(1, c.ng)]


def greet(partners):
    sem = pltpu.get_barrier_semaphore()
    for p in partners:
        pl.semaphore_signal(sem, inc=1, device_id=p, device_id_type=MESH)
    pl.semaphore_wait(sem, len(partners))


def line_partners(c):
    return [c.at(t=(c.t + o) % TP) for o in range(1, TP)]


def share(c, table):
    slots = [c.slot() for _ in range(1, c.ng)]
    for o, slot in enumerate(slots, 1):
        c.to(table.at[c.g], table.at[c.g], c.at(g=(c.g + o) % c.ng), slot).start()
    yield
    for o, slot in enumerate(slots, 1):
        frm = (c.g + c.ng - o) % c.ng
        c.to(table.at[frm], table.at[frm], c.at(g=frm), slot).wait_recv()
    for o, slot in enumerate(slots, 1):
        c.to(table.at[c.g], table.at[c.g], c.at(g=(c.g + o) % c.ng), slot).wait_send()


def entering(c, prod, last, width, reverse):
    rows = [None] * (2 * TP)
    spots = [(t, g) for t in range(TP) for g in range(c.ng)]
    for s in range(2):
        cur = jnp.zeros((1, width), F32)
        for t, g in (spots[::-1] if reverse else spots):
            b = s * TP + t
            old = rows[b]
            rows[b] = cur if old is None else jnp.where(c.g == g, cur, old)
            cur = last(g)[b:b + 1] + prod(g)[b:b + 1] * cur
    return jnp.concatenate(rows, axis=0)


def mix_fwd_kernel(na, wb0, wb1, gb, chan, db, wop, m0, zero, blank, mixed, conv, gates, state, rim, carry, table, br0, ci, wo, p0, a_ref, d_ref, ext, rim_in, send, recv):
    c = Comm(send, recv)
    greet(plane_partners(c) + line_partners(c))
    n, width = ci.shape[1], ci.shape[2]
    z0 = spread_z(c, *units_to(m0, lambda t: p0.at[t]))
    next(z0)
    fwd, rev = c.bits, c.bits[::-1]
    g0 = []
    for h in range(2):
        for q, order in ((0, fwd), (1, rev)):
            at, lane = pl.ds(2 * q, 2), pl.ds(256 * h, 256)
            g0.append(plane_gather(c, lambda g, at=at, lane=lane: wo.at[at, g, :, lane], order, wop.at[at, :, lane], c.fifth() if h else None))
    step(*g0)
    fills = [c.local(blank, wo.at[:, g, :, pl.ds(256, 256)], c.slot()) for g in range(c.ng)]
    idle = jnp.logical_not(c.fifth())
    pl.when(idle)(lambda: [f.start() for f in fills] and None)
    pad = zero.shape[2]
    fill = c.local(zero, p0.at[:, :, pl.ds(p0.shape[2] - pad, pad)], c.slot())
    pl.when(outer(c.t))(lambda: fill.start())

    def branch(i, _):
        rows = pl.ds(pl.multiple_of(i * 2 * n, 2 * n), 2 * n)
        v = jnp.dot(na[rows, :], wb1[...], preferred_element_type=F32).astype(BF)
        ci[2 * i] = v[:n]
        ci[2 * i + 1] = v[n:]
        return 0

    lax.fori_loop(0, TP, branch, 0)
    out = c.to(ci.at[:, pl.ds(n - 16, 16)], rim_in, c.at(g=(c.g + 1) % c.ng), c.slot())
    out.start()

    def gate(i, _):
        rows = pl.ds(pl.multiple_of(i * 2 * n, 2 * n), 2 * n)
        br0[rows, :] = jnp.dot(na[rows, :], wb0[...], preferred_element_type=F32)
        return 0

    lax.fori_loop(0, TP, gate, 0)
    out.wait()
    row = lax.broadcasted_iota(jnp.int32, (n, 1), 0)
    for b in range(2 * TP):
        t = b % TP
        same = rim_in[b].astype(F32)[8:]
        prev = jnp.zeros_like(same) if t == 0 else rim_in[b - 1].astype(F32)[8:]
        head = jnp.where(c.g == 0, prev, same)
        rim[b] = head
        ext[b % 2, pl.ds(0, 8), :] = head
        ext[b % 2, pl.ds(8, n), :] = ci[b].astype(F32)
        cv = chan[4:5] + chan[0:1] * ext[b % 2, pl.ds(8, n), :] + chan[1:2] * ext[b % 2, pl.ds(7, n), :]
        cv = cv + chan[2:3] * ext[b % 2, pl.ds(6, n), :] + chan[3:4] * ext[b % 2, pl.ds(5, n), :]
        low = cv.astype(BF)
        rows = pl.ds(b * n, n)
        conv[rows, :] = low
        cv = low.astype(F32)
        gv = []
        for k in range(2):
            pre = jnp.concatenate([jnp.dot(low[:, h * 256:(h + 1) * 256], gb[k, h], preferred_element_type=F32) for h in range(2)], axis=1)
            v = jax.nn.sigmoid(pre + chan[5 + k:6 + k])
            gates[k, rows, :] = v
            gv.append(v)
        decay, mult = decay_terms(gv[1], db[...])
        if t == 0:
            mult = jnp.where((row == 0) & (c.g == 0), 1.0, mult)
        lanes_in(a_ref, rows, decay)
        lanes_in(d_ref, rows, cv * gv[0] * mult)

    def step1(r, ph):
        at = pl.ds(r, 2 * TP, stride=n)
        return [(p * av, h * av + dv) for (p, h), av, dv in zip(ph, each(a_ref, at), each(d_ref, at))]

    one = jnp.ones((2 * TP, 128), F32)
    ph = lax.fori_loop(0, n, step1, [(one, 0.0 * one)] * (width // 128), unroll=8)
    p = jnp.concatenate([v[0] for v in ph], axis=1)
    h = jnp.concatenate([v[1] for v in ph], axis=1)
    table[c.g, 0] = p
    table[c.g, 1] = h
    sh = share(c, table)
    next(sh)
    for f in g0:
        next(f)
    finish(sh)
    cin = entering(c, lambda g: table[g, 0], lambda g: table[g, 1], width, False)
    carry[...] = cin

    def step2(r, hs):
        at = pl.ds(r, 2 * TP, stride=n)
        hs = [h * av + dv for h, av, dv in zip(hs, each(a_ref, at), each(d_ref, at))]
        for q, h in enumerate(hs):
            d_ref[q, at, :] = h
        return hs

    lax.fori_loop(0, n, step2, split(cin), unroll=8)
    for b in range(2 * TP):
        rows = pl.ds(b * n, n)
        v = lanes_out(d_ref, rows)
        state[rows, :] = v
        mixed[rows, :] = (v * gelu_pair(br0[rows, :])[0]).astype(BF)
    run(*g0, z0)
    pl.when(outer(c.t))(lambda: fill.wait())
    pl.when(idle)(lambda: [f.wait() for f in fills] and None)


def mix_fwd_call(na, wb0, wb1, gb, chan, db, wop, m0):
    ng = lax.axis_size("dp") // TP
    rows, width = na.shape[0], wb0.shape[1]
    n = rows // (2 * TP)
    r = m0.shape[0]
    _, big, small = cut(m0.shape[1], 0)
    S = jax.ShapeDtypeStruct
    return call(
        mix_fwd_kernel,
        (S((rows, width), BF), S((rows, width), BF), S((2, rows, width), F32), S((rows, width), F32),
         S((2 * TP, 8, width), F32), S((2 * TP, width), F32), S((ng, 2, 2 * TP, width), F32), S((rows, width), F32), S((2 * TP, n, width), BF), S((TP, ng, r, width), BF), S((TP, r, big), BF)),
        [VM] * 6 + [HBM, HBM, VM, VM],
        (VM,) * 9 + (HBM, HBM),
        [pltpu.VMEM((width // 128, rows, 128), F32), pltpu.VMEM((width // 128, rows, 128), F32), pltpu.VMEM((2, n + 8, width), F32), pltpu.VMEM((2 * TP, 16, width), BF)],
        5, 128,
    )(na, wb0, wb1, gb, chan, db[None], wop, m0, jnp.zeros((TP, r, big - small), BF), jnp.zeros((TP, r, 256), BF))


def mix_bwd_kernel(gmo, wo, br0, ci, gb, chan, db, conv, gates, state, rim, carry, table, r1, r2, gbr, ggb, sums, o1, o2,
                   gm, a_ref, adj, gc, gpl, ext, heads, etab, rim_in, send, recv):
    c = Comm(send, recv)
    greet(plane_partners(c) + line_partners(c))
    n, width = ci.shape[1], ci.shape[2]
    zs = [spread_z(c, *units_back(lambda t, rr=rr: rr.at[t], oo)) for rr, oo in ((r1, o1), (r2, o2))]
    step(*zs)
    def product(i, _):
        rows = pl.ds(pl.multiple_of(i * 2 * n, 2 * n), 2 * n)
        gm[rows, :] = jnp.dot(gmo[rows, :], wo[...], preferred_element_type=F32)
        return 0

    lax.fori_loop(0, TP, product, 0)
    for b in range(2 * TP):
        rows = pl.ds(b * n, n)
        act, slope = gelu_pair(br0[rows, :])
        g = gm[rows, :]
        lanes_in(adj, rows, g * act)
        gbr[0, rows, :] = (g * state[rows, :] * slope).astype(BF)
        lanes_in(a_ref, rows, jnp.exp(-8.0 * gates[1, rows, :] * db[...]))

    def step1(i, es):
        at = pl.ds(n - 1 - i, 2 * TP, stride=n)
        return [(v + e) * av for v, e, av in zip(each(adj, at), es, each(a_ref, at))]

    e = lax.fori_loop(0, n, step1, [jnp.zeros((2 * TP, 128), F32)] * (width // 128), unroll=8)
    e = jnp.concatenate(e, axis=1)
    etab[c.g] = e
    sh = share(c, etab)
    next(sh)
    finish(sh)
    ein = entering(c, lambda g: table[g, 0], lambda g: etab[g], width, True)

    def step2(i, es):
        at = pl.ds(n - 1 - i, 2 * TP, stride=n)
        vs = [v + e for v, e in zip(each(adj, at), es)]
        for q, v in enumerate(vs):
            adj[q, at, :] = v
        return [v * av for v, av in zip(vs, each(a_ref, at))]

    lax.fori_loop(0, n, step2, split(ein), unroll=8)
    row = lax.broadcasted_iota(jnp.int32, (n, 1), 0)
    total = [jnp.zeros((1, width), F32) for _ in range(8)]
    for b in range(2 * TP):
        rows = pl.ds(b * n, n)
        first = (row == 0) & (c.g == 0) if b % TP == 0 else None
        ad = lanes_out(adj, rows)
        gx, ga = gates[0, rows, :], gates[1, rows, :]
        decay, root = decay_terms(ga, db[...])
        mult = root if first is None else jnp.where(first, 1.0, root)
        cv = conv[rows, :].astype(F32)
        before = jnp.where(row == 0, carry[b:b + 1, :], pltpu.roll(state[rows, :], 1, 0))
        gmult = -(ad * cv * gx) * (decay * decay) / root
        if first is not None:
            gmult = jnp.where(first, 0.0, gmult)
        glog = ad * before * decay + gmult
        total[7] = total[7] + jnp.sum(glog * (-8.0 * ga), axis=0, keepdims=True)
        pre = [ad * cv * mult * gx * (1.0 - gx), glog * (-8.0 * db[...]) * ga * (1.0 - ga)]
        conved = ad * gx * mult
        for k in range(2):
            total[5 + k] = total[5 + k] + jnp.sum(pre[k], axis=0, keepdims=True)
            low = pre[k].astype(BF)
            gpl[k, rows, :] = low
            conved = conved + jnp.concatenate([
                lax.dot_general(low[:, h * 256:(h + 1) * 256], gb[k, h], (((1,), (1,)), ((), ())), preferred_element_type=F32)
                for h in range(2)], axis=1)
        gc[b, pl.ds(0, n), :] = conved
        heads[b] = conved[:8]
        ext[b % 2, pl.ds(0, 8), :] = rim[b]
        ext[b % 2, pl.ds(8, n), :] = ci[b].astype(F32)
        for k in range(4):
            total[k] = total[k] + jnp.sum(conved * ext[b % 2, pl.ds(8 - k, n), :], axis=0, keepdims=True)
        total[4] = total[4] + jnp.sum(conved, axis=0, keepdims=True)
    rslot = c.slot()
    out = c.to(heads, rim_in, c.at(g=(c.g + c.ng - 1) % c.ng), rslot)
    out.start()
    sums[...] = jnp.concatenate(total, axis=0)
    for k in range(2):
        for h in range(2):
            ggb[k, h] = lax.dot_general(conv[:, h * 256:(h + 1) * 256], gpl[k, :, h * 256:(h + 1) * 256], (((0,), (0,)), ((), ())), preferred_element_type=F32)
    out.wait()
    for b in range(2 * TP):
        rows = pl.ds(b * n, n)
        same = rim_in[b]
        nxt = jnp.zeros_like(same) if b % TP == TP - 1 else rim_in[b + 1]
        gc[b, pl.ds(n, 8), :] = jnp.where(c.g == c.ng - 1, nxt, same)
        v = chan[0:1] * gc[b, pl.ds(0, n), :]
        for k in range(1, 4):
            v = v + chan[k:k + 1] * gc[b, pl.ds(k, n), :]
        gbr[1, rows, :] = v.astype(BF)
    run(*zs)


def mix_bwd_call(gmo, wo, br0, ci, gb, chan, db, saved, r1, r2, units):
    ng = lax.axis_size("dp") // TP
    rows, width = br0.shape
    n = rows // (2 * TP)
    r = r1.shape[1]
    S = jax.ShapeDtypeStruct
    V = pltpu.VMEM
    return call(
        mix_bwd_kernel,
        (S((2, rows, width), BF), S((2, 2, 256, 256), F32), S((8, width), F32), S((r, units), BF), S((r, units), BF)),
        [VM] * 13 + [HBM] * 2,
        (VM,) * 3 + (HBM,) * 2,
        [V((rows, width), F32), V((width // 128, rows, 128), F32), V((width // 128, rows, 128), F32), V((2 * TP, n + 8, width), F32), V((2, rows, width), BF),
         V((2, n + 8, width), F32), V((2 * TP, 8, width), F32), V((ng, 2 * TP, width), F32), V((2 * TP, 8, width), F32)],
        6, 128,
    )(gmo, wo, br0, ci, gb, chan, db[None], *saved, r1, r2)


def mlp_kernel(nb, go, w0, w1, w2, hidden, gg0, gg1, part, gnb, v0, v1, v2, sems):
    copies = [pltpu.make_async_copy(a, b, sems.at[k]) for k, (a, b) in enumerate(((w0, v0), (w1, v1), (w2, v2)))]
    begin = pl.program_id(0) == 0

    @pl.when(begin)
    def _():
        for copy in copies:
            copy.start()

    def ready(k):
        pl.when(begin)(lambda: copies[k].wait())

    def back(a, w):
        return lax.dot_general(a, w, (((1,), (1,)), ((), ())), preferred_element_type=F32)

    ready(0)
    first = jnp.dot(nb[...], v0[...], preferred_element_type=F32)
    ready(1)
    second = jnp.dot(nb[...], v1[...], preferred_element_type=F32)
    act, slope = gelu_pair(first)
    low = (act * second).astype(BF)
    hidden[...] = low
    ready(2)
    gh = jnp.dot(go[...], v2[...], preferred_element_type=F32)
    a, b = (gh * second * slope).astype(BF), (gh * act).astype(BF)
    gg0[...] = a
    gg1[...] = b
    gnb[...] = (back(a, v0[...]) + back(b, v1[...])).astype(BF)
    part[...] = back(low, v2[...]).astype(BF)


def mlp_call(nb, go, w0, w1, w2):
    rows, d = nb.shape
    fs = w0.shape[1]
    n = 256
    S = jax.ShapeDtypeStruct
    wide = pl.BlockSpec((n, d), lambda i: (i, 0))
    slim = pl.BlockSpec((n, fs), lambda i: (i, 0))
    return pl.pallas_call(
        mlp_kernel,
        grid=(rows // n,),
        out_shape=(S((rows, fs), BF),) * 3 + (S((rows, d), BF),) * 2,
        in_specs=[wide, wide, HBM, HBM, HBM],
        out_specs=(slim,) * 3 + (wide,) * 2,
        scratch_shapes=[pltpu.VMEM((d, fs), BF)] * 3 + [pltpu.SemaphoreType.DMA((3,))],
        compiler_params=pltpu.CompilerParams(vmem_limit_bytes=VMEM_LIMIT),
    )(nb, go, w0, w1, w2)


def dot(a, b, ca, cb):
    return lax.dot_general(a, b, (((ca,), (cb,)), ((), ())), preferred_element_type=F32)


def body(block_input, lengths, norm_gains, w_branch, channel_params, gate_blocks, decay_param, w_out, w_mlp, w_down, out_grad):
    ndp, ng, t, g = plan()
    dp, mp = lax.axis_index("dp"), lax.axis_index("mp")
    rows, width = block_input.shape[1:]
    r, gr, units = w_branch.shape[1], gate_blocks.shape[2], w_mlp.shape[2]
    fs = cut(units, 0)[1]
    chan = heads_of(channel_params, 1)
    dpar = heads_of(decay_param[None], 1)[0]
    decay_base = jax.nn.softplus(dpar)
    pos = dp * 2 * rows + mp * rows + jnp.arange(rows, dtype=jnp.int32)
    valid = (pos[None] < lengths[:, None])[..., None]
    x = block_input
    grad_own = jnp.where(valid, out_grad, jnp.zeros_like(out_grad))
    na, wb0, wb1, wop, gb = start_call(x, norm_gains[0], w_branch, w_out.T, gate_blocks)
    na = na.reshape(-1, width)
    wb0, wb1 = wb0.reshape(width, 512), wb1.reshape(width, 512)
    gb = gb.reshape(2, 2, 256, 256)
    mixed, *saved, branch0, conv_input, wo, p0 = mix_fwd_call(na, wb0, wb1, gb, chan, decay_base, wop, w_mlp[0])
    wo = wo.reshape(width, 512)
    residual, nb, go, w0, w1, wd = mid_call(mixed, wo, x, grad_own, norm_gains[1], p0, w_mlp[1], w_down.T)
    nb, go = nb.reshape(-1, width), go.reshape(-1, width)
    w0, w1, wd = w0.reshape(width, fs), w1.reshape(width, fs), wd.reshape(width, fs)
    hidden, gg0, gg1, mlp_part, gnb = mlp_call(nb, go, w0, w1, wd)
    gres, gain_b, mlp_own, gmo, o0, r1, r2 = back_call(gnb, mlp_part, residual, grad_own, norm_gains[1], nb, go, gg0, gg1, hidden, ng, r, units)
    out = jnp.where(valid, residual + mlp_own, 0.0).astype(BF)
    gmo = gmo.reshape(-1, width)
    gbr, ggb, chan_rows, o1, o2 = mix_bwd_call(gmo, wo, branch0, conv_input, gb, chan, decay_base, saved, r1, r2, units)
    gin, gains, gchan, gdec, owb, owo, ogb = end_call(
        wb0, wb1, x, gres, norm_gains[0], na, gbr, gmo, mixed, ggb.astype(BF).reshape(2, 2, TP, ng, gr, 256), gain_b, chan_rows, r,
    )
    g_wb, g_wo, g_gb = owb.astype(F32), owo.astype(F32).T, ogb.astype(F32)
    g_wm, g_wd = jnp.stack([o0, o1]).astype(F32), o2.astype(F32).T
    return out, gin, gains.reshape(2, width), g_wb, gchan, g_gb, gdec[0] * jax.nn.sigmoid(decay_param), g_wo, g_wm, g_wd


def solution(mesh):
    return jax.shard_map(
        body,
        mesh=mesh,
        in_specs=(P(None, ("dp", "mp"), None), P(), P(), P(None, "dp", "mp"), P(None, "mp"), P(None, "mp", "dp", None), P("mp"), P("mp", "dp"), P(None, "dp", "mp"), P("mp", "dp"), P(None, ("dp", "mp"), None)),
        out_specs=(P(None, ("dp", "mp"), None), P(None, ("dp", "mp"), None), P(), P(None, "dp", "mp"), P(None, "mp"), P(None, "mp", "dp", None), P("mp"), P("mp", "dp"), P(None, "dp", "mp"), P("mp", "dp")),
        check_vma=False,
    )
```

```python
import functools

import jax
import jax.numpy as jnp
from jax import lax
from jax.experimental import pallas as pl
from jax.experimental.pallas import tpu as pltpu
from jax.sharding import PartitionSpec as P

MESH = pl.DeviceIdType.MESH
VMEM_LIMIT = 60 * 1024 * 1024


EPS = 1e-06
TP = 4
BF = jnp.bfloat16
F32 = jnp.float32


def plan():
    ndp = lax.axis_size("dp")
    ng = ndp // TP
    dp = lax.axis_index("dp")
    return ndp, ng, dp // ng, dp % ng


class Comm:
    def __init__(self, send, recv):
        self.send, self.recv, self.n = send, recv, 0
        self.ndp = lax.axis_size("dp")
        self.ng = self.ndp // TP
        dp = lax.axis_index("dp")
        self.t, self.g, self.m = dp // self.ng, dp % self.ng, lax.axis_index("mp")
        self.bits = [1 << k for k in range(self.ng.bit_length() - 1)]

    def at(self, t=None, g=None, m=None):
        t = self.t if t is None else t
        g = self.g if g is None else g
        return (t * self.ng + g, self.m if m is None else m)

    def fifth(self, t=None):
        return (self.t if t is None else t) == 1 + self.m

    def flip(self, g, b):
        return g + b - 2 * b * ((g // b) % 2)

    def barrier(self):
        sem = pltpu.get_barrier_semaphore()
        partners = [self.at(t=(self.t + o) % TP) for o in range(1, TP)]
        partners += [self.at(g=self.flip(self.g, b)) for b in self.bits] + [self.at(m=1 - self.m)]
        for p in partners:
            pl.semaphore_signal(sem, inc=1, device_id=p, device_id_type=MESH)
        pl.semaphore_wait(sem, len(partners))

    def slot(self):
        self.n += 1
        return self.n - 1

    def to(self, src, dst, dev, slot):
        return pltpu.make_async_remote_copy(
            src_ref=src, dst_ref=dst, send_sem=self.send.at[slot], recv_sem=self.recv.at[slot],
            device_id=dev, device_id_type=MESH,
        )

    def local(self, src, dst, slot):
        return pltpu.make_async_copy(src, dst, self.send.at[slot])


def finish(*flows):
    for f in flows:
        for _ in f:
            pass


def step(*flows):
    for f in flows:
        next(f)


def run(*flows):
    flows = list(flows)
    while flows:
        for f in list(flows):
            try:
                next(f)
            except StopIteration:
                flows.remove(f)


def ag_flow(c, own, full, late=False):
    t, m = c.t, c.m
    sib = c.at(m=1 - m)

    def slots():
        return [[c.slot() for _ in range(2)] for _ in range(TP - 1)]

    up, down, d2u, d2d = slots(), slots(), slots(), slots()
    d2o, loc = [c.slot() for _ in range(2)], [c.slot() for _ in range(2)]

    def row(b, s, mm):
        return full.at[s, b, mm]

    def up_copy(k, s):
        b = t - k
        return c.to(own.at[s] if k == 0 else row(b, s, m), row(b, s, m), c.at(t=t + 1), up[k][s])

    def down_copy(k, s):
        b = t + k
        return c.to(own.at[s] if k == 0 else row(b, s, m), row(b, s, m), c.at(t=t - 1), down[k][s])

    def side(b, slot, s, src=None):
        return c.to(row(b, s, m) if src is None else src, row(b, s, m), sib, slot)

    def got(b, slot, s, mm):
        return c.to(row(b, s, mm), row(b, s, mm), sib, slot)

    def both(f):
        return lambda: [f(s) for s in range(2)] and None

    pl.when((t < TP - 1) & (t > 0) if late else t < TP - 1)(both(lambda s: up_copy(0, s).start()))
    pl.when((t > 0) & (t < TP - 1) if late else t > 0)(both(lambda s: down_copy(0, s).start()))
    for s in range(2):
        side(t, d2o[s], s, own.at[s]).start()
        c.local(own.at[s], row(t, s, m), loc[s]).start()
    yield
    if late:
        pl.when(t == 0)(both(lambda s: up_copy(0, s).start()))
        pl.when(t == TP - 1)(both(lambda s: down_copy(0, s).start()))
        yield
    for k in range(TP - 1):
        def from_below(s):
            got(t - 1 - k, up[k][s], s, m).wait_recv()
            if k < TP - 2:
                pl.when(t < TP - 1)(lambda: up_copy(k + 1, s).start())
            side(t - 1 - k, d2u[k][s], s).start()

        def from_above(s):
            got(t + 1 + k, down[k][s], s, m).wait_recv()
            if k < TP - 2:
                pl.when(t > 0)(lambda: down_copy(k + 1, s).start())
            side(t + 1 + k, d2d[k][s], s).start()

        for s in range(2):
            pl.when(t - 1 - k >= 0)(lambda: from_below(s))
            pl.when(t + 1 + k < TP)(lambda: from_above(s))
        yield
    for s in range(2):
        c.local(own.at[s], row(t, s, m), loc[s]).wait()
        side(t, d2o[s], s, own.at[s]).wait_send()
        got(t, d2o[s], s, 1 - m).wait_recv()
    for k in range(TP - 1):
        pl.when((t < TP - 1) & (t - k >= 0))(both(lambda s: up_copy(k, s).wait_send()))
        pl.when((t > 0) & (t + k < TP))(both(lambda s: down_copy(k, s).wait_send()))

        def below(s):
            side(t - 1 - k, d2u[k][s], s).wait_send()
            got(t - 1 - k, d2u[k][s], s, 1 - m).wait_recv()

        def above(s):
            side(t + 1 + k, d2d[k][s], s).wait_send()
            got(t + 1 + k, d2d[k][s], s, 1 - m).wait_recv()

        pl.when(t - 1 - k >= 0)(both(below))
        pl.when(t + 1 + k < TP)(both(above))


def rs_scratch(rows, width, made=False):
    return [
        pltpu.VMEM((1 if made else 2, 2, TP, rows, width), BF),
        pltpu.VMEM((2, TP - 1, 2, rows, width), BF),
        pltpu.VMEM((TP - 1, 2, rows, width), BF),
    ]


def rs_flow(c, part, out, pair, inbox, outbox, make=None):
    t, m = c.t, c.m
    n = part.shape[3]
    other = c.at(m=1 - m)
    lower = t < TP // 2
    u = jnp.where(lower, t, TP - 1 - t)
    da = jnp.where(lower, 0, 1)
    hop = 1 - 2 * da
    near = [[c.slot() for _ in range(2)] for _ in range(TP)]
    here = [[c.slot() for _ in range(2)] for _ in range(TP)]
    sib = pair.at[pair.shape[0] - 1]
    own = (lambda s, b: part.at[s, b, m]) if make else (lambda s, b: pair.at[0, s, b])
    base = c.n
    for _ in range(4 * (TP - 1)):
        c.slot()

    def real(d):
        return jnp.where(lower, d, TP - 1 - d)

    def cross(d, s):
        return c.to(part.at[s, real(d), 1 - m], sib.at[s, real(d)], other, near[d][s])

    def load(d, s):
        return c.local(part.at[s, real(d), m], own(s, real(d)), here[d][s])

    def near_in(d, s):
        cross(d, s).wait_recv()
        if make is None:
            load(d, s).wait()

    def msg(flow, j, s):
        way = da if flow == 0 else 1 - da
        dev = c.at(t=t + hop if flow == 0 else t - hop)
        return c.to(outbox.at[j if flow == 0 else 2, s], inbox.at[way, j, s], dev, base + (way * (TP - 1) + j) * 2 + s)

    def add(d, s, into, terms):
        b = real(d)

        def rows16(i, _):
            sl = pl.ds(pl.multiple_of(i * 16, 16), 16)
            v = own(s, b)[sl, :].astype(F32) + sib[s, b, sl, :].astype(F32)
            for way, j in terms:
                v = v + inbox[way, j, s, sl, :].astype(F32)
            into(s, sl, v)
            return 0

        lax.fori_loop(0, n // 16, rows16, 0)

    def put(j):
        def into(s, sl, v):
            outbox[j, s, sl, :] = v.astype(BF)
        return into

    def final(s, sl, v):
        out[s, sl, :] = v

    def issue(d):
        if make is not None:
            b = real(d)
            rows = [pl.ds(pl.multiple_of((s * TP + b) * 2 * n, 2 * n), 2 * n) for s in range(2)]
            v = make(rows).astype(BF).reshape(2, 2, n, part.shape[4])
            for s in range(2):
                part[s, b] = v[s]
        for s in range(2):
            if make is None:
                load(d, s).start()
            cross(d, s).start()

    def send_out(d, j):
        for s in range(2):
            near_in(d, s)
            add(d, s, put(j), [])
            msg(0, j, s).start()

    issue(3)
    issue(2)
    yield
    pl.when(u == 0)(lambda: send_out(3, 0))
    issue(1)
    pl.when(u == 0)(lambda: send_out(2, 1))
    issue(0)
    pl.when(u == 0)(lambda: send_out(1, 2))
    yield
    for d, j in ((3, 0), (2, 1)):
        def pass_on():
            for s in range(2):
                near_in(d, s)
                msg(0, j, s).wait_recv()
                add(d, s, put(j), [(da, j)])
                msg(0, j, s).start()

        pl.when(u == 1)(pass_on)
        yield

    def back():
        for s in range(2):
            near_in(0, s)
            msg(1, 0, s).wait_recv()
            add(0, s, put(2), [(1 - da, 0)])
            msg(1, 0, s).start()

    pl.when(u == 1)(back)
    yield
    for s in range(2):
        def end0():
            near_in(0, s)
            msg(1, 0, s).wait_recv()
            add(0, s, final, [(1 - da, 0)])

        def end1():
            near_in(1, s)
            msg(0, 2, s).wait_recv()
            msg(1, 1, s).wait_recv()
            add(1, s, final, [(da, 2), (1 - da, 1)])

        pl.when(u == 0)(end0)
        pl.when(u == 1)(end1)
    for s in range(2):
        for d in range(TP):
            cross(d, s).wait_send()
        for j in range(2):
            msg(0, j, s).wait_send()
        pl.when(u == 0)(lambda: msg(0, 2, s).wait_send())
        pl.when(u == 1)(lambda: msg(1, 0, s).wait_send())


def inner(t):
    return (t == 1) | (t == 2)


def outer(t):
    return (t == 0) | (t == TP - 1)


def cut(width, t):
    tiles = width // 128
    big = -(-tiles // TP)
    small = (tiles - 2 * big) // 2
    return pl.multiple_of((small * t + (big - small) * (t > 1) * (t - 1)) * 128, 128), big * 128, small * 128


def spread_z(c, src, dst, kinds=((None, 0),), owner="to"):
    slots = [c.slot() for _ in range(TP)]

    def each_kind(sender, taker, f):
        own = taker if owner == "to" else sender
        for which, k in kinds:
            if which is None:
                f(k)
            else:
                pl.when(which(own))(functools.partial(f, k))

    def copy(o, k):
        to = (c.t + o) % TP
        return c.to(src(to, k), dst(c.t, k), c.at(t=to), slots[o])

    def back(o, k):
        frm = (c.t + TP - o) % TP
        return c.to(dst(frm, k), dst(frm, k), c.at(t=frm), slots[o])

    for o in range(1, TP):
        each_kind(c.t, (c.t + o) % TP, lambda k: copy(o, k).start())
    each_kind(c.t, c.t, lambda k: c.local(src(c.t, k), dst(c.t, k), slots[0]).start())
    yield
    each_kind(c.t, c.t, lambda k: c.local(src(c.t, k), dst(c.t, k), slots[0]).wait())
    for o in range(1, TP):
        each_kind((c.t + TP - o) % TP, c.t, lambda k: back(o, k).wait_recv())
    yield
    for o in range(1, TP):
        each_kind(c.t, (c.t + o) % TP, lambda k: copy(o, k).wait_send())


def only(cond, f):
    if cond is None:
        f()
    else:
        pl.when(cond)(f)


def plane_gather(c, block, order, own=None, cond=None):
    have = [0]
    done = []
    held = None
    if own is not None:
        held = c.local(own, block(c.g), c.slot())
        only(cond, lambda: held.start())
    for b in order:
        dev = c.at(g=c.flip(c.g, b))
        sent = []
        for x in have:
            gg = c.g
            for bit in c.bits:
                if x & bit:
                    gg = c.flip(gg, bit)
            src = own if own is not None and x == 0 else block(gg)
            sent.append(c.to(src, block(gg), dev, c.slot()))
        only(cond, lambda: [copy.start() for copy in sent] and None)
        yield
        only(cond, lambda: [copy.wait_recv() for copy in sent] and None)
        done += sent
        have = have + [x ^ b for x in have]
    only(cond, lambda: [copy.wait_send() for copy in done] and None)
    if held is not None:
        only(cond, lambda: held.wait())


def plane_reduce(c, own, sums, inbox, order, cond=None):
    def place(x):
        gg = c.g
        for bit in c.bits:
            if x & bit:
                gg = c.flip(gg, bit)
        return gg

    left = list(range(c.ng))
    spot = {}
    done = []
    base = 0
    for k, b in enumerate(order):
        dev = c.at(g=c.flip(c.g, b))
        away = [x for x in left if x & b]
        left = [x for x in left if not x & b]
        if k == 0:
            spot = {x: i for i, x in enumerate(left)}
        sent = [c.to(own(place(x)) if k == 0 else sums.at[spot[x]], inbox.at[base + i], dev, c.slot()) for i, x in enumerate(away)]
        held = [c.local(own(place(x)), sums.at[spot[x]], c.slot()) for x in left] if k == 0 else []

        def begin():
            for copy in sent + held:
                copy.start()

        only(cond, begin)
        yield

        def take():
            for i, x in enumerate(left):
                sent[i].wait_recv()
                if k == 0:
                    held[i].wait()
                add_blocks(sums.at[spot[x]], inbox.at[base + i])

        only(cond, take)
        base += len(away)
        done += sent
    only(cond, lambda: [copy.wait_send() for copy in done] and None)


def add_blocks(a, b):
    def one(i, _):
        a[i] = a[i] + b[i]
        return 0

    lax.fori_loop(0, a.shape[0], one, 0)


def grad_flow(c, lhs, rhs, out, rbuf, lbuf, stage, halves):
    wide = lbuf.shape[2]
    _, ng, r, cols = stage.shape
    load = c.local(rhs, rbuf, c.slot())
    load.start()
    pieces = [c.local(lhs.at[:, pl.ds(k * wide, wide)], lbuf.at[k % 2], c.slot()) for k in range(TP)]
    puts = [c.local(stage.at[k % 2], out.at[k], c.slot()) for k in range(TP)]
    pieces[0].start()
    pieces[1].start()
    load.wait()
    for k in range(TP):
        pieces[k].wait()
        v = lax.dot_general(lbuf[k % 2], rbuf[...], (((0,), (0,)), ((), ())), preferred_element_type=F32)
        if k + 2 < TP:
            pieces[k + 2].start()
        stage[k % 2] = v.astype(BF).reshape(ng, r, cols)
        puts[k].start()
        if k % 2:
            puts[k - 1].wait()
            puts[k].wait()
            step(*halves[k // 2])
            yield


def call(kernel, out_shape, in_specs, out_specs, scratch, cid, slots=160):
    return pl.pallas_call(
        kernel,
        out_shape=out_shape,
        in_specs=in_specs,
        out_specs=out_specs,
        scratch_shapes=list(scratch) + [pltpu.SemaphoreType.DMA((slots,)), pltpu.SemaphoreType.DMA((slots,))],
        compiler_params=pltpu.CompilerParams(collective_id=cid, has_side_effects=True, vmem_limit_bytes=VMEM_LIMIT),
    )


HBM = pl.BlockSpec(memory_space=pl.ANY)
VM = pl.BlockSpec(memory_space=pltpu.VMEM)


def heads_to(c, ref, dst, extra):
    def src(t, k):
        return ref.at[:, pl.ds(1024, 256)] if extra else ref.at[:, pl.ds(pl.multiple_of(t * 256, 256), 256)]

    def into(t, k):
        return dst(t).at[:, pl.ds(256 if extra else 0, 256)]

    return src, into, (((c.fifth, 0),) if extra else ((None, 0),))


def units_to(ref, dst):
    width = ref.shape[1]
    _, big, small = cut(width, 0)

    def src(t, k):
        return ref.at[:, pl.ds(cut(width, t)[0], k)]

    def into(t, k):
        return dst(t).at[:, pl.ds(0, k)]

    return src, into, ((inner, big), (outer, small))


def units_back(ref, dst):
    width = dst.shape[1]
    _, big, small = cut(width, 0)

    def src(t, k):
        return ref(t).at[:, pl.ds(0, k)]

    def into(t, k):
        return dst.at[:, pl.ds(cut(width, t)[0], k)]

    return src, into, ((inner, big), (outer, small)), "from"


def heads_out(c, ref, dst, extra):
    def src(t, k):
        return ref(t).at[:, pl.ds(256 if extra else 0, 256)]

    def into(t, k):
        return dst.at[:, pl.ds(1024, 256)] if extra else dst.at[:, pl.ds(pl.multiple_of(t * 256, 256), 256)]

    return src, into, (((c.fifth, 0),) if extra else ((None, 0),)), "from"


START_ORDER = "azgagaw"


def start_kernel(x, gain, wbr, wot, gates, full_a, wb0, wb1, wop, gb, own, zero, send, recv):
    c = Comm(send, recv)
    c.barrier()
    wb = (wb0, wb1)
    z = []
    for extra in (False, True):
        for k in range(2):
            z.append(spread_z(c, *heads_to(c, wbr.at[k], lambda t, k=k: wb[k].at[t, c.g], extra)))
    z.append(spread_z(c, lambda t, k: gates.at[:, t], lambda t, k: gb.at[:, 0, t, c.g]))
    z.append(spread_z(c, lambda t, k: gates.at[:, 4], lambda t, k: gb.at[:, 1, t, c.g], ((c.fifth, 0),)))
    for f in z:
        next(f)
    for s in range(2):
        v = x[s].astype(F32)
        own[s] = (v * lax.rsqrt(jnp.mean(v * v, axis=-1, keepdims=True) + EPS) * gain[...]).astype(BF)
    zero[...] = jnp.zeros_like(zero)
    fills = [(zero, wb[k].at[:, g, :, pl.ds(256, 256)], c.slot()) for k in range(2) for g in range(c.ng)]
    fills += [(zero.at[:, pl.ds(0, gates.shape[2])], gb.at[k, 1, :, g], c.slot()) for k in range(2) for g in range(c.ng)]
    idle = jnp.logical_not(c.fifth())
    pl.when(idle)(lambda: [c.local(*f).start() for f in fills] and None)
    fwd, rev = c.bits, c.bits[::-1]
    g1 = []
    for h in range(2):
        for k, order in ((0, fwd), (1, rev)):
            g1.append(plane_gather(c, lambda g, k=k, h=h: wb[k].at[:, g, :, pl.ds(256 * h, 256)], order, None, c.fifth() if h else None))
            g1.append(plane_gather(c, lambda g, k=k, h=h: gb.at[k, h, :, g], order, None, c.fifth() if h else None))
    ag = ag_flow(c, own, full_a)
    z2 = [spread_z(c, *heads_to(c, wot, lambda t: wop.at[t], extra)) for extra in (False, True)]
    does = {"z": lambda: step(*z), "g": lambda: step(*g1), "a": lambda: step(ag), "w": lambda: step(*z2)}
    for what in START_ORDER:
        does[what]()
    run(ag, *g1, *z, *z2)
    pl.when(idle)(lambda: [c.local(*f).wait() for f in fills] and None)


def start_call(x, gain, wbr, wot, gates):
    ng = lax.axis_size("dp") // TP
    _, n, d = x.shape
    r, gr = wbr.shape[1], gates.shape[2]
    S = jax.ShapeDtypeStruct
    return call(
        start_kernel,
        (S((2, TP, 2, n, d), BF), S((TP, ng, r, 512), BF), S((TP, ng, r, 512), BF), S((TP, r, 512), BF), S((2, 2, TP, ng, gr, 256), BF)),
        [VM, VM, HBM, HBM, HBM],
        (HBM,) * 5,
        [pltpu.VMEM((2, n, d), BF), pltpu.VMEM((TP, r, 256), BF)],
        1, 256,
    )(x, gain[None], wbr, wot, gates)


MID_LATE = False
MID_ORDER = "ra0yrr0ary1raNza1z2A2A"


def mid_kernel(mixed, wo, x, go, gain, p0, m1, m2, zero, res, full, full_g, w0, w1, w2, tot, own, part, pair, inbox, outbox, send, recv):
    c = Comm(send, recv)
    c.barrier()
    fwd, rev = c.bits, c.bits[::-1]
    pad = zero.shape[2]
    fills = [(zero, w.at[:, c.g, :, pl.ds(w.shape[3] - pad, pad)], c.slot()) for w in (w1, w2)]

    def gather(w, own=None):
        for k, order in ((0, fwd), (1, rev)):
            at = pl.ds(2 * k, 2)
            yield plane_gather(c, lambda g, at=at: w.at[at, g], order, None if own is None else own.at[at])

    last = len(c.bits) - 1

    def make(rows):
        v = jnp.concatenate([mixed[at, :] for at in rows], axis=0)
        return lax.dot_general(v, wo[...], (((1,), (1,)), ((), ())), preferred_element_type=F32)

    rs = rs_flow(c, part, tot, pair, inbox, outbox, make)
    ag, ag2 = ag_flow(c, own, full), ag_flow(c, go, full_g, MID_LATE)
    z1 = spread_z(c, *units_to(m1, lambda t: w1.at[t, c.g]))
    z2 = spread_z(c, *units_to(m2, lambda t: w2.at[t, c.g]))
    g = [list(gather(w0, p0)), list(gather(w1)), list(gather(w2))]

    def norm():
        finish(rs)
        for s in range(2):
            v = x[s].astype(F32) + tot[s]
            res[s] = v
            own[s] = (v * lax.rsqrt(jnp.mean(v * v, axis=-1, keepdims=True) + EPS) * gain[...]).astype(BF)
        step(ag)

    begun = [0, 0, 0]

    def plane(k):
        if not begun[k]:
            step(*g[k])
        else:
            for _ in range(last):
                step(*g[k])
        begun[k] = 1

    does = {"r": lambda: step(rs), "N": norm, "A": lambda: step(ag), "a": lambda: step(ag2), "y": lambda: step(z1), "z": lambda: step(z2),
            "0": lambda: plane(0), "1": lambda: plane(1), "2": lambda: plane(2)}
    for i, what in enumerate(MID_ORDER):
        does[what]()
        if i == 4:
            pl.when(outer(c.t))(lambda: [c.local(*f).start() for f in fills] and [c.local(*f).wait() for f in fills] and None)
    finish(ag, ag2, *g[0], *g[1], *g[2], z1, z2)


def mid_call(mixed, wo, x, go, gain, p0, m1, m2):
    _, n, d = x.shape
    ng = lax.axis_size("dp") // TP
    _, r, fs = p0.shape
    _, big, small = cut(m1.shape[1], 0)
    zero = jnp.zeros((TP, r, big - small), BF)
    S = jax.ShapeDtypeStruct
    w = S((TP, ng, r, fs), BF)
    return call(
        mid_kernel,
        (S((2, n, d), F32), S((2, TP, 2, n, d), BF), S((2, TP, 2, n, d), BF), w, w, w),
        [VM, VM, VM, VM, VM, HBM, HBM, HBM, VM],
        (VM,) + (HBM,) * 5,
        [pltpu.VMEM((2, n, d), F32), pltpu.VMEM((2, n, d), BF), pltpu.VMEM((2, TP, 2, n, d), BF)] + rs_scratch(n, d, True),
        2,
    )(mixed, wo, x, go, gain[None], p0, m1, m2, zero)


def back_kernel(part, part2, res, go, gain, nb, gall, gg0, gg1, hidden, gres, gsum, mlp_own, full, o0, r1, r2, h0, h1, h2,
                tot, own, pair, inbox, outbox, pair2, inbox2, outbox2, su, ib, rbuf, lbuf, stage, send, recv):
    c = Comm(send, recv)
    c.barrier()
    fwd, rev = c.bits, c.bits[::-1]
    rs = rs_flow(c, part, tot, pair, inbox, outbox)
    next(rs)
    red, grad = [], []
    for k, h in enumerate((h0, h1, h2)):
        red.append([plane_reduce(c, lambda g, h=h, q=q: h.at[pl.ds(2 * q, 2), g], su.at[2 * k + q], ib.at[2 * k + q], (fwd, rev)[q]) for q in range(2)])
        grad.append(grad_flow(c, gall if k == 2 else nb, (gg0, gg1, hidden)[k], h, rbuf, lbuf, stage, [[f] for f in red[k]]))
    last = len(c.bits) - 1

    def onward(parts):
        for _ in range(last):
            step(*parts)

    step(rs)
    step(grad[0])
    step(grad[0])
    step(rs)
    step(grad[1])
    step(rs)
    step(grad[1])
    onward(red[0])
    step(rs)
    rs2 = rs_flow(c, part2, mlp_own, pair2, inbox2, outbox2)
    finish(rs)
    total = jnp.zeros_like(gsum)
    for s in range(2):
        v = res[s]
        scale = lax.rsqrt(jnp.mean(v * v, axis=-1, keepdims=True) + EPS)
        normal = v * scale
        gn = tot[s]
        total = total + jnp.sum(gn * normal, axis=0, keepdims=True)
        q = gn * gain[...]
        gr = scale * (q - normal * jnp.mean(q * normal, axis=-1, keepdims=True)) + go[s].astype(F32)
        gres[s] = gr
        own[s] = gr.astype(BF)
    gsum[...] = total
    ag = ag_flow(c, own, full)
    step(ag, rs2)
    step(rs2)
    step(grad[2])
    step(grad[2])
    finish(*red[0])
    s0 = spread_z(c, *units_back(lambda t: su.at[t // 2, 0, t % 2], o0))
    step(s0)
    onward(red[1])
    step(ag, rs2)
    held = []

    def keep(k, out):
        finish(*red[k])
        for q in range(2):
            held.append(c.local(su.at[2 * k + q, 0], out.at[pl.ds(2 * q, 2)], c.slot()))
            held[-1].start()

    step(ag, rs2)
    onward(red[2])
    keep(1, r1)
    step(rs2)
    finish(ag, rs2)
    keep(2, r2)
    finish(s0, *grad)
    for h in held:
        h.wait()


def back_call(part, part2, res, go, gain, nb, gall, gg0, gg1, hidden, ng, r, units):
    _, n, d = go.shape
    rows, fs = hidden.shape
    S = jax.ShapeDtypeStruct
    shape = (2, TP, 2, n, d)
    h = S((TP, ng, r, fs), BF)
    *outs, _, _, _ = call(
        back_kernel,
        (S((2, n, d), F32), S((1, d), F32), S((2, n, d), F32), S(shape, BF), S((r, units), BF), S((TP, r, fs), BF), S((TP, r, fs), BF), h, h, h),
        [HBM] * 2 + [VM] * 3 + [HBM] * 5,
        (VM, VM, VM) + (HBM,) * 7,
        [pltpu.VMEM((2, n, d), F32), pltpu.VMEM((2, n, d), BF)] + rs_scratch(n, d) + rs_scratch(n, d)
        + [pltpu.VMEM((6, ng // 2, 2, r, fs), BF), pltpu.VMEM((6, ng - 1, 2, r, fs), BF)]
        + [pltpu.VMEM((rows, fs), BF), pltpu.VMEM((2, rows, ng * r), BF), pltpu.VMEM((2, ng, r, fs), BF)],
        3, 256,
    )(part.reshape(shape), part2.reshape(shape), res, go, gain[None], nb, gall, gg0, gg1, hidden)
    return outs


def small_flow(c, small, inbox, zbox):
    for k, b in enumerate(c.bits):
        copy = c.to(small.at[k], inbox.at[k], c.at(g=c.flip(c.g, b)), c.slot())
        copy.start()
        yield
        copy.wait()
        small[k + 1] = small[k] + inbox[k]
    last = len(c.bits)
    z = spread_z(c, lambda t, k: small.at[last], lambda t, k: zbox.at[t])
    next(z)
    yield
    run(z)


def end_kernel(wb0, wb1, gbr, x, gres, gain, na, gsrc, gmo, mixed, ggb, gain_b, chan_rows, gin, gains, gchan, gdec, owb, owo, ogb, gwb0, gwb1, gwo,
               sm_a, in_a, z_a, sm_b, in_b, sbox, z_b, tot, part, pair, inbox, outbox, su_x, in_x, su_g, in_g, rbuf, lbuf, stage, send, recv):
    c = Comm(send, recv)
    c.barrier()
    fwd, rev = c.bits, c.bits[::-1]
    red, gate, every = [], [], []
    for k, gw in enumerate((gwb0, gwb1, gwo)):
        red.append(([], []))
        for h in range(2):
            i, cond = 2 * k + h, c.fifth() if h else None
            lane = (lambda t: pl.ds(1024, 256)) if h else (lambda t: pl.ds(pl.multiple_of(t * 256, 256), 256))
            which = ((c.fifth, 0),) if h else ((None, 0),)
            dst = (lambda t, q, k=k, lane=lane: owb.at[k, :, lane(t)]) if k < 2 else (lambda t, q, lane=lane: owo.at[:, lane(t)])
            flows = []
            for q, order in ((0, fwd), (1, rev)):
                at = pl.ds(2 * q, 2)
                flows.append(plane_reduce(c, lambda g, gw=gw, h=h, at=at: gw.at[at, g, :, pl.ds(256 * h, 256)], su_x.at[i, :, at], in_x.at[i, :, at], order, cond))
                red[k][q].append(flows[q])
            every.append((flows, spread_z(c, lambda t, q, i=i: su_x.at[i, 0, t], dst, which, "from")))
            if k < 2:
                gate.append(plane_reduce(c, lambda g, k=k, h=h: ggb.at[k, h, :, g], su_g.at[i], in_g.at[i], rev if k else fwd, cond))
                every.append((gate[-1:], spread_z(c, lambda t, q, i=i: su_g.at[i, 0, t], lambda t, q, k=k, h=h: ogb.at[k, 4 if h else t], which, "from")))

    def onward(*flows):
        for _ in range(len(c.bits) - 1):
            step(*flows)

    def make(rows):
        v = [jnp.concatenate([gbr[k, at, :] for at in rows], axis=0) for k in range(2)]
        v = [lax.dot_general(v[k], w[...], (((1,), (1,)), ((), ())), preferred_element_type=F32) for k, w in enumerate((wb0, wb1))]
        return v[0] + v[1]

    rs = rs_flow(c, part, tot, pair, inbox, outbox, make)
    next(rs)
    grad = [grad_flow(c, lhs, rhs, gw, rbuf, lbuf, stage, red[k]) for k, (lhs, rhs, gw) in enumerate(((na, gsrc.at[0], gwb0), (na, gsrc.at[1], gwb1), (gmo, mixed, gwo)))]
    step(*gate)
    sm_a[0] = chan_rows[...]
    chan = small_flow(c, sm_a, in_a, z_a)
    step(chan)
    step(rs)
    step(grad[2])
    step(grad[2])
    step(rs)
    step(grad[0])
    step(grad[0])
    step(chan)
    step(rs)
    step(grad[1])
    step(grad[1])
    onward(*red[2][0], *red[2][1], *red[0][0], *red[0][1])
    for _ in c.bits[1:]:
        step(chan)
    step(rs)
    onward(*red[1][0], *red[1][1], *gate)
    for flows, z in every:
        finish(*flows)
        step(z)
    finish(rs)
    total = jnp.zeros_like(gain)
    for s in range(2):
        v = x[s].astype(F32)
        scale = lax.rsqrt(jnp.mean(v * v, axis=-1, keepdims=True) + EPS)
        normal = v * scale
        gn = tot[s]
        total = total + jnp.sum(gn * normal, axis=0, keepdims=True)
        q = gn * gain[...]
        gin[s] = scale * (q - normal * jnp.mean(q * normal, axis=-1, keepdims=True)) + gres[s]
    quarter = sm_b.shape[2]
    for k in range(4):
        sm_b[0, k:k + 1, :] = total[:, k * quarter:(k + 1) * quarter]
        sm_b[0, 4 + k:5 + k, :] = gain_b[:, k * quarter:(k + 1) * quarter]
    finish(small_flow(c, sm_b, in_b, z_b))
    sbox[0] = z_b[0] + z_b[1] + z_b[2] + z_b[3]
    copy = c.to(sbox.at[0], sbox.at[1], c.at(m=1 - c.m), c.slot())
    copy.start()
    finish(chan)
    fifth = z_a[1 + c.m]
    for out, rows in ((gchan, slice(0, 7)), (gdec, slice(7, 8))):
        for t in range(TP):
            out[:, t * 256:(t + 1) * 256] = z_a[t, rows, :256]
        out[:, 1024:] = fifth[rows, 256:]
    copy.wait()
    gains[...] = sbox[0] + sbox[1]
    run(*grad, *[z for _, z in every])


def end_call(wb0, wb1, x, gres, gain, na, gsrc, gmo, mixed, ggb, gain_b, chan_rows, r):
    _, n, d = x.shape
    ng = lax.axis_size("dp") // TP
    gr, steps = ggb.shape[4], (lax.axis_size("dp") // TP).bit_length()
    V = pltpu.VMEM
    S = jax.ShapeDtypeStruct

    def sets(k, rows, width):
        return [pltpu.VMEM((k, ng // 2, TP, rows, width), BF), pltpu.VMEM((k, ng - 1, TP, rows, width), BF)]

    *outs, _, _, _ = call(
        end_kernel,
        (S((2, n, d), F32), S((8, d // 4), F32), S((7, 1280), F32), S((1, 1280), F32), S((2, r, 1280), BF), S((r, 1280), BF), S((2, 5, gr, 256), BF))
        + (S((TP, ng, r, 512), BF),) * 3,
        [VM] * 6 + [HBM] * 4 + [HBM] + [VM] * 2,
        (VM,) * 4 + (HBM,) * 6,
        [V((steps, 8, 512), F32), V((steps - 1, 8, 512), F32), V((TP, 8, 512), F32),
         V((steps, 8, d // 4), F32), V((steps - 1, 8, d // 4), F32), V((2, 8, d // 4), F32), V((TP, 8, d // 4), F32),
         pltpu.VMEM((2, n, d), F32), pltpu.VMEM((2, TP, 2, n, d), BF)] + rs_scratch(n, d, True) + sets(6, r, 256) + sets(4, gr, 256)
        + [pltpu.VMEM((na.shape[0], 512), BF), pltpu.VMEM((2, na.shape[0], ng * r), BF), pltpu.VMEM((2, ng, r, 512), BF)],
        4, 256,
    )(wb0, wb1, gsrc, x, gres, gain[None], na, gsrc, gmo, mixed, ggb, gain_b, chan_rows)
    return outs


def gelu_pair(v):
    k = 0.7978845608028654
    v2 = v * v
    th = jnp.tanh(k * v * (1.0 + 0.044715 * v2))
    half = 0.5 * (1.0 + th)
    return v * half, half + 0.5 * v * (1.0 - th * th) * k * (1.0 + 3.0 * 0.044715 * v2)


def decay_terms(ga, db):
    log_a = -8.0 * ga * db
    y = 2.0 * log_a
    series = 1.0 + y * (1 / 8)
    for k in range(7, 1, -1):
        series = 1.0 + y * (1 / k) * series
    m1 = jnp.where(y > -0.35, y * series, jnp.exp(y) - 1.0)
    return jnp.exp(log_a), jnp.sqrt(-m1)


def lanes_in(ref, rows, v):
    for q in range(ref.shape[0]):
        ref[q, rows, :] = v[:, q * 128:(q + 1) * 128]


def lanes_out(ref, rows):
    return jnp.concatenate([ref[q, rows, :] for q in range(ref.shape[0])], axis=1)


def each(ref, at):
    return [ref[q, at, :] for q in range(ref.shape[0])]


def split(v):
    return [v[:, q * 128:(q + 1) * 128] for q in range(v.shape[1] // 128)]


def plane_partners(c):
    return [c.at(g=(c.g + o) % c.ng) for o in range(1, c.ng)]


def greet(partners):
    sem = pltpu.get_barrier_semaphore()
    for p in partners:
        pl.semaphore_signal(sem, inc=1, device_id=p, device_id_type=MESH)
    pl.semaphore_wait(sem, len(partners))


def line_partners(c):
    return [c.at(t=(c.t + o) % TP) for o in range(1, TP)]


def share(c, table):
    slots = [c.slot() for _ in range(1, c.ng)]
    for o, slot in enumerate(slots, 1):
        c.to(table.at[c.g], table.at[c.g], c.at(g=(c.g + o) % c.ng), slot).start()
    yield
    for o, slot in enumerate(slots, 1):
        frm = (c.g + c.ng - o) % c.ng
        c.to(table.at[frm], table.at[frm], c.at(g=frm), slot).wait_recv()
    for o, slot in enumerate(slots, 1):
        c.to(table.at[c.g], table.at[c.g], c.at(g=(c.g + o) % c.ng), slot).wait_send()


def entering(c, prod, last, width, reverse):
    rows = [None] * (2 * TP)
    spots = [(t, g) for t in range(TP) for g in range(c.ng)]
    for s in range(2):
        cur = jnp.zeros((1, width), F32)
        for t, g in (spots[::-1] if reverse else spots):
            b = s * TP + t
            old = rows[b]
            rows[b] = cur if old is None else jnp.where(c.g == g, cur, old)
            cur = last(g)[b:b + 1] + prod(g)[b:b + 1] * cur
    return jnp.concatenate(rows, axis=0)


def mix_fwd_kernel(na, wb0, wb1, gb, chan_all, db_all, wop, m0, zero, blank, mixed, conv, gates, state, rim, carry, table, br0, ci, chan, db, wo, p0, a_ref, d_ref, ext, rim_in, send, recv):
    c = Comm(send, recv)
    greet(plane_partners(c) + line_partners(c))
    n, width = ci.shape[1], ci.shape[2]
    z0 = spread_z(c, *units_to(m0, lambda t: p0.at[t]))
    next(z0)
    fwd, rev = c.bits, c.bits[::-1]
    g0 = []
    for h in range(2):
        for q, order in ((0, fwd), (1, rev)):
            at, lane = pl.ds(2 * q, 2), pl.ds(256 * h, 256)
            g0.append(plane_gather(c, lambda g, at=at, lane=lane: wo.at[at, g, :, lane], order, wop.at[at, :, lane], c.fifth() if h else None))
    step(*g0)
    fills = [c.local(blank, wo.at[:, g, :, pl.ds(256, 256)], c.slot()) for g in range(c.ng)]
    idle = jnp.logical_not(c.fifth())
    pl.when(idle)(lambda: [f.start() for f in fills] and None)
    pad = zero.shape[2]
    fill = c.local(zero, p0.at[:, :, pl.ds(p0.shape[2] - pad, pad)], c.slot())
    pl.when(outer(c.t))(lambda: fill.start())

    for own, whole, empty in ((chan, chan_all, 0.0), (db, db_all, 1.0)):
        last = whole[:, 1024:]
        own[:, :256] = whole[:, pl.ds(pl.multiple_of(c.t * 256, 256), 256)]
        own[:, 256:] = jnp.where(c.fifth(), last, jnp.full_like(last, empty))

    def branch(i, _):
        rows = pl.ds(pl.multiple_of(i * 2 * n, 2 * n), 2 * n)
        v = jnp.dot(na[rows, :], wb1[...], preferred_element_type=F32).astype(BF)
        ci[2 * i] = v[:n]
        ci[2 * i + 1] = v[n:]
        return 0

    lax.fori_loop(0, TP, branch, 0)
    out = c.to(ci.at[:, pl.ds(n - 16, 16)], rim_in, c.at(g=(c.g + 1) % c.ng), c.slot())
    out.start()

    def gate(i, _):
        rows = pl.ds(pl.multiple_of(i * 2 * n, 2 * n), 2 * n)
        br0[rows, :] = jnp.dot(na[rows, :], wb0[...], preferred_element_type=F32)
        return 0

    lax.fori_loop(0, TP, gate, 0)
    out.wait()
    row = lax.broadcasted_iota(jnp.int32, (n, 1), 0)
    for b in range(2 * TP):
        t = b % TP
        same = rim_in[b].astype(F32)[8:]
        prev = jnp.zeros_like(same) if t == 0 else rim_in[b - 1].astype(F32)[8:]
        head = jnp.where(c.g == 0, prev, same)
        rim[b] = head
        ext[b % 2, pl.ds(0, 8), :] = head
        ext[b % 2, pl.ds(8, n), :] = ci[b].astype(F32)
        cv = chan[4:5] + chan[0:1] * ext[b % 2, pl.ds(8, n), :] + chan[1:2] * ext[b % 2, pl.ds(7, n), :]
        cv = cv + chan[2:3] * ext[b % 2, pl.ds(6, n), :] + chan[3:4] * ext[b % 2, pl.ds(5, n), :]
        low = cv.astype(BF)
        rows = pl.ds(b * n, n)
        conv[rows, :] = low
        cv = low.astype(F32)
        gv = []
        for k in range(2):
            pre = jnp.concatenate([jnp.dot(low[:, h * 256:(h + 1) * 256], gb[k, h], preferred_element_type=F32) for h in range(2)], axis=1)
            v = jax.nn.sigmoid(pre + chan[5 + k:6 + k])
            gates[k, rows, :] = v
            gv.append(v)
        decay, mult = decay_terms(gv[1], db[...])
        if t == 0:
            mult = jnp.where((row == 0) & (c.g == 0), 1.0, mult)
        lanes_in(a_ref, rows, decay)
        lanes_in(d_ref, rows, cv * gv[0] * mult)

    def step1(r, ph):
        at = pl.ds(r, 2 * TP, stride=n)
        return [(p * av, h * av + dv) for (p, h), av, dv in zip(ph, each(a_ref, at), each(d_ref, at))]

    one = jnp.ones((2 * TP, 128), F32)
    ph = lax.fori_loop(0, n, step1, [(one, 0.0 * one)] * (width // 128), unroll=8)
    p = jnp.concatenate([v[0] for v in ph], axis=1)
    h = jnp.concatenate([v[1] for v in ph], axis=1)
    table[c.g, 0] = p
    table[c.g, 1] = h
    sh = share(c, table)
    next(sh)
    for f in g0:
        next(f)
    finish(sh)
    cin = entering(c, lambda g: table[g, 0], lambda g: table[g, 1], width, False)
    carry[...] = cin

    def step2(r, hs):
        at = pl.ds(r, 2 * TP, stride=n)
        hs = [h * av + dv for h, av, dv in zip(hs, each(a_ref, at), each(d_ref, at))]
        for q, h in enumerate(hs):
            d_ref[q, at, :] = h
        return hs

    lax.fori_loop(0, n, step2, split(cin), unroll=8)
    for b in range(2 * TP):
        rows = pl.ds(b * n, n)
        v = lanes_out(d_ref, rows)
        state[rows, :] = v
        mixed[rows, :] = (v * gelu_pair(br0[rows, :])[0]).astype(BF)
    run(*g0, z0)
    pl.when(outer(c.t))(lambda: fill.wait())
    pl.when(idle)(lambda: [f.wait() for f in fills] and None)


def mix_fwd_call(na, wb0, wb1, gb, chan, db, wop, m0):
    ng = lax.axis_size("dp") // TP
    rows, width = na.shape[0], wb0.shape[1]
    n = rows // (2 * TP)
    r = m0.shape[0]
    _, big, small = cut(m0.shape[1], 0)
    S = jax.ShapeDtypeStruct
    return call(
        mix_fwd_kernel,
        (S((rows, width), BF), S((rows, width), BF), S((2, rows, width), F32), S((rows, width), F32),
         S((2 * TP, 8, width), F32), S((2 * TP, width), F32), S((ng, 2, 2 * TP, width), F32), S((rows, width), F32), S((2 * TP, n, width), BF), S((7, width), F32), S((1, width), F32), S((TP, ng, r, width), BF), S((TP, r, big), BF)),
        [VM] * 6 + [HBM, HBM, VM, VM],
        (VM,) * 11 + (HBM, HBM),
        [pltpu.VMEM((width // 128, rows, 128), F32), pltpu.VMEM((width // 128, rows, 128), F32), pltpu.VMEM((2, n + 8, width), F32), pltpu.VMEM((2 * TP, 16, width), BF)],
        5, 128,
    )(na, wb0, wb1, gb, chan, db[None], wop, m0, jnp.zeros((TP, r, big - small), BF), jnp.zeros((TP, r, 256), BF))


def mix_bwd_kernel(gmo, wo, br0, ci, gb, chan, db, conv, gates, state, rim, carry, table, r1, r2, gbr, ggb, sums, o1, o2,
                   gm, a_ref, adj, gc, gpl, ext, heads, etab, rim_in, send, recv):
    c = Comm(send, recv)
    greet(plane_partners(c) + line_partners(c))
    n, width = ci.shape[1], ci.shape[2]
    zs = [spread_z(c, *units_back(lambda t, rr=rr: rr.at[t], oo)) for rr, oo in ((r1, o1), (r2, o2))]
    step(*zs)
    def product(i, _):
        rows = pl.ds(pl.multiple_of(i * 2 * n, 2 * n), 2 * n)
        gm[rows, :] = jnp.dot(gmo[rows, :], wo[...], preferred_element_type=F32)
        return 0

    lax.fori_loop(0, TP, product, 0)
    for b in range(2 * TP):
        rows = pl.ds(b * n, n)
        act, slope = gelu_pair(br0[rows, :])
        g = gm[rows, :]
        lanes_in(adj, rows, g * act)
        gbr[0, rows, :] = (g * state[rows, :] * slope).astype(BF)
        lanes_in(a_ref, rows, jnp.exp(-8.0 * gates[1, rows, :] * db[...]))

    def step1(i, es):
        at = pl.ds(n - 1 - i, 2 * TP, stride=n)
        return [(v + e) * av for v, e, av in zip(each(adj, at), es, each(a_ref, at))]

    e = lax.fori_loop(0, n, step1, [jnp.zeros((2 * TP, 128), F32)] * (width // 128), unroll=8)
    e = jnp.concatenate(e, axis=1)
    etab[c.g] = e
    sh = share(c, etab)
    next(sh)
    finish(sh)
    ein = entering(c, lambda g: table[g, 0], lambda g: etab[g], width, True)

    def step2(i, es):
        at = pl.ds(n - 1 - i, 2 * TP, stride=n)
        vs = [v + e for v, e in zip(each(adj, at), es)]
        for q, v in enumerate(vs):
            adj[q, at, :] = v
        return [v * av for v, av in zip(vs, each(a_ref, at))]

    lax.fori_loop(0, n, step2, split(ein), unroll=8)
    row = lax.broadcasted_iota(jnp.int32, (n, 1), 0)
    total = [jnp.zeros((1, width), F32) for _ in range(8)]
    for b in range(2 * TP):
        rows = pl.ds(b * n, n)
        first = (row == 0) & (c.g == 0) if b % TP == 0 else None
        ad = lanes_out(adj, rows)
        gx, ga = gates[0, rows, :], gates[1, rows, :]
        decay, root = decay_terms(ga, db[...])
        mult = root if first is None else jnp.where(first, 1.0, root)
        cv = conv[rows, :].astype(F32)
        before = jnp.where(row == 0, carry[b:b + 1, :], pltpu.roll(state[rows, :], 1, 0))
        gmult = -(ad * cv * gx) * (decay * decay) / root
        if first is not None:
            gmult = jnp.where(first, 0.0, gmult)
        glog = ad * before * decay + gmult
        total[7] = total[7] + jnp.sum(glog * (-8.0 * ga), axis=0, keepdims=True)
        pre = [ad * cv * mult * gx * (1.0 - gx), glog * (-8.0 * db[...]) * ga * (1.0 - ga)]
        conved = ad * gx * mult
        for k in range(2):
            total[5 + k] = total[5 + k] + jnp.sum(pre[k], axis=0, keepdims=True)
            low = pre[k].astype(BF)
            gpl[k, rows, :] = low
            conved = conved + jnp.concatenate([
                lax.dot_general(low[:, h * 256:(h + 1) * 256], gb[k, h], (((1,), (1,)), ((), ())), preferred_element_type=F32)
                for h in range(2)], axis=1)
        gc[b, pl.ds(0, n), :] = conved
        heads[b] = conved[:8]
        ext[b % 2, pl.ds(0, 8), :] = rim[b]
        ext[b % 2, pl.ds(8, n), :] = ci[b].astype(F32)
        for k in range(4):
            total[k] = total[k] + jnp.sum(conved * ext[b % 2, pl.ds(8 - k, n), :], axis=0, keepdims=True)
        total[4] = total[4] + jnp.sum(conved, axis=0, keepdims=True)
    rslot = c.slot()
    out = c.to(heads, rim_in, c.at(g=(c.g + c.ng - 1) % c.ng), rslot)
    out.start()
    sums[...] = jnp.concatenate(total, axis=0)
    for k in range(2):
        for h in range(2):
            ggb[k, h] = lax.dot_general(conv[:, h * 256:(h + 1) * 256], gpl[k, :, h * 256:(h + 1) * 256], (((0,), (0,)), ((), ())), preferred_element_type=F32).astype(BF)
    out.wait()
    for b in range(2 * TP):
        rows = pl.ds(b * n, n)
        same = rim_in[b]
        nxt = jnp.zeros_like(same) if b % TP == TP - 1 else rim_in[b + 1]
        gc[b, pl.ds(n, 8), :] = jnp.where(c.g == c.ng - 1, nxt, same)
        v = chan[0:1] * gc[b, pl.ds(0, n), :]
        for k in range(1, 4):
            v = v + chan[k:k + 1] * gc[b, pl.ds(k, n), :]
        gbr[1, rows, :] = v.astype(BF)
    run(*zs)


def mix_bwd_call(gmo, wo, br0, ci, gb, chan, db, saved, r1, r2, units):
    ng = lax.axis_size("dp") // TP
    rows, width = br0.shape
    n = rows // (2 * TP)
    r = r1.shape[1]
    S = jax.ShapeDtypeStruct
    V = pltpu.VMEM
    return call(
        mix_bwd_kernel,
        (S((2, rows, width), BF), S((2, 2, 256, 256), BF), S((8, width), F32), S((r, units), BF), S((r, units), BF)),
        [VM] * 13 + [HBM] * 2,
        (VM,) * 3 + (HBM,) * 2,
        [V((rows, width), F32), V((width // 128, rows, 128), F32), V((width // 128, rows, 128), F32), V((2 * TP, n + 8, width), F32), V((2, rows, width), BF),
         V((2, n + 8, width), F32), V((2 * TP, 8, width), F32), V((ng, 2 * TP, width), F32), V((2 * TP, 8, width), F32)],
        6, 128,
    )(gmo, wo, br0, ci, gb, chan, db, *saved, r1, r2)


def mlp_kernel(nb, go, w0, w1, w2, hidden, gg0, gg1, part, gnb, v0, v1, v2, sems):
    copies = [pltpu.make_async_copy(a, b, sems.at[k]) for k, (a, b) in enumerate(((w0, v0), (w1, v1), (w2, v2)))]
    begin = pl.program_id(0) == 0

    @pl.when(begin)
    def _():
        for copy in copies:
            copy.start()

    def ready(k):
        pl.when(begin)(lambda: copies[k].wait())

    def back(a, w):
        return lax.dot_general(a, w, (((1,), (1,)), ((), ())), preferred_element_type=F32)

    ready(0)
    first = jnp.dot(nb[...], v0[...], preferred_element_type=F32)
    ready(1)
    second = jnp.dot(nb[...], v1[...], preferred_element_type=F32)
    act, slope = gelu_pair(first)
    low = (act * second).astype(BF)
    hidden[...] = low
    ready(2)
    gh = jnp.dot(go[...], v2[...], preferred_element_type=F32)
    a, b = (gh * second * slope).astype(BF), (gh * act).astype(BF)
    gg0[...] = a
    gg1[...] = b
    gnb[...] = (back(a, v0[...]) + back(b, v1[...])).astype(BF)
    part[...] = back(low, v2[...]).astype(BF)


def mlp_call(nb, go, w0, w1, w2):
    rows, d = nb.shape
    fs = w0.shape[1]
    n = 256
    S = jax.ShapeDtypeStruct
    wide = pl.BlockSpec((n, d), lambda i: (i, 0))
    slim = pl.BlockSpec((n, fs), lambda i: (i, 0))
    return pl.pallas_call(
        mlp_kernel,
        grid=(rows // n,),
        out_shape=(S((rows, fs), BF),) * 3 + (S((rows, d), BF),) * 2,
        in_specs=[wide, wide, HBM, HBM, HBM],
        out_specs=(slim,) * 3 + (wide,) * 2,
        scratch_shapes=[pltpu.VMEM((d, fs), BF)] * 3 + [pltpu.SemaphoreType.DMA((3,))],
        compiler_params=pltpu.CompilerParams(vmem_limit_bytes=VMEM_LIMIT),
    )(nb, go, w0, w1, w2)


def dot(a, b, ca, cb):
    return lax.dot_general(a, b, (((ca,), (cb,)), ((), ())), preferred_element_type=F32)


def body(block_input, lengths, norm_gains, w_branch, channel_params, gate_blocks, decay_param, w_out, w_mlp, w_down, out_grad):
    ndp, ng, t, g = plan()
    dp, mp = lax.axis_index("dp"), lax.axis_index("mp")
    rows, width = block_input.shape[1:]
    r, gr, units = w_branch.shape[1], gate_blocks.shape[2], w_mlp.shape[2]
    fs = cut(units, 0)[1]
    decay_base = jax.nn.softplus(decay_param)
    pos = dp * 2 * rows + mp * rows + jnp.arange(rows, dtype=jnp.int32)
    valid = (pos[None] < lengths[:, None])[..., None]
    x = block_input
    grad_own = jnp.where(valid, out_grad, jnp.zeros_like(out_grad))
    na, wb0, wb1, wop, gb = start_call(x, norm_gains[0], w_branch, w_out.T, gate_blocks)
    na = na.reshape(-1, width)
    wb0, wb1 = wb0.reshape(width, 512), wb1.reshape(width, 512)
    gb = gb.reshape(2, 2, 256, 256)
    mixed, *saved, branch0, conv_input, chan, db, wo, p0 = mix_fwd_call(na, wb0, wb1, gb, channel_params, decay_base, wop, w_mlp[0])
    wo = wo.reshape(width, 512)
    residual, nb, go, w0, w1, wd = mid_call(mixed, wo, x, grad_own, norm_gains[1], p0, w_mlp[1], w_down.T)
    nb, go = nb.reshape(-1, width), go.reshape(-1, width)
    w0, w1, wd = w0.reshape(width, fs), w1.reshape(width, fs), wd.reshape(width, fs)
    hidden, gg0, gg1, mlp_part, gnb = mlp_call(nb, go, w0, w1, wd)
    gres, gain_b, mlp_own, gmo, o0, r1, r2 = back_call(gnb, mlp_part, residual, grad_own, norm_gains[1], nb, go, gg0, gg1, hidden, ng, r, units)
    out = jnp.where(valid, residual + mlp_own, 0.0).astype(BF)
    gmo = gmo.reshape(-1, width)
    gbr, ggb, chan_rows, o1, o2 = mix_bwd_call(gmo, wo, branch0, conv_input, gb, chan, db, saved, r1, r2, units)
    gin, gains, gchan, gdec, owb, owo, ogb = end_call(
        wb0, wb1, x, gres, norm_gains[0], na, gbr, gmo, mixed, ggb.reshape(2, 2, TP, ng, gr, 256), gain_b, chan_rows, r,
    )
    g_wb, g_wo, g_gb = owb.astype(F32), owo.astype(F32).T, ogb.astype(F32)
    g_wm, g_wd = jnp.stack([o0, o1]).astype(F32), o2.astype(F32).T
    return out, gin, gains.reshape(2, width), g_wb, gchan, g_gb, gdec[0] * jax.nn.sigmoid(decay_param), g_wo, g_wm, g_wd


def solution(mesh):
    return jax.shard_map(
        body,
        mesh=mesh,
        in_specs=(P(None, ("dp", "mp"), None), P(), P(), P(None, "dp", "mp"), P(None, "mp"), P(None, "mp", "dp", None), P("mp"), P("mp", "dp"), P(None, "dp", "mp"), P("mp", "dp"), P(None, ("dp", "mp"), None)),
        out_specs=(P(None, ("dp", "mp"), None), P(None, ("dp", "mp"), None), P(), P(None, "dp", "mp"), P(None, "mp"), P(None, "mp", "dp", None), P("mp"), P("mp", "dp"), P(None, "dp", "mp"), P("mp", "dp")),
        check_vma=False,
    )
```
